32 devices in a mesh: dp: 16 (over z, x, core), tensor: 2 (over y).
Axes of the slice: x: 2, y: 2, z: 4, core: 2. Of those that a mesh axis runs over, the one named last changes fastest.
Arguments:
- hidden_in: bfloat16 [24576, 768], P(('dp', 'tensor')), may hold values from -6 to 6
- bounds: int32 [16, 6], P('dp'), may hold values from 0 to 1536, as said below
- attn_gain: float32 [768], replicated, may hold values from 0.1 to 1.9
- w_qkv: bfloat16 [3, 768, 768], P(None, None, 'tensor'), may hold values from -0.21875 to 0.21875
- w_attn: bfloat16 [768, 768], P('tensor'), may hold values from -3 to 3
- mlp_gain: float32 [768], replicated, may hold values from 0.1 to 1.9
- w_in: bfloat16 [2, 768, 1152], P(None, None, 'tensor'), may hold values from -0.21875 to 0.21875
- w_out: bfloat16 [1152, 768], P('tensor'), may hold values from -0.1875 to 0.1875
- cotangent: bfloat16 [24576, 768], P(('dp', 'tensor')), may hold values from -6 to 6
Outputs:
- hidden_out: bfloat16 [24576, 768], P(('dp', 'tensor'))
- grad_in: bfloat16 [24576, 768], P(('dp', 'tensor'))
- grad_attn_gain: float32 [768], replicated
- grad_w_qkv: float32 [3, 768, 768], P(None, None, 'tensor')
- grad_w_attn: float32 [768, 768], P('tensor')
- grad_mlp_gain: float32 [768], replicated
- grad_w_in: float32 [2, 768, 1152], P(None, None, 'tensor')
- grad_w_out: float32 [1152, 768], P('tensor')
The draws below stay inside these ranges and needn't reach their ends.
Inputs may be any that keep to these rules, and one draw needn't show every extreme that they name: Each row of bounds holds 6 nondecreasing offsets into the 1536 slots of one index of dp, the first 0; consecutive offsets bound one sequence (some empty), slots from the last offset on are padding. In every row one sequence holds slots 1536 // 2 - 1 and 768; in some row a single sequence fills all 1536 slots.
All inputs are finite; a program needn't handle non-finite values.
Results may differ from the reference program's by a relative error of at most 0.015.
The reference program's roundings to bfloat16 on the way count: a program that leaves them out, or rounds other values in their place, can miss the bound.
Values may be sent and summed in bfloat16 or wider, within the bound.
No kernel may reach another device: no remote copies, remote signals or barrier semaphores. Data moves between devices by JAX's collectives and lax.ppermute only.
A program may use at most 192 MiB of HBM per device.

```python
import jax
import jax.numpy as jnp
from jax import lax

D = 768
H = 12
HD = 64
FF = 1152
CAP = 1536
QB = 512
ROWS = 24576
N_DP = 16


def draw_bounds(key, part):
    key = jax.random.fold_in(key, 7)
    key_list = jax.random.split(key, 6)
    middle = CAP // 2
    filled = jax.random.randint(key_list[0], (N_DP,), 5 * CAP // 8, CAP + 1)
    lower_cut = jax.random.randint(key_list[1], (N_DP,), 0, middle)
    upper_cut = jnp.minimum(jax.random.randint(key_list[2], (N_DP,), middle + 1, CAP + 1), filled)
    first_cut = jax.random.randint(key_list[3], (N_DP,), 0, lower_cut + 1)
    last_cut = jax.random.randint(key_list[4], (N_DP,), upper_cut, filled + 1)
    zero_edge = jnp.zeros((N_DP,), jnp.int32)
    edge_rows = jnp.stack([zero_edge, first_cut, lower_cut, upper_cut, last_cut, filled], axis=1)
    whole_row = jax.random.randint(key_list[5], (), 0, N_DP)
    single_row = jnp.array([0, 0, 0, CAP, CAP, CAP], jnp.int32)
    chosen_row = jnp.arange(N_DP)[:, None] == whole_row
    return jnp.where(chosen_row, single_row[None, :], edge_rows).astype(jnp.int32)


def steps_of(rng, dims, shards, smallest, top_value):
    def one(dim, blocks):
        heights = jax.random.uniform(jax.random.fold_in(jax.random.fold_in(rng, 6), dim), (blocks,), jnp.float32, smallest / len(shards), top_value / len(shards))
        return jnp.repeat(jnp.exp(heights), dims[dim] // blocks).reshape((-1,) + (1,) * (len(dims) - dim - 1))

    loudness = one(*shards[0])
    for cut in shards[1:]:
        loudness = loudness * one(*cut)
    return loudness


def scatter_about(stream_key, shape, spread, bound, cuts=(), held_as=jnp.bfloat16):
    entries = spread * jax.random.normal(stream_key, shape, jnp.float32)
    if cuts:
        entries = entries * steps_of(stream_key, shape, cuts, -0.22, 0.18)
    return jnp.clip(entries, -bound, bound).astype(held_as)


def setup_inputs(seed: int = 0) -> dict:
    keys = jax.random.split(jax.random.key(seed), 10)
    return {
        "hidden_in": scatter_about(keys[0], (ROWS, D), 1.0, 6.0, ((0, 32),)),
        "bounds": draw_bounds(jax.random.fold_in(keys[9], 71), 0),
        "attn_gain": jnp.clip(1.0 + 0.18 * jax.random.normal(keys[2], (D,), jnp.float32), 0.1, 1.9),
        "w_qkv": scatter_about(keys[3], (3, D, H * HD), D ** -0.5, 0.21875, ((2, 2),)),
        "w_attn": scatter_about(keys[4], (H * HD, D), 4 ** -0.5, 3.0, ((0, 2),)),
        "mlp_gain": jnp.clip(1.0 + 0.18 * jax.random.normal(keys[5], (D,), jnp.float32), 0.1, 1.9),
        "w_in": scatter_about(keys[6], (2, D, FF), D ** -0.5, 0.21875, ((2, 2),)),
        "w_out": scatter_about(keys[7], (FF, D), FF ** -0.5, 0.1875, ((0, 2),)),
        "cotangent": scatter_about(keys[8], (ROWS, D), 1.0, 6.0, ((0, 32),)),
    }


rope_theta = 160000.0
norm_eps = 1e-05
masked_score = -1e+30
highest = lax.Precision.HIGHEST

@jax.custom_vjp
def low(v):
    return lax.optimization_barrier(v.astype(jnp.bfloat16)).astype(jnp.float32)

@jax.custom_vjp
def low_back(v):
    return v

def low_keep(v):
    return (low(v), None)

def low_pass(kept, grad):
    return (grad,)

def back_keep(v):
    return (v, None)

def back_low(kept, grad):
    return (low(grad),)
low.defvjp(low_keep, low_pass)
low_back.defvjp(back_keep, back_low)

def layout(edge_row, count):
    row_ids = jnp.arange(count, dtype=jnp.int32)
    passed = edge_row[1:][None, :] <= row_ids[:, None]
    segment = lax.optimization_barrier(jnp.sum(passed.astype(jnp.int32), axis=1, dtype=jnp.int32))
    widths = (edge_row[1:] - edge_row[:-1]).astype(jnp.int32)
    begins = lax.optimization_barrier(jnp.sum(jnp.where(passed, widths[None, :], 0), axis=1, dtype=jnp.int32))
    position = (row_ids - begins).astype(jnp.float32)
    is_valid = (row_ids < edge_row[-1]).astype(jnp.float32)
    return (segment, position, is_valid)

def rotary(position):
    half_size = HD // 2
    frequency = jnp.exp(-(2.0 * jnp.arange(half_size, dtype=jnp.float32) / HD) * jnp.log(jnp.float32(rope_theta)))
    angles = position[:, None] * frequency[None, :]
    return (jnp.cos(angles), jnp.sin(angles))

def rotate(flat, cosine, sine):
    shaped = flat.reshape(flat.shape[0], -1, HD)
    leading = shaped[..., :HD // 2]
    trailing = shaped[..., HD // 2:]
    cos_part = cosine[:, None, :]
    sin_part = sine[:, None, :]
    turned = jnp.concatenate([leading * cos_part - trailing * sin_part, trailing * cos_part + leading * sin_part], axis=-1)
    return turned.reshape(flat.shape)

def layer_norm(values, weight):
    centred = values - lax.optimization_barrier(jnp.mean(values, axis=-1, keepdims=True))
    inv_std = lax.rsqrt(lax.optimization_barrier(jnp.mean(centred * centred, axis=-1, keepdims=True)) + norm_eps)
    return centred * inv_std * weight

def geglu(active, gate_part):
    return jax.nn.gelu(active, approximate=False) * gate_part

def product(left, right):
    return jnp.dot(left, right, precision=highest, preferred_element_type=jnp.float32)

def attention(query, key_rows, value_rows, segment):
    count = query.shape[0]
    heads = query.shape[1] // HD
    key_heads = key_rows.reshape(count, heads, HD)
    value_heads = value_rows.reshape(count, heads, HD)

    def one_block(start):
        query_block = lax.dynamic_slice_in_dim(query, start, QB, 0).reshape(QB, heads, HD)
        segment_block = lax.dynamic_slice_in_dim(segment, start, QB, 0)
        raw_scores = jnp.einsum('qhd,khd->hqk', query_block, key_heads, precision=highest)
        scores = low_back(raw_scores * 0.125)
        scores = jnp.where(segment_block[None, :, None] == segment[None, None, :], scores, masked_score)
        row_top = lax.optimization_barrier(jnp.max(scores, axis=-1, keepdims=True))
        expo = jnp.exp(scores - row_top)
        probs = low(expo / lax.optimization_barrier(jnp.sum(expo, axis=-1, keepdims=True)))
        mixed = jnp.einsum('hqk,khd->qhd', probs, value_heads, precision=highest)
        return mixed.reshape(QB, heads * HD)
    starts = jnp.arange(count // QB, dtype=jnp.int32) * QB
    blocks = lax.map(jax.checkpoint(one_block), starts)
    return blocks.reshape(count, heads * HD)

def layer(tokens, attn_gain, w_qkv, w_attn, mlp_gain, w_in, w_out, segment, cosine, sine):
    normed = low(layer_norm(tokens, attn_gain))
    query = low(rotate(low_back(product(normed, w_qkv[0])), cosine, sine))
    key_rows = low(rotate(low_back(product(normed, w_qkv[1])), cosine, sine))
    value_rows = low(low_back(product(normed, w_qkv[2])))
    mixed = low(low_back(attention(query, key_rows, value_rows, segment)))
    residual = tokens + low_back(product(mixed, w_attn))
    normed_mlp = low(layer_norm(residual, mlp_gain))
    active = low_back(product(normed_mlp, w_in[0]))
    gate_part = low_back(product(normed_mlp, w_in[1]))
    hidden = low(geglu(active, gate_part))
    return residual + low_back(product(hidden, w_out))

def reference(hidden_in, bounds, attn_gain, w_qkv, w_attn, mlp_gain, w_in, w_out, cotangent):
    params = (attn_gain.astype(jnp.float32), w_qkv.astype(jnp.float32), w_attn.astype(jnp.float32), mlp_gain.astype(jnp.float32), w_in.astype(jnp.float32), w_out.astype(jnp.float32))

    def one_device(running, inputs):
        rows_in, rows_cot, edge_row = inputs
        segment, position, is_valid = layout(edge_row, CAP)
        cosine, sine = rotary(position)

        def forward(tokens, gain_one, qkv_mat, attn_mat, gain_two, in_mat, out_mat):
            return layer(tokens, gain_one, qkv_mat, attn_mat, gain_two, in_mat, out_mat, segment, cosine, sine)
        result, pull = jax.vjp(forward, rows_in.astype(jnp.float32), params[0], params[1], params[2], params[3], params[4], params[5])
        grads = pull(rows_cot.astype(jnp.float32) * is_valid[:, None])
        running = tuple((earlier + update for earlier, update in zip(running, grads[1:])))
        return (running, (result.astype(jnp.bfloat16), grads[0].astype(jnp.bfloat16)))
    start_sums = tuple((jnp.zeros_like(param) for param in params))
    sums_out, (outputs, grads_in) = lax.scan(one_device, start_sums, (hidden_in.reshape(N_DP, CAP, D), cotangent.reshape(N_DP, CAP, D), bounds))
    return (outputs.reshape(ROWS, D), grads_in.reshape(ROWS, D), sums_out[0], sums_out[1], sums_out[2], sums_out[3], sums_out[4], sums_out[5])
```

```python
import functools

import jax
import jax.numpy as jnp
from jax import lax
from jax.experimental import pallas as pl
from jax.experimental.pallas import tpu as pltpu
from jax.sharding import PartitionSpec as P

HD = 64
NSEG = 6
PAIR = 2 * HD
BLK = 256
QBLK = 512
KBLK = 512
rope_theta = 160000.0
norm_eps = 1e-05
masked_score = -1e30
VMEM_BYTES = 56 * 1024 * 1024
f32 = jnp.float32
bf16 = jnp.bfloat16


def params():
    return pltpu.CompilerParams(vmem_limit_bytes=VMEM_BYTES)


def cost(flops, nbytes):
    return pl.CostEstimate(flops=int(flops), bytes_accessed=int(nbytes), transcendentals=0)


def nn(a, b):
    return jnp.dot(a, b, preferred_element_type=f32)


def nt(a, b):
    return lax.dot_general(a, b, (((1,), (1,)), ((), ())), preferred_element_type=f32)


def whole(shape):
    return pl.BlockSpec(shape, lambda i: (0,) * len(shape))


def unit_rows(x):
    centred = x - jnp.mean(x, axis=-1, keepdims=True)
    inv = lax.rsqrt(jnp.mean(centred * centred, axis=-1, keepdims=True) + norm_eps)
    return centred * inv, inv


def norm_back(e, xh, inv):
    return inv * (
        e - jnp.mean(e, axis=-1, keepdims=True) - xh * jnp.mean(e * xh, axis=-1, keepdims=True)
    )


def turn(x, cosine, sine, back):
    lane = lax.broadcasted_iota(jnp.int32, x.shape, 1) % HD
    other = jnp.where(lane < HD // 2, pltpu.roll(x, PAIR - HD // 2, 1), pltpu.roll(x, HD // 2, 1))
    return x * cosine - other * sine if back else x * cosine + other * sine


def tables(edges, ids):
    lane = lax.broadcasted_iota(jnp.int32, ids.shape, 1)
    seg = jnp.zeros(ids.shape, jnp.int32)
    begin = jnp.zeros(ids.shape, jnp.int32)
    for n in range(1, NSEG):
        passed = edges[n] <= ids
        seg += passed.astype(jnp.int32)
        begin += jnp.where(passed, edges[n] - edges[n - 1], 0)
    place = (ids - begin).astype(f32)
    freq = jnp.exp(
        -(2.0 * (lane % (HD // 2)).astype(f32) / HD) * jnp.log(jnp.float32(rope_theta))
    )
    angle = place * freq
    sign = jnp.where(lane % HD < HD // 2, -1.0, 1.0)
    slot = lane % HD
    same = slot == seg
    feat_q = jnp.where(same, 1.0, 0.0).astype(bf16)
    feat_k = jnp.where(
        slot < NSEG,
        jnp.where(same, 0.0, masked_score),
        jnp.where(slot < NSEG + 3, 1.0, 0.0),
    ).astype(bf16)
    return jnp.cos(angle), jnp.sin(angle) * sign, feat_q, feat_k


def qkv_body(h_ref, gain_ref, w_ref, cos_ref, sin_ref, *refs):
    n1_ref, q_ref, k_ref, v_ref = refs[-4:]
    unit, inv = unit_rows(h_ref[...].astype(f32))
    n1 = (unit * gain_ref[...]).astype(bf16)
    n1_ref[...] = n1
    cosine, sine = cos_ref[...], sin_ref[...]
    width = w_ref.shape[2]
    for which, out, scale in ((0, q_ref, 0.125), (1, k_ref, 1.0)):
        full = nn(n1, w_ref[which])
        for at in range(0, width, PAIR):
            turned = turn(full[:, at : at + PAIR], cosine, sine, False).astype(bf16)
            if scale != 1.0:
                turned = (turned.astype(f32) * scale).astype(bf16)
            out[:, at : at + PAIR] = turned
    v_ref[...] = nn(n1, w_ref[2]).astype(bf16)


def qkv(h, gain, w, cosine, sine, first, held):
    rows, d = h.shape
    cap, width = cosine.shape[0], w.shape[2]
    off = first // BLK
    by_row = lambda n: pl.BlockSpec((BLK, n), lambda i: (i + off, 0))
    shapes = [jax.ShapeDtypeStruct((cap, n), bf16) for n in (d, width, width, width)]
    return pl.pallas_call(
        qkv_body,
        grid=(rows // BLK,),
        in_specs=[
            pl.BlockSpec((BLK, d), lambda i: (i, 0)),
            whole((1, d)),
            whole(w.shape),
            by_row(PAIR),
            by_row(PAIR),
        ]
        + [pl.BlockSpec(memory_space=pl.ANY)] * len(held),
        out_specs=[by_row(d), by_row(width), by_row(width), by_row(width)],
        out_shape=shapes,
        input_output_aliases={5 + n: n for n in range(len(held))},
        compiler_params=params(),
        cost_estimate=cost(2 * rows * d * 3 * width, 12e6),
        name="qkv",
    )(h, gain, w, cosine, sine, *held)


def lanes_of(head, shape):
    lane = lax.broadcasted_iota(jnp.int32, shape, 1)
    return (lane < HD) if head == 0 else (lane >= HD)


def attend_body(q_ref, k_ref, v_ref, fq_ref, fk_ref, o_ref, qa_ref, qb_ref):
    q, k, v, fq, fk = q_ref[...], k_ref[...], v_ref[...], fq_ref[...], fk_ref[...]
    slot = lax.broadcasted_iota(jnp.int32, q.shape, 1) % HD
    mixed = []
    for head, keep in ((0, qa_ref), (1, qb_ref)):
        mine = lanes_of(head, q.shape)
        q_in = jnp.where(mine, q, fq)
        k_in = jnp.where(lanes_of(head, k.shape), k, fk)
        score = nt(q_in, k_in)
        top = jnp.max(score, axis=-1, keepdims=True)
        expo = jnp.exp(score - top)
        total = jnp.sum(expo, axis=-1, keepdims=True)
        probs = (expo * (1.0 / total)).astype(bf16)
        mixed.append(nn(probs, v))
        left = -(top + jnp.log(total))
        tagged = q_in.astype(f32)
        for part in range(3):
            head_bits = left.astype(bf16).astype(f32)
            left = left - head_bits
            tagged = jnp.where(
                jnp.logical_and(jnp.logical_not(mine), slot == NSEG + part), head_bits, tagged
            )
        keep[...] = tagged.astype(bf16)
    o_ref[...] = jnp.where(lanes_of(0, q.shape), mixed[0], mixed[1]).astype(bf16)


def attend(pair, q, k, v, feat_q, feat_k):
    cap = q.shape[0]
    part = pl.BlockSpec((QBLK, PAIR), lambda i: (i, 0))
    full = pl.BlockSpec((cap, PAIR), lambda i: (0, pair))
    return pl.pallas_call(
        attend_body,
        grid=(cap // QBLK,),
        in_specs=[
            pl.BlockSpec((QBLK, PAIR), lambda i: (i, pair)),
            full,
            full,
            part,
            whole((cap, PAIR)),
        ],
        out_specs=[part] * 3,
        out_shape=[jax.ShapeDtypeStruct((cap, PAIR), bf16)] * 3,
        compiler_params=params(),
        cost_estimate=cost(2 * 2 * 2 * cap * cap * 256 * 2, 3e6),
        name="attend",
    )(q, k, v, feat_q, feat_k)


def back_body(
    qa_ref, qb_ref, q_ref, k_ref, v_ref, fk_ref, o_ref, d0_ref, d1_ref, cos_ref, sin_ref,
    dq_ref, dk_ref, dv_ref, dol_ref, da_ref, db_ref, dqt_ref,
):
    step = pl.program_id(0)
    cap = o_ref.shape[0]
    half = d0_ref.shape[0]

    @pl.when(step == 0)
    def _():
        dol_ref[:half] = d0_ref[...]
        dol_ref[half:] = d1_ref[...]
        dol = dol_ref[...]
        slot = lax.broadcasted_iota(jnp.int32, dol.shape, 1) % HD
        wide = dol.astype(f32)
        prod = wide * o_ref[...].astype(f32)
        for head, out in ((0, da_ref), (1, db_ref)):
            mine = lanes_of(head, dol.shape)
            left = -jnp.sum(jnp.where(mine, prod, 0.0), axis=-1, keepdims=True)
            tagged = jnp.where(mine, wide, 0.0)
            for part in range(3):
                head_bits = left.astype(bf16).astype(f32)
                left = left - head_bits
                tagged = jnp.where(
                    jnp.logical_and(jnp.logical_not(mine), slot == NSEG + part), head_bits, tagged
                )
            out[...] = tagged.astype(bf16)
        dqt_ref[...] = jnp.zeros_like(dqt_ref)

    k, v, fk, q, dol = k_ref[...], v_ref[...], fk_ref[...], q_ref[...], dol_ref[...]
    k_turned = k.T
    slot = lax.broadcasted_iota(jnp.int32, v.shape, 1) % HD
    ones = jnp.where(
        jnp.logical_and(slot >= NSEG, slot < NSEG + 3), 1.0, 0.0
    ).astype(bf16)
    dks, dvs = [], []
    for head, qe_ref, de_ref in ((0, qa_ref, da_ref), (1, qb_ref, db_ref)):
        mine = lanes_of(head, k.shape)
        probs = jnp.exp(nt(jnp.where(mine, k, fk), qe_ref[...]))
        dvs.append(nn(probs.astype(bf16), dol))
        ds = (probs * nt(jnp.where(mine, v, ones), de_ref[...])).astype(bf16)
        dks.append(nn(ds, q))
        at = head * HD
        dqt_ref[at : at + HD] += nn(k_turned[at : at + HD], ds)
    first = lanes_of(0, k.shape)
    rows = pl.ds(pl.multiple_of(step * KBLK, KBLK), KBLK)
    dk = jnp.where(first, dks[0], dks[1])
    dk_ref[...] = turn(dk, cos_ref[rows], sin_ref[rows], True).astype(bf16)
    dv_ref[...] = jnp.where(first, dvs[0], dvs[1]).astype(bf16)

    @pl.when(step == cap // KBLK - 1)
    def _():
        dq = dqt_ref[...].T * 0.125
        dq_ref[...] = turn(dq, cos_ref[...], sin_ref[...], True).astype(bf16)


def attend_back(pair, qa, qb, q, k, v, feat_k, o, d0, d1, cosine, sine):
    cap = q.shape[0]
    full = whole((cap, PAIR))
    block = pl.BlockSpec((KBLK, PAIR), lambda i: (i, pair))
    part = pl.BlockSpec((KBLK, PAIR), lambda i: (i, 0))
    half = whole((cap // 2, PAIR))
    return pl.pallas_call(
        back_body,
        grid=(cap // KBLK,),
        in_specs=[
            full,
            full,
            pl.BlockSpec((cap, PAIR), lambda i: (0, pair)),
            block,
            block,
            part,
            full,
            half,
            half,
            full,
            full,
        ],
        out_specs=[full, part, part],
        out_shape=[jax.ShapeDtypeStruct((cap, PAIR), bf16)] * 3,
        scratch_shapes=[
            pltpu.VMEM((cap, PAIR), bf16),
            pltpu.VMEM((cap, PAIR), bf16),
            pltpu.VMEM((cap, PAIR), bf16),
            pltpu.VMEM((PAIR, cap), f32),
        ],
        compiler_params=params(),
        cost_estimate=cost(5 * 2 * 2 * cap * cap * 256 * 2, 6e6),
        name="attend_back",
    )(qa, qb, q, k, v, feat_k, o, d0, d1, cosine, sine)


def mlp_body(
    sc_ref, h_ref, cot_ref, oa0, oa1, oa2, ob0, ob1, ob2, gain_ref, wa_ref, wb_ref,
    ia0, ia1, ib0, ib1, ua_ref, ub_ref,
    out_ref, n2_ref, ga_ref, dx_ref, gm_ref, ha_ref, hb_ref,
    fa0, fa1, fb0, fb1, da0, da1, da2, db0, db1, db2, gg_ref,
):
    step = pl.program_id(0)
    oa = jnp.concatenate([oa0[...], oa1[...], oa2[...]], axis=1)
    ob = jnp.concatenate([ob0[...], ob1[...], ob2[...]], axis=1)
    x1 = h_ref[...].astype(f32) + (nn(oa, wa_ref[...]) + nn(ob, wb_ref[...]))
    xh, inv = unit_rows(x1)
    gain = gain_ref[...]
    n2 = (xh * gain).astype(bf16)
    n2_ref[...] = n2
    ids = sc_ref[0] + step * BLK + lax.broadcasted_iota(jnp.int32, x1.shape, 0)
    g = jnp.where(ids < sc_ref[1], cot_ref[...].astype(f32), 0.0)
    gm = g.astype(bf16)
    gm_ref[...] = gm
    m = jnp.zeros_like(x1)
    dn2 = jnp.zeros_like(x1)
    for i0, i1, u_ref, h_out, f0, f1 in (
        (ia0, ia1, ua_ref, ha_ref, fa0, fa1),
        (ib0, ib1, ub_ref, hb_ref, fb0, fb1),
    ):
        act = nn(n2, i0[...])
        gate = nn(n2, i1[...])
        phi = 0.5 * (1.0 + lax.erf(act * 0.7071067811865476))
        bell = jnp.exp(-0.5 * act * act) * 0.3989422804014327
        gelu = act * phi
        hidden = (gelu * gate).astype(bf16)
        h_out[...] = hidden
        m = m + nn(hidden, u_ref[...])
        dh = nt(gm, u_ref[...])
        dact = (dh * gate * (phi + act * bell)).astype(bf16)
        dgate = (dh * gelu).astype(bf16)
        f0[...] = dact
        f1[...] = dgate
        dn2 = dn2 + nt(dact, i0[...]) + nt(dgate, i1[...])
    out_ref[...] = (x1 + m).astype(bf16)

    @pl.when(step == 0)
    def _():
        gg_ref[...] = jnp.zeros_like(gg_ref)

    gg_ref[...] += jnp.sum((dn2 * xh).reshape(-1, 8, x1.shape[1]), axis=0)
    dx = g + norm_back(dn2 * gain, xh, inv)
    dx_ref[...] = dx
    ga = dx.astype(bf16)
    ga_ref[...] = ga
    da = nt(ga, wa_ref[...]).astype(bf16)
    db = nt(ga, wb_ref[...]).astype(bf16)
    for n, (a_out, b_out) in enumerate(((da0, db0), (da1, db1), (da2, db2))):
        a_out[...] = da[:, n * PAIR : (n + 1) * PAIR]
        b_out[...] = db[:, n * PAIR : (n + 1) * PAIR]


def mlp(scalars, h, cot, o_own, o_got, gain, wa, wb, ia, ib, ua, ub):
    rows, d = h.shape
    units = ua.shape[0]
    row = lambda n: pl.BlockSpec((BLK, n), lambda i: (i, 0))
    out = lambda n, t=bf16: jax.ShapeDtypeStruct((rows, n), t)
    flops = 2 * rows * d * (2 * 2 * wa.shape[0] + 6 * 2 * units)
    return pl.pallas_call(
        mlp_body,
        grid=(rows // BLK,),
        in_specs=[pl.BlockSpec(memory_space=pltpu.SMEM), row(d), row(d)]
        + [row(PAIR)] * 6
        + [whole((1, d)), whole(wa.shape), whole(wb.shape)]
        + [whole((d, units))] * 4
        + [whole(ua.shape)] * 2,
        out_specs=[row(d)] * 5
        + [row(units)] * 6
        + [row(PAIR)] * 6
        + [whole((8, d))],
        out_shape=[out(d), out(d), out(d), out(d, f32), out(d)]
        + [out(units)] * 6
        + [out(PAIR)] * 6
        + [jax.ShapeDtypeStruct((8, d), f32)],
        compiler_params=params(),
        cost_estimate=cost(1.5 * flops, 24e6),
        name="mlp",
    )(scalars, h, cot, *o_own, *o_got, gain, wa, wb, *ia, *ib, ua, ub)


def tail_body(
    dq0, dq1, dq2, dk0, dk1, dk2, dv0, dv1, dv2, w_ref, h_ref, dn_ref, gg_ref
):
    parts = [
        jnp.concatenate([a[...], b[...], c[...]], axis=1)
        for a, b, c in ((dq0, dq1, dq2), (dk0, dk1, dk2), (dv0, dv1, dv2))
    ]
    dn = nt(parts[0], w_ref[0]) + nt(parts[1], w_ref[1]) + nt(parts[2], w_ref[2])
    dn_ref[...] = dn.astype(dn_ref.dtype)
    xh, unused = unit_rows(h_ref[...].astype(f32))

    @pl.when(pl.program_id(0) == 0)
    def _():
        gg_ref[...] = jnp.zeros_like(gg_ref)

    gg_ref[...] += jnp.sum((dn * xh).reshape(-1, 8, dn.shape[1]), axis=0)


def tail(parts, w, h, first, dtype):
    rows, d = h.shape
    off = first // BLK
    part = pl.BlockSpec((BLK, PAIR), lambda i: (i + off, 0))
    row = pl.BlockSpec((BLK, d), lambda i: (i, 0))
    return pl.pallas_call(
        tail_body,
        grid=(rows // BLK,),
        in_specs=[part] * 9 + [whole(w.shape), row],
        out_specs=[row, whole((8, d))],
        out_shape=[
            jax.ShapeDtypeStruct((rows, d), dtype),
            jax.ShapeDtypeStruct((8, d), f32),
        ],
        compiler_params=params(),
        cost_estimate=cost(2 * rows * d * 3 * w.shape[2], 8e6),
        name="tail",
    )(*parts, w, h)


def last_body(h_ref, gain_ref, own_ref, got_ref, dx_ref, out_ref):
    xh, inv = unit_rows(h_ref[...].astype(f32))
    dn = own_ref[...] + got_ref[...].astype(f32)
    out_ref[...] = (dx_ref[...] + norm_back(dn * gain_ref[...], xh, inv)).astype(bf16)


def last(h, gain, own, got, dx):
    rows, d = h.shape
    row = pl.BlockSpec((BLK, d), lambda i: (i, 0))
    return pl.pallas_call(
        last_body,
        grid=(rows // BLK,),
        in_specs=[row, whole((1, d)), row, row, row],
        out_specs=row,
        out_shape=jax.ShapeDtypeStruct((rows, d), bf16),
        compiler_params=params(),
        cost_estimate=cost(40 * rows * d, 9e6),
        name="last",
    )(h, gain, own, got, dx)


def on_device(dp, hidden_in, bounds, attn_gain, w_qkv, w_attn, mlp_gain, w_in, w_out, cotangent):
    rows, d = hidden_in.shape
    cap = 2 * rows
    shard = lax.axis_index("tensor")
    core = lax.axis_index("dp") % 2
    core_zero = core == 0
    groups = [list(range(c, dp, 2)) for c in range(2)]

    def over_y(x):
        return lax.ppermute(x, "tensor", [(0, 1), (1, 0)])

    def over_core(x):
        return lax.ppermute(x, "dp", [(n, n ^ 1) for n in range(dp)])

    def halves(x):
        return x.reshape((2, x.shape[0] // 2) + x.shape[1:])

    def pick(x, which):
        return lax.dynamic_index_in_dim(x, which, 0, keepdims=False)

    def join(mine, got):
        return jnp.concatenate(
            [jnp.where(core_zero, mine, got), jnp.where(core_zero, got, mine)], axis=0
        )

    hidden_got = over_y(hidden_in)
    edges = [bounds[0, n] for n in range(NSEG)]
    ids = lax.broadcasted_iota(jnp.int32, (cap, PAIR), 0)
    ids = jnp.where(shard == 0, ids, jnp.where(ids < rows, ids + rows, ids - rows))
    cosine, sine, feat_q, feat_k = tables(edges, ids)
    gain_a = attn_gain.reshape(1, d)
    gain_m = mlp_gain.reshape(1, d)
    held = qkv(hidden_in, gain_a, w_qkv, cosine, sine, 0, ())
    pieces = (pick(halves(w_attn), core), pick(w_in, core), pick(halves(w_out), core))
    hidden_got, pieces = lax.optimization_barrier((hidden_got, pieces))
    n1, q, k, v = qkv(hidden_got, gain_a, w_qkv, cosine, sine, rows, held)

    pieces = [over_y(x) for x in pieces]
    others = [over_core(x) for x in pieces]
    w_attn_got = join(pieces[0], others[0])
    w_in_got = (
        jnp.where(core_zero, pieces[1], others[1]),
        jnp.where(core_zero, others[1], pieces[1]),
    )
    w_out_got = join(pieces[2], others[2])

    o, q_tag, o_got = [], [], []
    for pair in range(3):
        mixed, qa, qb = attend(pair, q, k, v, feat_q, feat_k)
        o.append(mixed)
        q_tag.append((qa, qb))
        o_got.append(over_y(mixed[rows:]))

    scalars = jnp.stack([shard * rows, edges[NSEG - 1]]).astype(jnp.int32)
    (
        hidden_out, n2, ga, dx, gm, hid_a, hid_b, fa0, fa1, fb0, fb1,
        da0, da1, da2, db0, db1, db2, gg_mlp,
    ) = mlp(
        scalars, hidden_in, cotangent, o, o_got, gain_m, w_attn, w_attn_got,
        (w_in[0], w_in[1]), w_in_got, w_out, w_out_got,
    )
    d_got = [over_y(x) for x in (db0, db1, db2)]

    def tn(a, b):
        return lax.dot_general(a, b, (((0,), (0,)), ((), ())), preferred_element_type=f32)

    own_o = jnp.concatenate([x[:rows] for x in o], axis=1)
    got_o = jnp.concatenate(o_got, axis=1)
    grads = []
    for o_rows, hid, f0, f1 in ((own_o, hid_a, fa0, fa1), (got_o, hid_b, fb0, fb1)):
        grads.append(
            (
                halves(tn(o_rows, ga).astype(bf16)),
                jnp.stack([tn(n2, f0).astype(bf16), tn(n2, f1).astype(bf16)]),
                halves(tn(hid, gm).astype(bf16)),
            )
        )
    grads = [
        [
            (pick(x, core).astype(f32) + over_core(pick(x, 1 - core)).astype(f32)).astype(bf16)
            for x in side
        ]
        for side in grads
    ]
    grads = [
        (own.astype(f32) + over_y(other).astype(f32)).astype(bf16)
        for own, other in zip(grads[0], grads[1])
    ]
    grads = lax.psum(tuple(grads), "dp", axis_index_groups=groups)
    grads_got = [over_core(x) for x in grads]
    grad_w_attn = join(grads[0], grads_got[0]).astype(f32)
    grad_w_in = join(grads[1][None], grads_got[1][None]).astype(f32)
    grad_w_out = join(grads[2], grads_got[2]).astype(f32)

    d_rows = ((da0, d_got[0]), (da1, d_got[1]), (da2, d_got[2]))
    dqs, dks, dvs = [], [], []
    for pair in range(3):
        dq, dk, dv = attend_back(
            pair, *q_tag[pair], q, k, v, feat_k, o[pair], *d_rows[pair], cosine, sine
        )
        dqs.append(dq)
        dks.append(dk)
        dvs.append(dv)
    parts = dqs + dks + dvs
    dn_other, gg_other = tail(parts, w_qkv, hidden_got, rows, bf16)
    dn_got = over_y(dn_other)
    dn_own, gg_own = tail(parts, w_qkv, hidden_in, 0, f32)

    grad_qkv = jnp.stack(
        [tn(n1, jnp.concatenate(x, axis=1)).astype(bf16) for x in (dqs, dks, dvs)]
    )
    by_half = jnp.moveaxis(grad_qkv.reshape(3, 2, d // 2, -1), 1, 0)
    grad_qkv = (
        pick(by_half, core).astype(f32) + over_core(pick(by_half, 1 - core)).astype(f32)
    ).astype(bf16)
    gains = jnp.stack(
        [jnp.sum(gg_own, axis=0) + jnp.sum(gg_other, axis=0), jnp.sum(gg_mlp, axis=0)]
    )
    gains = gains + over_core(gains)
    gains = (gains + over_y(gains)).astype(bf16)
    grad_qkv, gains = lax.psum((grad_qkv, gains), "dp", axis_index_groups=groups)
    gains = gains.astype(f32)
    qkv_got = over_core(grad_qkv)
    grad_w_qkv = jnp.concatenate(
        [
            jnp.where(core_zero, grad_qkv, qkv_got),
            jnp.where(core_zero, qkv_got, grad_qkv),
        ],
        axis=1,
    ).astype(f32)
    grad_in = last(hidden_in, gain_a, dn_own, dn_got, dx)
    return (
        hidden_out,
        grad_in,
        gains[0],
        grad_w_qkv,
        grad_w_attn,
        gains[1],
        grad_w_in,
        grad_w_out,
    )


def solution(mesh):
    in_specs = (
        P(("dp", "tensor"), None),
        P("dp", None),
        P(),
        P(None, None, "tensor"),
        P("tensor", None),
        P(),
        P(None, None, "tensor"),
        P("tensor", None),
        P(("dp", "tensor"), None),
    )
    out_specs = (
        P(("dp", "tensor"), None),
        P(("dp", "tensor"), None),
        P(),
        P(None, None, "tensor"),
        P("tensor", None),
        P(),
        P(None, None, "tensor"),
        P("tensor", None),
    )
    return jax.shard_map(
        functools.partial(on_device, mesh.shape["dp"]),
        mesh=mesh,
        in_specs=in_specs,
        out_specs=out_specs,
        check_vma=False,
    )
```

```python
import functools

import jax
import jax.numpy as jnp
import numpy as np
from jax import lax
from jax.experimental import pallas as pl
from jax.experimental.pallas import tpu as pltpu
from jax.sharding import PartitionSpec as P

HD = 64
NSEG = 6
PAIR = 2 * HD
BLK = 384
MLP_BLK = 256
COST = 0.15
KBLK = 512
rope_theta = 160000.0
norm_eps = 1e-05
masked_score = -1e30
f32 = jnp.float32
bf16 = jnp.bfloat16


def params(mib):
    return pltpu.CompilerParams(vmem_limit_bytes=mib * 1024 * 1024)


def cost(flops, nbytes):
    return pl.CostEstimate(
        flops=int(flops * COST), bytes_accessed=int(nbytes * COST), transcendentals=0
    )


def nn(a, b):
    return jnp.dot(a, b, preferred_element_type=f32)


def nt(a, b):
    return lax.dot_general(a, b, (((1,), (1,)), ((), ())), preferred_element_type=f32)


def call(body, args, deps=(), *, in_specs, **kw):
    first = len(in_specs)

    def run(*refs):
        body(*refs[:first], *refs[first + len(deps) :])

    return pl.pallas_call(
        run, in_specs=list(in_specs) + [pl.BlockSpec(memory_space=pl.ANY)] * len(deps), **kw
    )(*args, *deps)


def whole(shape):
    return pl.BlockSpec(shape, lambda i: (0,) * len(shape))


def unit_rows(x):
    centred = x - jnp.mean(x, axis=-1, keepdims=True)
    inv = lax.rsqrt(jnp.mean(centred * centred, axis=-1, keepdims=True) + norm_eps)
    return centred * inv, inv


def norm_back(e, xh, inv):
    return inv * (
        e - jnp.mean(e, axis=-1, keepdims=True) - xh * jnp.mean(e * xh, axis=-1, keepdims=True)
    )


def turn(x, cosine, sine, back):
    lane = lax.broadcasted_iota(jnp.int32, x.shape, 1) % HD
    other = jnp.where(lane < HD // 2, pltpu.roll(x, PAIR - HD // 2, 1), pltpu.roll(x, HD // 2, 1))
    return x * cosine - other * sine if back else x * cosine + other * sine


def sincos(x):
    turns = jnp.floor(x * 0.6366197723675814 + 0.5)
    r = ((x - turns * 1.5703125) - turns * 4.837512969970703125e-4) - turns * 7.54978995489188e-8
    z = r * r
    s = r + r * z * (-1.6666654611e-1 + z * (8.3321608736e-3 + z * -1.9515295891e-4))
    c = 1.0 - 0.5 * z + z * z * (
        4.166664568298827e-2 + z * (-1.388731625493765e-3 + z * 2.443315711809948e-5)
    )
    quarter = turns.astype(jnp.int32) & 3
    odd = (quarter & 1) == 1
    sine = jnp.where(odd, c, s)
    cosine = jnp.where(odd, s, c)
    sine = jnp.where(quarter >= 2, -sine, sine)
    cosine = jnp.where(jnp.logical_or(quarter == 1, quarter == 2), -cosine, cosine)
    return sine, cosine


def tables_body(edge_ref, first_ref, freq_ref, cos_ref, sin_ref, fq_ref, fk_ref):
    cap = cos_ref.shape[0]
    ids = lax.broadcasted_iota(jnp.int32, (cap, PAIR), 0) + first_ref[0]
    ids = jnp.where(ids >= cap, ids - cap, ids)
    lane = lax.broadcasted_iota(jnp.int32, ids.shape, 1)
    seg = jnp.zeros(ids.shape, jnp.int32)
    begin = jnp.zeros(ids.shape, jnp.int32)
    for n in range(1, NSEG):
        passed = ids >= edge_ref[0, n]
        seg = jnp.where(passed, seg + 1, seg)
        begin = jnp.where(passed, edge_ref[0, n], begin)
    angle = (ids - begin).astype(f32) * freq_ref[...]
    sine, cosine = sincos(angle)
    slot = lane % HD
    cos_ref[...] = cosine
    sin_ref[...] = jnp.where(slot < HD // 2, -sine, sine)
    same = slot == seg
    fq_ref[...] = jnp.where(same, 1.0, 0.0).astype(bf16)
    fk_ref[...] = jnp.where(
        slot < NSEG,
        jnp.where(same, 0.0, masked_score),
        jnp.where(slot < NSEG + 3, 1.0, 0.0),
    ).astype(bf16)


def tables(edges, first, cap):
    steps = 2.0 * (np.arange(PAIR) % (HD // 2)) / HD
    freq = jnp.asarray(np.exp(-steps * np.log(rope_theta))[None].astype(np.float32))
    smem = pl.BlockSpec(memory_space=pltpu.SMEM)
    table = lambda t: jax.ShapeDtypeStruct((cap, PAIR), t)
    return pl.pallas_call(
        tables_body,
        in_specs=[smem, smem, pl.BlockSpec(memory_space=pltpu.VMEM)],
        out_shape=[table(f32), table(f32), table(bf16), table(bf16)],
        compiler_params=params(8),
        cost_estimate=cost(80 * cap * PAIR, 3e6),
        name="tables",
    )(edges, first, freq)


def stack_body(a_ref, i_ref, u_ref, w_ref, out_ref, qkv_ref):
    at = a_ref.shape[0]
    units = u_ref.shape[0]
    width = w_ref.shape[2]
    out_ref[:at] = a_ref[...]
    for n in range(2):
        out_ref[at + n * units : at + (n + 1) * units] = i_ref[n]
    out_ref[at + 2 * units :] = u_ref[...]
    for n in range(3):
        turned = w_ref[n].T
        for pair in range(width // PAIR):
            to = (3 * pair + n) * PAIR
            qkv_ref[to : to + PAIR] = turned[pair * PAIR : (pair + 1) * PAIR]


def stack(w_attn, w_in_turned, w_out, w_qkv, deps=()):
    at, d = w_attn.shape
    rows = at + 3 * w_out.shape[0]
    vmem = pl.BlockSpec(memory_space=pltpu.VMEM)
    return call(
        stack_body,
        (w_attn, w_in_turned, w_out, w_qkv),
        deps,
        in_specs=[vmem] * 4,
        out_shape=[
            jax.ShapeDtypeStruct((rows, d), bf16),
            jax.ShapeDtypeStruct((3 * w_qkv.shape[2], d), bf16),
        ],
        compiler_params=params(12),
        cost_estimate=cost(1e8, 10e6),
        name="stack",
    )


def qkv_body(h_ref, gain_ref, w_ref, cos_ref, sin_ref, *refs):
    n1_ref, q_ref, k_ref, v_ref = refs[-4:]
    unit, inv = unit_rows(h_ref[...].astype(f32))
    n1 = (unit * gain_ref[...]).astype(bf16)
    n1_ref[...] = n1
    cosine, sine = cos_ref[...], sin_ref[...]
    width = w_ref.shape[2]
    for which, out, scale in ((0, q_ref, 0.125), (1, k_ref, 1.0)):
        full = nn(n1, w_ref[which])
        for at in range(0, width, PAIR):
            turned = turn(full[:, at : at + PAIR], cosine, sine, False).astype(bf16)
            if scale != 1.0:
                turned = (turned.astype(f32) * scale).astype(bf16)
            out[:, at : at + PAIR] = turned
    v_ref[...] = nn(n1, w_ref[2]).astype(bf16)


def qkv(h, gain, w, cosine, sine, first, held, deps=()):
    rows, d = h.shape
    cap, width = cosine.shape[0], w.shape[2]
    off = first // BLK
    by_row = lambda n: pl.BlockSpec((BLK, n), lambda i: (i + off, 0))
    shapes = [jax.ShapeDtypeStruct((cap, n), bf16) for n in (d, width, width, width)]
    return call(
        qkv_body,
        (h, gain, w, cosine, sine, *held),
        deps,
        grid=(rows // BLK,),
        in_specs=[
            pl.BlockSpec((BLK, d), lambda i: (i, 0)),
            whole((1, d)),
            whole(w.shape),
            by_row(PAIR),
            by_row(PAIR),
        ]
        + [pl.BlockSpec(memory_space=pl.ANY)] * len(held),
        out_specs=[by_row(d), by_row(width), by_row(width), by_row(width)],
        out_shape=shapes,
        input_output_aliases={5 + n: n for n in range(len(held))},
        compiler_params=params(14),
        cost_estimate=cost(2 * 2 * rows * d * 3 * width, 12e6),
        name="qkv",
    )


def assemble_body(at_ref, *refs):
    pieces, out_ref, sems = refs[:-2], refs[-2], refs[-1]
    copies = []
    for n, ref in enumerate(pieces):
        to = pl.ds(pl.multiple_of(at_ref[n], 8), ref.shape[0])
        copies.append(pltpu.make_async_copy(ref, out_ref.at[to], sems.at[n]))
        copies[-1].start()
    for copy in copies:
        copy.wait()


def assemble(at, pieces, shape, deps=()):
    anywhere = pl.BlockSpec(memory_space=pl.ANY)
    return call(
        assemble_body,
        (at, *pieces),
        deps,
        in_specs=[pl.BlockSpec(memory_space=pltpu.SMEM)] + [anywhere] * len(pieces),
        out_specs=pl.BlockSpec(memory_space=pltpu.VMEM),
        out_shape=jax.ShapeDtypeStruct(shape, bf16),
        scratch_shapes=[pltpu.SemaphoreType.DMA((len(pieces),))],
        compiler_params=params(8),
        cost_estimate=cost(1e6, 6e6),
        name="assemble",
    )


def lanes_of(head, shape):
    lane = lax.broadcasted_iota(jnp.int32, shape, 1)
    return (lane < HD) if head == 0 else (lane >= HD)


def attend_body(q_ref, k_ref, v_ref, fq_ref, fk_ref, *refs):
    o0_ref, o1_ref, qa_ref, qb_ref = refs[-4:]
    q, k, v, fq, fk = q_ref[...], k_ref[...], v_ref[...], fq_ref[...], fk_ref[...]
    v_turned = v.T
    rows = q.shape[0]
    line = lax.broadcasted_iota(jnp.int32, (PAIR, rows), 0)
    tag = jnp.zeros((PAIR, rows), f32)
    mixed = []
    for head in (0, 1):
        q_in = jnp.where(lanes_of(head, q.shape), q, fq)
        k_in = jnp.where(lanes_of(head, k.shape), k, fk)
        score = nt(k_in, q_in)
        top = jnp.max(score, axis=0, keepdims=True)
        expo = jnp.exp(score - top)
        total = jnp.sum(expo, axis=0, keepdims=True)
        at = head * HD
        mixed.append(nn(v_turned[at : at + HD], expo.astype(bf16)) * (1.0 / total))
        left = -(top + jnp.log(total))
        for part in range(3):
            head_bits = left.astype(bf16).astype(f32)
            left = left - head_bits
            tag = jnp.where(line == HD - at + NSEG + part, head_bits, tag)
    o = jnp.concatenate(mixed, axis=0).T.astype(bf16)
    tag = tag.T
    fq = fq.astype(f32) + tag
    wide = q.astype(f32)
    qa_ref[...] = jnp.where(lanes_of(0, q.shape), wide, fq).astype(bf16)
    qb_ref[...] = jnp.where(lanes_of(1, q.shape), wide, fq).astype(bf16)

    @pl.when(pl.program_id(0) == 0)
    def _():
        o0_ref[...] = o

    @pl.when(pl.program_id(0) == 1)
    def _():
        o1_ref[...] = o


def attend(pair, q, k, v, feat_q, feat_k, held):
    cap, width = q.shape
    rows = cap // 2
    part = pl.BlockSpec((rows, PAIR), lambda i: (i, 0))
    full = pl.BlockSpec((cap, PAIR), lambda i: (0, pair))
    column = lambda n: pl.BlockSpec((rows, PAIR), lambda i: (0, n))
    far = width - PAIR if pair < 2 else PAIR
    return pl.pallas_call(
        attend_body,
        grid=(2,),
        in_specs=[
            pl.BlockSpec((rows, PAIR), lambda i: (i, pair)),
            full,
            full,
            part,
            whole((cap, PAIR)),
        ]
        + [pl.BlockSpec(memory_space=pl.ANY)] * len(held),
        out_specs=[column(pair), column(pair % 2)] + [part] * 2,
        out_shape=[
            jax.ShapeDtypeStruct((rows, width), bf16),
            jax.ShapeDtypeStruct((rows, far), bf16),
        ]
        + [jax.ShapeDtypeStruct((cap, PAIR), bf16)] * 2,
        input_output_aliases={5 + n: n for n in range(len(held))},
        compiler_params=params(12),
        cost_estimate=cost(2 * 2 * 2 * cap * cap * 256 * 2, 3e6),
        name="attend",
    )(q, k, v, feat_q, feat_k, *held)


def back_body(
    qa_ref, qb_ref, q_ref, k_ref, v_ref, fk_ref, o0_ref, o1_ref, d0_ref, d1_ref, cos_ref, sin_ref,
    out_ref, dol_ref, da_ref, db_ref, dqt_ref,
):
    step = pl.program_id(0)
    half = d0_ref.shape[0]
    cap = 2 * half

    @pl.when(step == 0)
    def _():
        dol_ref[:half] = d0_ref[...]
        dol_ref[half:] = d1_ref[...]
        dol = dol_ref[...]
        slot = lax.broadcasted_iota(jnp.int32, dol.shape, 1) % HD
        wide = dol.astype(f32)
        prod = wide * jnp.concatenate([o0_ref[...], o1_ref[...]], axis=0).astype(f32)
        for head, out in ((0, da_ref), (1, db_ref)):
            mine = lanes_of(head, dol.shape)
            left = -jnp.sum(jnp.where(mine, prod, 0.0), axis=-1, keepdims=True)
            tagged = jnp.where(mine, wide, 0.0)
            for part in range(3):
                head_bits = left.astype(bf16).astype(f32)
                left = left - head_bits
                tagged = jnp.where(
                    jnp.logical_and(jnp.logical_not(mine), slot == NSEG + part), head_bits, tagged
                )
            out[...] = tagged.astype(bf16)
        dqt_ref[...] = jnp.zeros_like(dqt_ref)

    k, v, fk, q, dol = k_ref[...], v_ref[...], fk_ref[...], q_ref[...], dol_ref[...]
    k_turned = k.T
    slot = lax.broadcasted_iota(jnp.int32, v.shape, 1) % HD
    ones = jnp.where(
        jnp.logical_and(slot >= NSEG, slot < NSEG + 3), 1.0, 0.0
    ).astype(bf16)
    dks, dvs = [], []
    for head, qe_ref, de_ref in ((0, qa_ref, da_ref), (1, qb_ref, db_ref)):
        mine = lanes_of(head, k.shape)
        probs = jnp.exp(nt(jnp.where(mine, k, fk), qe_ref[...]))
        dvs.append(nn(probs.astype(bf16), dol))
        ds = (probs * nt(jnp.where(mine, v, ones), de_ref[...])).astype(bf16)
        dks.append(nn(ds, q))
        at = head * HD
        dqt_ref[at : at + HD] += nn(k_turned[at : at + HD], ds)
    first = lanes_of(0, k.shape)
    rows = pl.ds(pl.multiple_of(step * KBLK, KBLK), KBLK)
    dk = jnp.where(first, dks[0], dks[1])
    out_ref[rows, PAIR : 2 * PAIR] = turn(dk, cos_ref[rows], sin_ref[rows], True).astype(bf16)
    out_ref[rows, 2 * PAIR :] = jnp.where(first, dvs[0], dvs[1]).astype(bf16)

    @pl.when(step == cap // KBLK - 1)
    def _():
        dq = dqt_ref[...].T * 0.125
        out_ref[:, :PAIR] = turn(dq, cos_ref[...], sin_ref[...], True).astype(bf16)


def attend_back(pair, qa, qb, q, k, v, feat_k, o0, o1, d0, d1, cosine, sine, deps=()):
    cap = q.shape[0]
    full = whole((cap, PAIR))
    block = pl.BlockSpec((KBLK, PAIR), lambda i: (i, pair))
    part = pl.BlockSpec((KBLK, PAIR), lambda i: (i, 0))
    column = lambda n: pl.BlockSpec((cap // 2, PAIR), lambda i: (0, n))
    return call(
        back_body,
        (qa, qb, q, k, v, feat_k, o0, o1, d0, d1, cosine, sine,),
        deps,
        grid=(cap // KBLK,),
        in_specs=[
            full,
            full,
            pl.BlockSpec((cap, PAIR), lambda i: (0, pair)),
            block,
            block,
            part,
            column(pair),
            column(pair % 2),
            column(pair),
            column(pair % 2),
            full,
            full,
        ],
        out_specs=whole((cap, 3 * PAIR)),
        out_shape=jax.ShapeDtypeStruct((cap, 3 * PAIR), bf16),
        scratch_shapes=[
            pltpu.VMEM((cap, PAIR), bf16),
            pltpu.VMEM((cap, PAIR), bf16),
            pltpu.VMEM((cap, PAIR), bf16),
            pltpu.VMEM((PAIR, cap), f32),
        ],
        compiler_params=params(58),
        cost_estimate=cost(5 * 2 * 2 * cap * cap * 256 * 2, 6e6),
        name="attend_back",
    )


def mlp_body(
    sc_ref, h_ref, cot_ref, oa_ref, ob01, ob2, gain_ref, own_ref, got_ref,
    out_ref, n2_ref, ga_ref, dx_ref, gm_ref, unit_ref, da_ref, db01, db2, gg_ref,
):
    step = pl.program_id(0)
    oa = oa_ref[...]
    ob = jnp.concatenate([ob01[...], ob2[...]], axis=1)
    width = oa.shape[1]
    units = unit_ref.shape[2]
    in0 = slice(width, width + units)
    in1 = slice(width + units, width + 2 * units)
    up = slice(width + 2 * units, width + 3 * units)
    x1 = h_ref[...].astype(f32) + (nn(oa, own_ref[:width]) + nn(ob, got_ref[:width]))
    xh, inv = unit_rows(x1)
    gain = gain_ref[...]
    n2 = (xh * gain).astype(bf16)
    n2_ref[...] = n2
    ids = sc_ref[0] + step * MLP_BLK + lax.broadcasted_iota(jnp.int32, x1.shape, 0)
    g = jnp.where(ids < sc_ref[1], cot_ref[...].astype(f32), 0.0)
    gm = g.astype(bf16)
    gm_ref[...] = gm
    m = jnp.zeros_like(x1)
    dn2 = jnp.zeros_like(x1)
    for n, w_ref in enumerate((own_ref, got_ref)):
        act = nt(n2, w_ref[in0])
        gate = nt(n2, w_ref[in1])
        phi = 0.5 * (1.0 + lax.erf(act * 0.7071067811865476))
        bell = jnp.exp(-0.5 * act * act) * 0.3989422804014327
        gelu = act * phi
        hidden = (gelu * gate).astype(bf16)
        unit_ref[3 * n + 2] = hidden
        m = m + nn(hidden, w_ref[up])
        dh = nt(gm, w_ref[up])
        dact = (dh * gate * (phi + act * bell)).astype(bf16)
        dgate = (dh * gelu).astype(bf16)
        unit_ref[3 * n] = dact
        unit_ref[3 * n + 1] = dgate
        dn2 = dn2 + nn(dact, w_ref[in0]) + nn(dgate, w_ref[in1])
    out_ref[...] = (x1 + m).astype(bf16)

    @pl.when(step == 0)
    def _():
        gg_ref[...] = jnp.zeros_like(gg_ref)

    gg_ref[...] += jnp.sum((dn2 * xh).reshape(-1, 8, x1.shape[1]), axis=0)
    dx = g + norm_back(dn2 * gain, xh, inv)
    dx_ref[...] = dx
    ga = dx.astype(bf16)
    ga_ref[...] = ga
    da_ref[...] = nt(ga, own_ref[:width]).astype(bf16)
    db = nt(ga, got_ref[:width]).astype(bf16)
    db01[...] = db[:, : 2 * PAIR]
    db2[...] = db[:, 2 * PAIR :]


def mlp(scalars, h, cot, o_own, o_got, gain, w_own, w_got, units, deps=()):
    rows, d = h.shape
    row = lambda n: pl.BlockSpec((MLP_BLK, n), lambda i: (i, 0))
    out = lambda n, t=bf16: jax.ShapeDtypeStruct((rows, n), t)
    return call(
        mlp_body,
        (scalars, h, cot, o_own, *o_got, gain, w_own, w_got),
        deps,
        grid=(rows // MLP_BLK,),
        in_specs=[pl.BlockSpec(memory_space=pltpu.SMEM), row(d), row(d)]
        + [row(3 * PAIR), row(2 * PAIR), row(PAIR)]
        + [whole((1, d))]
        + [whole(w_own.shape)] * 2,
        out_specs=[row(d)] * 5
        + [pl.BlockSpec((6, MLP_BLK, units), lambda i: (0, i, 0))]
        + [row(3 * PAIR), row(2 * PAIR), row(PAIR)]
        + [whole((8, d))],
        out_shape=[out(d), out(d), out(d), out(d, f32), out(d)]
        + [jax.ShapeDtypeStruct((6, rows, units), bf16)]
        + [out(3 * PAIR), out(2 * PAIR), out(PAIR)]
        + [jax.ShapeDtypeStruct((8, d), f32)],
        compiler_params=params(26),
        cost_estimate=cost(2 * 2 * 4 * rows * w_own.size, 24e6),
        name="mlp",
    )


def tn(a, b):
    return lax.dot_general(a, b, (((0,), (0,)), ((), ())), preferred_element_type=f32)


def grads_body(
    side, many, core_ref, *refs
):
    outs, unit_ref = refs[:many], refs[many]
    n2_ref, ga_ref, gm_ref, keep_ref, send_ref, held_ref, sems = refs[many + 1 :]
    core = core_ref[0]
    half = keep_ref.shape[0]
    n2, ga, gm = n2_ref[...], ga_ref[...], gm_ref[...]
    parts = [(x[...], ga) for x in outs]
    parts += [(unit_ref[n], n2 if n < 2 else gm) for n in range(3)]
    at = 0
    for left, right in parts:
        res = tn(left, right).astype(bf16)
        held_ref[at : at + res.shape[0]] = res
        at += res.shape[0]
    copies = []
    for out, which in ((keep_ref, core), (send_ref, 1 - core)):
        rows = pl.ds(pl.multiple_of(which * half, 16), half)
        copies.append(pltpu.make_async_copy(held_ref.at[rows], out, sems.at[len(copies)]))
        copies[-1].start()
    for copy in copies:
        copy.wait()


def weight_grads(side, core, o, by_unit, n2, ga, gm, deps=()):
    rows, d = n2.shape
    units = by_unit.shape[2]
    total = 3 * PAIR + 3 * units
    shape = jax.ShapeDtypeStruct((total // 2, d), bf16)
    vmem = pl.BlockSpec(memory_space=pltpu.VMEM)
    anywhere = pl.BlockSpec(memory_space=pl.ANY)
    return call(
        functools.partial(grads_body, side, len(o)),
        (core, *o, by_unit, n2, ga, gm),
        deps,
        grid=(1,),
        in_specs=[pl.BlockSpec(memory_space=pltpu.SMEM)]
        + [whole(x.shape) for x in o]
        + [pl.BlockSpec((3, rows, units), lambda i: (side, 0, 0))]
        + [whole((rows, d))] * 3,
        out_specs=[anywhere] * 2,
        out_shape=[shape] * 2,
        scratch_shapes=[pltpu.VMEM((total, d), bf16), pltpu.SemaphoreType.DMA((2,))],
        compiler_params=params(18),
        cost_estimate=cost(2 * 2 * rows * d * total, 9e6),
        name="weight_grads",
    )


def pair_body(core_ref, back_ref, n1_ref, keep_ref, send_ref, held_ref, sems):
    half = keep_ref.shape[0]
    held_ref[...] = tn(back_ref[...], n1_ref[...]).astype(bf16)
    copies = []
    for out, which in ((keep_ref, core_ref[0]), (send_ref, 1 - core_ref[0])):
        rows = pl.ds(pl.multiple_of(which * half, 16), half)
        copies.append(pltpu.make_async_copy(held_ref.at[rows], out, sems.at[len(copies)]))
        copies[-1].start()
    for copy in copies:
        copy.wait()


def pair_grads(core, back, n1, deps=()):
    cap, d = n1.shape
    shape = jax.ShapeDtypeStruct((3 * PAIR // 2, d), bf16)
    vmem = pl.BlockSpec(memory_space=pltpu.VMEM)
    anywhere = pl.BlockSpec(memory_space=pl.ANY)
    return call(
        pair_body,
        (core, back, n1,),
        deps,
        in_specs=[pl.BlockSpec(memory_space=pltpu.SMEM)] + [vmem] * 2,
        out_specs=[anywhere] * 2,
        out_shape=[shape] * 2,
        scratch_shapes=[pltpu.VMEM((3 * PAIR, d), bf16), pltpu.SemaphoreType.DMA((2,))],
        compiler_params=params(10),
        cost_estimate=cost(2 * 2 * cap * d * 3 * PAIR, 5e6),
        name="pair_grads",
    )


def unstack_body(core_ref, mine_ref, got_ref, a_ref, i_ref, u_ref):
    first = core_ref[0] == 0
    mine, got = mine_ref[...], got_ref[...]
    full = jnp.concatenate([jnp.where(first, mine, got), jnp.where(first, got, mine)], axis=0)
    at, units = a_ref.shape[0], u_ref.shape[0]
    a_ref[...] = full[:at].astype(f32)
    for n in range(2):
        i_ref[n] = full[at + n * units : at + (n + 1) * units].astype(f32)
    u_ref[...] = full[at + 2 * units :].astype(f32)


def unstack(core, mine, got, width, units, deps=()):
    d = mine.shape[1]
    vmem = pl.BlockSpec(memory_space=pltpu.VMEM)
    return call(
        unstack_body,
        (core, mine, got,),
        deps,
        in_specs=[pl.BlockSpec(memory_space=pltpu.SMEM), vmem, vmem],
        out_shape=[
            jax.ShapeDtypeStruct((width, d), f32),
            jax.ShapeDtypeStruct((2, units, d), f32),
            jax.ShapeDtypeStruct((units, d), f32),
        ],
        compiler_params=params(20),
        cost_estimate=cost(1e8, 10e6),
        name="unstack",
    )


def unpair_body(core_ref, mine_ref, got_ref, out_ref):
    first = core_ref[0] == 0
    half = mine_ref.shape[0] // 3
    for pair in range(3):
        rows = slice(pair * half, (pair + 1) * half)
        mine, got = mine_ref[rows], got_ref[rows]
        full = jnp.concatenate([jnp.where(first, mine, got), jnp.where(first, got, mine)], axis=0)
        for n in range(3):
            turned = full[n * PAIR : (n + 1) * PAIR].T.astype(f32)
            out_ref[n, :, pair * PAIR : (pair + 1) * PAIR] = turned


def unpair(core, mine, got, deps=()):
    d = mine.shape[1]
    vmem = pl.BlockSpec(memory_space=pltpu.VMEM)
    return call(
        unpair_body,
        (core, mine, got,),
        deps,
        in_specs=[pl.BlockSpec(memory_space=pltpu.SMEM), vmem, vmem],
        out_shape=jax.ShapeDtypeStruct((3, d, 3 * PAIR), f32),
        compiler_params=params(14),
        cost_estimate=cost(1e8, 6e6),
        name="unpair",
    )


def combine_body(side_ref, k0, c0, k1, c1, own_ref, far_ref, mine_ref, other_ref):
    low = side_ref[0] == 0
    head = own_ref.shape[0]
    half = mine_ref.shape[1]
    for n, (keep, came, out) in enumerate(((k0, c0, own_ref), (k1, c1, far_ref))):
        total = (keep[...].astype(f32) + came[...].astype(f32)).astype(bf16)
        out[...] = total[:head]
        first, second = total[head : head + half], total[head + half :]
        mine_ref[n] = jnp.where(low, first, second)
        other_ref[n] = jnp.where(low, second, first)


def combine(side, keep0, came0, keep1, came1, head, deps=()):
    rows, d = keep0.shape
    half = (rows - head) // 2
    vmem = pl.BlockSpec(memory_space=pltpu.VMEM)
    cut = jax.ShapeDtypeStruct((2, half, d), bf16)
    return call(
        combine_body,
        (side, keep0, came0, keep1, came1),
        deps,
        in_specs=[pl.BlockSpec(memory_space=pltpu.SMEM)] + [vmem] * 4,
        out_shape=[jax.ShapeDtypeStruct((head, d), bf16)] * 2 + [cut] * 2,
        compiler_params=params(20),
        cost_estimate=cost(4 * rows * d, 12e6),
        name="combine",
    )


def tail_body(
    b0, b1, b2, w_ref, h_ref, dn_ref, gg_ref
):
    dn = nn(jnp.concatenate([b0[...], b1[...], b2[...]], axis=1), w_ref[...])
    dn_ref[...] = dn.astype(dn_ref.dtype)
    xh, unused = unit_rows(h_ref[...].astype(f32))

    @pl.when(pl.program_id(0) == 0)
    def _():
        gg_ref[...] = jnp.zeros_like(gg_ref)

    gg_ref[...] += jnp.sum((dn * xh).reshape(-1, 8, dn.shape[1]), axis=0)


def tail(parts, w, h, first, dtype, deps=()):
    rows, d = h.shape
    off = first // BLK
    part = pl.BlockSpec((BLK, 3 * PAIR), lambda i: (i + off, 0))
    row = pl.BlockSpec((BLK, d), lambda i: (i, 0))
    return call(
        tail_body,
        (*parts, w, h,),
        deps,
        grid=(rows // BLK,),
        in_specs=[part] * 3 + [whole(w.shape), row],
        out_specs=[row, whole((8, d))],
        out_shape=[
            jax.ShapeDtypeStruct((rows, d), dtype),
            jax.ShapeDtypeStruct((8, d), f32),
        ],
        compiler_params=params(14),
        cost_estimate=cost(2 * 2 * rows * w.size, 8e6),
        name="tail",
    )


def last_body(h_ref, gain_ref, own_ref, got_ref, dx_ref, out_ref):
    xh, inv = unit_rows(h_ref[...].astype(f32))
    dn = own_ref[...] + got_ref[...].astype(f32)
    out_ref[...] = (dx_ref[...] + norm_back(dn * gain_ref[...], xh, inv)).astype(bf16)


def last(h, gain, own, got, dx, deps=()):
    rows, d = h.shape
    row = pl.BlockSpec((BLK, d), lambda i: (i, 0))
    return call(
        last_body,
        (h, gain, own, got, dx,),
        deps,
        grid=(rows // BLK,),
        in_specs=[row, whole((1, d)), row, row, row],
        out_specs=row,
        out_shape=jax.ShapeDtypeStruct((rows, d), bf16),
        compiler_params=params(12),
        cost_estimate=cost(40 * rows * d, 9e6),
        name="last",
    )


def on_device(dp, hidden_in, bounds, attn_gain, w_qkv, w_attn, mlp_gain, w_in, w_out, cotangent):
    rows, d = hidden_in.shape
    cap = 2 * rows
    width = w_attn.shape[0]
    units = w_out.shape[0]
    shard = lax.axis_index("tensor")
    place = lax.axis_index("dp")
    core = place % 2
    core_at = core.astype(jnp.int32).reshape(1)
    side = (place // 2) % 2
    groups = [list(range(c, dp, 2)) for c in range(2)]
    bits = [1 << n for n in range(dp.bit_length() - 1)]

    def over_y(x):
        return lax.ppermute(x, "tensor", [(0, 1), (1, 0)])

    def over(x, bit):
        return lax.ppermute(x, "dp", [(n, n ^ bit) for n in range(dp)])

    def over_core(x):
        return over(x, 1)

    def add(a, b):
        return (a.astype(f32) + b.astype(f32)).astype(bf16)

    def in_order(first, mine, got):
        return jnp.concatenate(
            [jnp.where(first, mine, got), jnp.where(first, got, mine)], axis=0
        )

    hidden_got = over_y(hidden_in)
    cosine, sine, feat_q, feat_k = tables(
        bounds, (shard * rows).astype(jnp.int32).reshape(1), cap
    )
    gain_a = attn_gain.reshape(1, d)
    gain_m = mlp_gain.reshape(1, d)
    held = qkv(hidden_in, gain_a, w_qkv, cosine, sine, 0, ())
    w_own, w_qkv_turned = stack(w_attn, jnp.swapaxes(w_in, 1, 2), w_out, w_qkv)
    quarter = w_own.shape[0] // 4
    piece = lax.dynamic_slice_in_dim(w_own, (2 * core + side) * quarter, quarter, 0)
    hidden_got, piece, held = lax.optimization_barrier((hidden_got, piece, held))
    n1, q, k, v = qkv(hidden_got, gain_a, w_qkv, cosine, sine, rows, held)

    def after(x, *done):
        return lax.optimization_barrier((x, done))[0]

    cut = (quarter // 2 + 15) // 16 * 16
    cuts = (piece[:cut], piece[cut:])
    from_y = [over_y(x) for x in cuts]
    first = attend(0, q, k, v, feat_q, feat_k, ())
    from_x = [over(after(from_y[0], first[0]), 2)]
    second = attend(1, q, k, v, feat_q, feat_k, first[:2])
    from_x.append(over(after(from_y[1], second[0]), 2))
    third = attend(2, q, k, v, feat_q, feat_k, second[:1])
    o_got = [over_y(second[1]), over_y(third[1])]
    pieces = [from_y[0], from_x[0], over_core(from_y[0]), over_core(after(from_x[0], second[0]))]
    pieces += [from_y[1], from_x[1], over_core(from_y[1]), over_core(after(from_x[1], third[0]))]
    at = jnp.arange(2, dtype=jnp.int32)[:, None] * cut + jnp.stack(
        [(2 * c + s) * quarter for c in (core, 1 - core) for s in (side, 1 - side)]
    )
    o_own = third[0]
    o_far = (second[1], second[1], third[1])
    q_tag = [x[2:] for x in (first, second, third)]
    w_got = assemble(at.reshape(8), pieces, w_own.shape, (o_got[0],))
    scalars = jnp.stack([shard * rows, bounds[0, NSEG - 1]]).astype(jnp.int32)
    (
        hidden_out, n2, ga, dx, gm, by_unit, d_own, db01, db2, gg_mlp,
    ) = mlp(scalars, hidden_in, cotangent, o_own, o_got, gain_m, w_own, w_got, units)
    d_got = [over_y(db01), over_y(db2)]
    d_far = (d_got[0], d_got[0], d_got[1])

    def back(pair, *deps):
        out = attend_back(
            pair, *q_tag[pair], q, k, v, feat_k, o_own, o_far[pair], d_own, d_far[pair],
            cosine, sine, deps,
        )
        return out

    def pair_sum(out, *deps):
        keep, send = pair_grads(core_at, out, n1, deps)
        return add(keep, over_core(send))

    def split(x, bit):
        low = (place & bit) == 0
        half = x.shape[0] // 2
        first, second = x[:half], x[half:]
        return jnp.where(low, first, second), jnp.where(low, second, first)

    def merge(x, bit):
        return in_order((place & bit) == 0, x, over(x, bit))

    def over_rest(x):
        if len(bits) < 3:
            return x
        mine, other = split(x, bits[2])
        mine = add(mine, over(other, bits[2]))
        for bit in bits[3:]:
            mine = add(mine, over(mine, bit))
        return merge(mine, bits[2])

    keep1, send1 = weight_grads(1, core_at, o_got, by_unit, n2, ga, gm)
    keep0, send0 = weight_grads(0, core_at, (o_own,), by_unit, n2, ga, gm, (keep1, d_got[0]))
    came1 = over_core(after(send1, d_got[0]))
    came0 = over_core(send0)
    head = send0.shape[0] // 32 * 16 - 16
    own_a, far_a, mine_b, other_b = combine(
        side.astype(jnp.int32).reshape(1), keep0, came0, keep1, came1, head
    )
    got_a, got_b = over_y(far_a), over(other_b, 2)
    back0 = back(0, mine_b, far_a)
    keep, send = pair_grads(core_at, back0, n1)
    pair0 = add(keep, over_core(send))

    own_a = add(own_a, after(got_a, back0))
    mine_b = add(mine_b, after(got_b, back0))
    mine_a, other_a = split(own_a, 2)
    got_a, got_b = over(other_a, 2), over_y(mine_b[1])
    back1 = back(1, keep, mine_a, mine_b)
    keep, send = pair_grads(core_at, back1, n1)
    pair1 = add(keep, over_core(send))

    got_a, got_b = after((got_a, got_b), back1)
    mine = jnp.concatenate([add(mine_a, got_a), add(mine_b[0], got_b)], axis=0)
    if len(bits) > 2:
        mine, other = split(mine, bits[2])
        got = over(other, bits[2])
    back2 = back(2, keep, mine)
    if len(bits) > 2:
        mine = add(mine, after(got, back2))
    parts = (back0, back1, back2)
    dn_other, gg_other = tail(parts, w_qkv_turned, hidden_got, rows, bf16, (mine,))
    dn_got = over_y(dn_other)
    keep, send = pair_grads(core_at, back2, n1, (dn_other,))
    pair2 = add(keep, over_core(send))
    dn_own, gg_own = tail(parts, w_qkv_turned, hidden_in, 0, f32, (keep,))

    if len(bits) > 2:
        for bit in bits[3:]:
            mine = add(mine, over(mine, bit))
        mine = merge(mine, bits[2])
    grad_in = last(hidden_in, gain_a, dn_own, dn_got, dx)
    got = over(after(mine, grad_in), 2)
    low = (place & 2) == 0
    grads = jnp.concatenate(
        [in_order(low, mine[: head // 2], got[: head // 2]),
         in_order(low, mine[head // 2 :], got[head // 2 :])],
        axis=0,
    )

    gains = jnp.stack(
        [jnp.sum(gg_own, axis=0) + jnp.sum(gg_other, axis=0), jnp.sum(gg_mlp, axis=0)]
    )
    gains = gains + over_core(gains)
    gains = gains + over(gains, 2)
    gains = jnp.pad(gains, ((0, 14), (0, 0))).astype(bf16)
    mine, other = split(jnp.concatenate([pair0, pair1, pair2], axis=0), 2)
    mine = add(mine, over(other, 2))
    count = mine.shape[0]
    mine = over_rest(jnp.concatenate([mine, gains], axis=0))
    gains = mine[count : count + 2].astype(f32)
    gains = gains + over_y(gains)
    pairs = merge(mine[:count], 2)

    grad_w_attn, grad_w_in, grad_w_out = unstack(core_at, grads, over_core(grads), width, units)
    grad_w_in = jnp.swapaxes(grad_w_in, 1, 2)
    grad_w_qkv = unpair(core_at, pairs, over_core(pairs))
    return (
        hidden_out,
        grad_in,
        gains[0],
        grad_w_qkv,
        grad_w_attn,
        gains[1],
        grad_w_in,
        grad_w_out,
    )


def solution(mesh):
    in_specs = (
        P(("dp", "tensor"), None),
        P("dp", None),
        P(),
        P(None, None, "tensor"),
        P("tensor", None),
        P(),
        P(None, None, "tensor"),
        P("tensor", None),
        P(("dp", "tensor"), None),
    )
    out_specs = (
        P(("dp", "tensor"), None),
        P(("dp", "tensor"), None),
        P(),
        P(None, None, "tensor"),
        P("tensor", None),
        P(),
        P(None, None, "tensor"),
        P("tensor", None),
    )
    return jax.shard_map(
        functools.partial(on_device, mesh.shape["dp"]),
        mesh=mesh,
        in_specs=in_specs,
        out_specs=out_specs,
        check_vma=False,
    )
```

```python
import functools

import jax
import jax.numpy as jnp
import numpy as np
from jax import lax
from jax.experimental import pallas as pl
from jax.experimental.pallas import tpu as pltpu
from jax.sharding import PartitionSpec as P

HD = 64
NSEG = 6
PAIR = 2 * HD
BLK = 384
MLP_BLK = 256
COST = 0.15
KBLK = 512
rope_theta = 160000.0
norm_eps = 1e-05
masked_score = -1e30
f32 = jnp.float32
bf16 = jnp.bfloat16


def params(mib):
    return pltpu.CompilerParams(vmem_limit_bytes=mib * 1024 * 1024)


def cost(flops, nbytes):
    return pl.CostEstimate(
        flops=int(flops * COST), bytes_accessed=int(nbytes * COST), transcendentals=0
    )


def nn(a, b):
    return jnp.dot(a, b, preferred_element_type=f32)


def nt(a, b):
    return lax.dot_general(a, b, (((1,), (1,)), ((), ())), preferred_element_type=f32)


def call(body, args, deps=(), *, in_specs, **kw):
    first = len(in_specs)

    def run(*refs):
        body(*refs[:first], *refs[first + len(deps) :])

    return pl.pallas_call(
        run, in_specs=list(in_specs) + [pl.BlockSpec(memory_space=pl.ANY)] * len(deps), **kw
    )(*args, *deps)


def whole(shape):
    return pl.BlockSpec(shape, lambda i: (0,) * len(shape))


def unit_rows(x):
    centred = x - jnp.mean(x, axis=-1, keepdims=True)
    inv = lax.rsqrt(jnp.mean(centred * centred, axis=-1, keepdims=True) + norm_eps)
    return centred * inv, inv


def norm_back(e, xh, inv):
    return inv * (
        e - jnp.mean(e, axis=-1, keepdims=True) - xh * jnp.mean(e * xh, axis=-1, keepdims=True)
    )


def turn(x, cosine, sine, back):
    lane = lax.broadcasted_iota(jnp.int32, x.shape, 1) % HD
    other = jnp.where(lane < HD // 2, pltpu.roll(x, PAIR - HD // 2, 1), pltpu.roll(x, HD // 2, 1))
    return x * cosine - other * sine if back else x * cosine + other * sine


def sincos(x):
    turns = jnp.floor(x * 0.6366197723675814 + 0.5)
    r = ((x - turns * 1.5703125) - turns * 4.837512969970703125e-4) - turns * 7.54978995489188e-8
    z = r * r
    s = r + r * z * (-1.6666654611e-1 + z * (8.3321608736e-3 + z * -1.9515295891e-4))
    c = 1.0 - 0.5 * z + z * z * (
        4.166664568298827e-2 + z * (-1.388731625493765e-3 + z * 2.443315711809948e-5)
    )
    quarter = turns.astype(jnp.int32) & 3
    odd = (quarter & 1) == 1
    sine = jnp.where(odd, c, s)
    cosine = jnp.where(odd, s, c)
    sine = jnp.where(quarter >= 2, -sine, sine)
    cosine = jnp.where(jnp.logical_or(quarter == 1, quarter == 2), -cosine, cosine)
    return sine, cosine


def tables_body(edge_ref, first_ref, freq_ref, cos_ref, sin_ref, fq_ref, fk_ref):
    cap = cos_ref.shape[0]
    ids = lax.broadcasted_iota(jnp.int32, (cap, PAIR), 0) + first_ref[0]
    ids = jnp.where(ids >= cap, ids - cap, ids)
    lane = lax.broadcasted_iota(jnp.int32, ids.shape, 1)
    seg = jnp.zeros(ids.shape, jnp.int32)
    begin = jnp.zeros(ids.shape, jnp.int32)
    for n in range(1, NSEG):
        passed = ids >= edge_ref[0, n]
        seg = jnp.where(passed, seg + 1, seg)
        begin = jnp.where(passed, edge_ref[0, n], begin)
    angle = (ids - begin).astype(f32) * freq_ref[...]
    sine, cosine = sincos(angle)
    slot = lane % HD
    cos_ref[...] = cosine
    sin_ref[...] = jnp.where(slot < HD // 2, -sine, sine)
    same = slot == seg
    fq_ref[...] = jnp.where(same, 1.0, 0.0).astype(bf16)
    fk_ref[...] = jnp.where(
        slot < NSEG,
        jnp.where(same, 0.0, masked_score),
        jnp.where(slot < NSEG + 3, 1.0, 0.0),
    ).astype(bf16)


def tables(edges, first, cap):
    steps = 2.0 * (np.arange(PAIR) % (HD // 2)) / HD
    freq = jnp.asarray(np.exp(-steps * np.log(rope_theta))[None].astype(np.float32))
    smem = pl.BlockSpec(memory_space=pltpu.SMEM)
    table = lambda t: jax.ShapeDtypeStruct((cap, PAIR), t)
    return pl.pallas_call(
        tables_body,
        in_specs=[smem, smem, pl.BlockSpec(memory_space=pltpu.VMEM)],
        out_shape=[table(f32), table(f32), table(bf16), table(bf16)],
        compiler_params=params(8),
        cost_estimate=cost(80 * cap * PAIR, 3e6),
        name="tables",
    )(edges, first, freq)


def stack_body(a_ref, i_ref, u_ref, w_ref, out_ref, qkv_ref):
    at = a_ref.shape[0]
    units = u_ref.shape[0]
    width = w_ref.shape[2]
    out_ref[:at] = a_ref[...]
    for n in range(2):
        out_ref[at + n * units : at + (n + 1) * units] = i_ref[n]
    out_ref[at + 2 * units :] = u_ref[...]
    for n in range(3):
        turned = w_ref[n].T
        for pair in range(width // PAIR):
            to = (3 * pair + n) * PAIR
            qkv_ref[to : to + PAIR] = turned[pair * PAIR : (pair + 1) * PAIR]


def stack(w_attn, w_in_turned, w_out, w_qkv, deps=()):
    at, d = w_attn.shape
    rows = at + 3 * w_out.shape[0]
    vmem = pl.BlockSpec(memory_space=pltpu.VMEM)
    return call(
        stack_body,
        (w_attn, w_in_turned, w_out, w_qkv),
        deps,
        in_specs=[vmem] * 4,
        out_shape=[
            jax.ShapeDtypeStruct((rows, d), bf16),
            jax.ShapeDtypeStruct((3 * w_qkv.shape[2], d), bf16),
        ],
        compiler_params=params(12),
        cost_estimate=cost(1e8, 10e6),
        name="stack",
    )


def qkv_body(h_ref, gain_ref, w_ref, cos_ref, sin_ref, *refs):
    n1_ref, q_ref, k_ref, v_ref = refs[-4:]
    unit, inv = unit_rows(h_ref[...].astype(f32))
    n1 = (unit * gain_ref[...]).astype(bf16)
    n1_ref[...] = n1
    cosine, sine = cos_ref[...], sin_ref[...]
    width = w_ref.shape[2]
    for which, out, scale in ((0, q_ref, 0.125), (1, k_ref, 1.0)):
        full = nn(n1, w_ref[which])
        for at in range(0, width, PAIR):
            turned = turn(full[:, at : at + PAIR], cosine, sine, False).astype(bf16)
            if scale != 1.0:
                turned = (turned.astype(f32) * scale).astype(bf16)
            out[:, at : at + PAIR] = turned
    v_ref[...] = nn(n1, w_ref[2]).astype(bf16)


def qkv(h, gain, w, cosine, sine, first, held, deps=()):
    rows, d = h.shape
    cap, width = cosine.shape[0], w.shape[2]
    off = first // BLK
    by_row = lambda n: pl.BlockSpec((BLK, n), lambda i: (i + off, 0))
    shapes = [jax.ShapeDtypeStruct((cap, n), bf16) for n in (d, width, width, width)]
    return call(
        qkv_body,
        (h, gain, w, cosine, sine, *held),
        deps,
        grid=(rows // BLK,),
        in_specs=[
            pl.BlockSpec((BLK, d), lambda i: (i, 0)),
            whole((1, d)),
            whole(w.shape),
            by_row(PAIR),
            by_row(PAIR),
        ]
        + [pl.BlockSpec(memory_space=pl.ANY)] * len(held),
        out_specs=[by_row(d), by_row(width), by_row(width), by_row(width)],
        out_shape=shapes,
        input_output_aliases={5 + n: n for n in range(len(held))},
        compiler_params=params(14),
        cost_estimate=cost(2 * 2 * rows * d * 3 * width, 12e6),
        name="qkv",
    )


def assemble_body(at_ref, *refs):
    pieces, out_ref, sems = refs[:-2], refs[-2], refs[-1]
    copies = []
    for n, ref in enumerate(pieces):
        to = pl.ds(pl.multiple_of(at_ref[n], 8), ref.shape[0])
        copies.append(pltpu.make_async_copy(ref, out_ref.at[to], sems.at[n]))
        copies[-1].start()
    for copy in copies:
        copy.wait()


def assemble(at, pieces, shape, deps=()):
    anywhere = pl.BlockSpec(memory_space=pl.ANY)
    return call(
        assemble_body,
        (at, *pieces),
        deps,
        in_specs=[pl.BlockSpec(memory_space=pltpu.SMEM)] + [anywhere] * len(pieces),
        out_specs=pl.BlockSpec(memory_space=pltpu.VMEM),
        out_shape=jax.ShapeDtypeStruct(shape, bf16),
        scratch_shapes=[pltpu.SemaphoreType.DMA((len(pieces),))],
        compiler_params=params(8),
        cost_estimate=cost(1e6, 6e6),
        name="assemble",
    )


def lanes_of(head, shape):
    lane = lax.broadcasted_iota(jnp.int32, shape, 1)
    return (lane < HD) if head == 0 else (lane >= HD)


def attend_body(q_ref, k_ref, v_ref, fq_ref, fk_ref, *refs):
    o0_ref, o1_ref, qa_ref, qb_ref = refs[-4:]
    q, k, v, fq, fk = q_ref[...], k_ref[...], v_ref[...], fq_ref[...], fk_ref[...]
    v_turned = v.T
    rows = q.shape[0]
    line = lax.broadcasted_iota(jnp.int32, (PAIR, rows), 0)
    tag = jnp.zeros((PAIR, rows), f32)
    mixed = []
    for head in (0, 1):
        q_in = jnp.where(lanes_of(head, q.shape), q, fq)
        k_in = jnp.where(lanes_of(head, k.shape), k, fk)
        score = nt(k_in, q_in)
        top = jnp.max(score, axis=0, keepdims=True)
        expo = jnp.exp(score - top)
        total = jnp.sum(expo, axis=0, keepdims=True)
        at = head * HD
        mixed.append(nn(v_turned[at : at + HD], expo.astype(bf16)) * (1.0 / total))
        left = -(top + jnp.log(total))
        for part in range(3):
            head_bits = left.astype(bf16).astype(f32)
            left = left - head_bits
            tag = jnp.where(line == HD - at + NSEG + part, head_bits, tag)
    o = jnp.concatenate(mixed, axis=0).T.astype(bf16)
    tag = tag.T
    fq = fq.astype(f32) + tag
    wide = q.astype(f32)
    qa_ref[...] = jnp.where(lanes_of(0, q.shape), wide, fq).astype(bf16)
    qb_ref[...] = jnp.where(lanes_of(1, q.shape), wide, fq).astype(bf16)

    @pl.when(pl.program_id(0) == 0)
    def _():
        o0_ref[...] = o

    @pl.when(pl.program_id(0) == 1)
    def _():
        o1_ref[...] = o


def attend(pair, q, k, v, feat_q, feat_k, held):
    cap, width = q.shape
    rows = cap // 2
    part = pl.BlockSpec((rows, PAIR), lambda i: (i, 0))
    full = pl.BlockSpec((cap, PAIR), lambda i: (0, pair))
    column = lambda n: pl.BlockSpec((rows, PAIR), lambda i: (0, n))
    far = width - PAIR if pair < 2 else PAIR
    return pl.pallas_call(
        attend_body,
        grid=(2,),
        in_specs=[
            pl.BlockSpec((rows, PAIR), lambda i: (i, pair)),
            full,
            full,
            part,
            whole((cap, PAIR)),
        ]
        + [pl.BlockSpec(memory_space=pl.ANY)] * len(held),
        out_specs=[column(pair), column(pair % 2)] + [part] * 2,
        out_shape=[
            jax.ShapeDtypeStruct((rows, width), bf16),
            jax.ShapeDtypeStruct((rows, far), bf16),
        ]
        + [jax.ShapeDtypeStruct((cap, PAIR), bf16)] * 2,
        input_output_aliases={5 + n: n for n in range(len(held))},
        compiler_params=params(12),
        cost_estimate=cost(2 * 2 * 2 * cap * cap * 256 * 2, 3e6),
        name="attend",
    )(q, k, v, feat_q, feat_k, *held)


def back_body(
    start, begun, ends, qa_ref, qb_ref, q_ref, k_ref, v_ref, fk_ref, o0_ref, o1_ref, d0_ref, d1_ref, cos_ref, sin_ref,
    *refs,
):
    dqt_in, low_in = refs[:2] if begun else (None, None)
    outs = refs[2:-4] if begun else refs[:-4]
    dol_ref, da_ref, db_ref, dqt_ref = refs[-4:]
    out_ref = outs[0]
    step = pl.program_id(0)
    half = d0_ref.shape[0]
    cap = 2 * half

    @pl.when(step == 0)
    def _():
        dol_ref[:half] = d0_ref[...]
        dol_ref[half:] = d1_ref[...]
        dol = dol_ref[...]
        slot = lax.broadcasted_iota(jnp.int32, dol.shape, 1) % HD
        wide = dol.astype(f32)
        prod = wide * jnp.concatenate([o0_ref[...], o1_ref[...]], axis=0).astype(f32)
        for head, out in ((0, da_ref), (1, db_ref)):
            mine = lanes_of(head, dol.shape)
            left = -jnp.sum(jnp.where(mine, prod, 0.0), axis=-1, keepdims=True)
            tagged = jnp.where(mine, wide, 0.0)
            for part in range(3):
                head_bits = left.astype(bf16).astype(f32)
                left = left - head_bits
                tagged = jnp.where(
                    jnp.logical_and(jnp.logical_not(mine), slot == NSEG + part), head_bits, tagged
                )
            out[...] = tagged.astype(bf16)
        if begun:
            dqt_ref[...] = dqt_in[...]
            out_ref[: start * KBLK, PAIR:] = low_in[...]
        else:
            dqt_ref[...] = jnp.zeros_like(dqt_ref)

    k, v, fk, q, dol = k_ref[...], v_ref[...], fk_ref[...], q_ref[...], dol_ref[...]
    k_turned = k.T
    slot = lax.broadcasted_iota(jnp.int32, v.shape, 1) % HD
    ones = jnp.where(
        jnp.logical_and(slot >= NSEG, slot < NSEG + 3), 1.0, 0.0
    ).astype(bf16)
    dks, dvs = [], []
    for head, qe_ref, de_ref in ((0, qa_ref, da_ref), (1, qb_ref, db_ref)):
        mine = lanes_of(head, k.shape)
        probs = jnp.exp(nt(jnp.where(mine, k, fk), qe_ref[...]))
        dvs.append(nn(probs.astype(bf16), dol))
        ds = (probs * nt(jnp.where(mine, v, ones), de_ref[...])).astype(bf16)
        dks.append(nn(ds, q))
        at = head * HD
        dqt_ref[at : at + HD] += nn(k_turned[at : at + HD], ds)
    first = lanes_of(0, k.shape)
    rows = pl.ds(pl.multiple_of((step + start) * KBLK, KBLK), KBLK)
    dk = turn(jnp.where(first, dks[0], dks[1]), cos_ref[rows], sin_ref[rows], True).astype(bf16)
    dv = jnp.where(first, dvs[0], dvs[1]).astype(bf16)
    if ends:
        out_ref[rows, PAIR : 2 * PAIR] = dk
        out_ref[rows, 2 * PAIR :] = dv
    else:
        outs[1][:, :PAIR] = dk
        outs[1][:, PAIR:] = dv

    @pl.when(step == pl.num_programs(0) - 1)
    def _():
        if ends:
            dq = dqt_ref[...].T * 0.125
            out_ref[:, :PAIR] = turn(dq, cos_ref[...], sin_ref[...], True).astype(bf16)
        else:
            out_ref[...] = dqt_ref[...]


def attend_back(
    pair, start, stop, begun, qa, qb, q, k, v, feat_k, o0, o1, d0, d1, cosine, sine, deps=()
):
    cap = q.shape[0]
    ends = stop * KBLK == cap
    full = whole((cap, PAIR))
    block = pl.BlockSpec((KBLK, PAIR), lambda i: (i + start, pair))
    part = pl.BlockSpec((KBLK, PAIR), lambda i: (i + start, 0))
    column = lambda n: pl.BlockSpec((cap // 2, PAIR), lambda i: (0, n))
    if ends:
        out_specs = [whole((cap, 3 * PAIR))]
        out_shape = [jax.ShapeDtypeStruct((cap, 3 * PAIR), bf16)]
    else:
        out_specs = [whole((PAIR, cap)), pl.BlockSpec((KBLK, 2 * PAIR), lambda i: (i, 0))]
        out_shape = [
            jax.ShapeDtypeStruct((PAIR, cap), f32),
            jax.ShapeDtypeStruct(((stop - start) * KBLK, 2 * PAIR), bf16),
        ]
    return call(
        functools.partial(back_body, start, bool(begun), ends),
        (qa, qb, q, k, v, feat_k, o0, o1, d0, d1, cosine, sine, *begun),
        deps,
        grid=(stop - start,),
        in_specs=[
            full,
            full,
            pl.BlockSpec((cap, PAIR), lambda i: (0, pair)),
            block,
            block,
            part,
            column(pair),
            column(pair % 2),
            column(pair),
            column(pair % 2),
            full,
            full,
        ]
        + [whole(x.shape) for x in begun],
        out_specs=out_specs,
        out_shape=out_shape,
        scratch_shapes=[
            pltpu.VMEM((cap, PAIR), bf16),
            pltpu.VMEM((cap, PAIR), bf16),
            pltpu.VMEM((cap, PAIR), bf16),
            pltpu.VMEM((PAIR, cap), f32),
        ],
        compiler_params=params(58),
        cost_estimate=cost(5 * 2 * 2 * (stop - start) * KBLK * cap * 256 * 2, 6e6),
        name="attend_back",
    )


def mlp_body(
    sc_ref, h_ref, cot_ref, oa_ref, ob01, ob2, gain_ref, own_ref, got_ref,
    out_ref, n2_ref, ga_ref, dx_ref, gm_ref, unit_ref, da_ref, db01, db2, gg_ref,
):
    step = pl.program_id(0)
    oa = oa_ref[...]
    ob = jnp.concatenate([ob01[...], ob2[...]], axis=1)
    width = oa.shape[1]
    units = unit_ref.shape[2]
    in0 = slice(width, width + units)
    in1 = slice(width + units, width + 2 * units)
    up = slice(width + 2 * units, width + 3 * units)
    x1 = h_ref[...].astype(f32) + (nn(oa, own_ref[:width]) + nn(ob, got_ref[:width]))
    xh, inv = unit_rows(x1)
    gain = gain_ref[...]
    n2 = (xh * gain).astype(bf16)
    n2_ref[...] = n2
    ids = sc_ref[0] + step * MLP_BLK + lax.broadcasted_iota(jnp.int32, x1.shape, 0)
    g = jnp.where(ids < sc_ref[1], cot_ref[...].astype(f32), 0.0)
    gm = g.astype(bf16)
    gm_ref[...] = gm
    m = jnp.zeros_like(x1)
    dn2 = jnp.zeros_like(x1)
    for n, w_ref in enumerate((own_ref, got_ref)):
        act = nt(n2, w_ref[in0])
        gate = nt(n2, w_ref[in1])
        phi = 0.5 * (1.0 + lax.erf(act * 0.7071067811865476))
        bell = jnp.exp(-0.5 * act * act) * 0.3989422804014327
        gelu = act * phi
        hidden = (gelu * gate).astype(bf16)
        unit_ref[3 * n + 2] = hidden
        m = m + nn(hidden, w_ref[up])
        dh = nt(gm, w_ref[up])
        dact = (dh * gate * (phi + act * bell)).astype(bf16)
        dgate = (dh * gelu).astype(bf16)
        unit_ref[3 * n] = dact
        unit_ref[3 * n + 1] = dgate
        dn2 = dn2 + nn(dact, w_ref[in0]) + nn(dgate, w_ref[in1])
    out_ref[...] = (x1 + m).astype(bf16)

    @pl.when(step == 0)
    def _():
        gg_ref[...] = jnp.zeros_like(gg_ref)

    gg_ref[...] += jnp.sum((dn2 * xh).reshape(-1, 8, x1.shape[1]), axis=0)
    dx = g + norm_back(dn2 * gain, xh, inv)
    dx_ref[...] = dx
    ga = dx.astype(bf16)
    ga_ref[...] = ga
    da_ref[...] = nt(ga, own_ref[:width]).astype(bf16)
    db = nt(ga, got_ref[:width]).astype(bf16)
    db01[...] = db[:, : 2 * PAIR]
    db2[...] = db[:, 2 * PAIR :]


def mlp(scalars, h, cot, o_own, o_got, gain, w_own, w_got, units, deps=()):
    rows, d = h.shape
    row = lambda n: pl.BlockSpec((MLP_BLK, n), lambda i: (i, 0))
    out = lambda n, t=bf16: jax.ShapeDtypeStruct((rows, n), t)
    return call(
        mlp_body,
        (scalars, h, cot, o_own, *o_got, gain, w_own, w_got),
        deps,
        grid=(rows // MLP_BLK,),
        in_specs=[pl.BlockSpec(memory_space=pltpu.SMEM), row(d), row(d)]
        + [row(3 * PAIR), row(2 * PAIR), row(PAIR)]
        + [whole((1, d))]
        + [whole(w_own.shape)] * 2,
        out_specs=[row(d)] * 5
        + [pl.BlockSpec((6, MLP_BLK, units), lambda i: (0, i, 0))]
        + [row(3 * PAIR), row(2 * PAIR), row(PAIR)]
        + [whole((8, d))],
        out_shape=[out(d), out(d), out(d), out(d, f32), out(d)]
        + [jax.ShapeDtypeStruct((6, rows, units), bf16)]
        + [out(3 * PAIR), out(2 * PAIR), out(PAIR)]
        + [jax.ShapeDtypeStruct((8, d), f32)],
        compiler_params=params(26),
        cost_estimate=cost(2 * 2 * 4 * rows * w_own.size, 24e6),
        name="mlp",
    )


def tn(a, b):
    return lax.dot_general(a, b, (((0,), (0,)), ((), ())), preferred_element_type=f32)


def grads_body(
    side, many, core_ref, *refs
):
    outs, unit_ref = refs[:many], refs[many]
    n2_ref, ga_ref, gm_ref, keep_ref, send_ref, held_ref, sems = refs[many + 1 :]
    core = core_ref[0]
    half = keep_ref.shape[0]
    n2, ga, gm = n2_ref[...], ga_ref[...], gm_ref[...]
    parts = [(x[...], ga) for x in outs]
    parts += [(unit_ref[n], n2 if n < 2 else gm) for n in range(3)]
    at = 0
    for left, right in parts:
        res = tn(left, right).astype(bf16)
        held_ref[at : at + res.shape[0]] = res
        at += res.shape[0]
    copies = []
    for out, which in ((keep_ref, core), (send_ref, 1 - core)):
        rows = pl.ds(pl.multiple_of(which * half, 16), half)
        copies.append(pltpu.make_async_copy(held_ref.at[rows], out, sems.at[len(copies)]))
        copies[-1].start()
    for copy in copies:
        copy.wait()


def weight_grads(side, core, o, by_unit, n2, ga, gm, deps=()):
    rows, d = n2.shape
    units = by_unit.shape[2]
    total = 3 * PAIR + 3 * units
    shape = jax.ShapeDtypeStruct((total // 2, d), bf16)
    vmem = pl.BlockSpec(memory_space=pltpu.VMEM)
    anywhere = pl.BlockSpec(memory_space=pl.ANY)
    return call(
        functools.partial(grads_body, side, len(o)),
        (core, *o, by_unit, n2, ga, gm),
        deps,
        grid=(1,),
        in_specs=[pl.BlockSpec(memory_space=pltpu.SMEM)]
        + [whole(x.shape) for x in o]
        + [pl.BlockSpec((3, rows, units), lambda i: (side, 0, 0))]
        + [whole((rows, d))] * 3,
        out_specs=[anywhere] * 2,
        out_shape=[shape] * 2,
        scratch_shapes=[pltpu.VMEM((total, d), bf16), pltpu.SemaphoreType.DMA((2,))],
        compiler_params=params(18),
        cost_estimate=cost(1e5, 1e4),
        name="weight_grads",
    )


def pair_body(core_ref, back_ref, n1_ref, keep_ref, send_ref, held_ref, sems):
    half = keep_ref.shape[0]
    held_ref[...] = tn(back_ref[...], n1_ref[...]).astype(bf16)
    copies = []
    for out, which in ((keep_ref, core_ref[0]), (send_ref, 1 - core_ref[0])):
        rows = pl.ds(pl.multiple_of(which * half, 16), half)
        copies.append(pltpu.make_async_copy(held_ref.at[rows], out, sems.at[len(copies)]))
        copies[-1].start()
    for copy in copies:
        copy.wait()


def pair_grads(core, back, n1, deps=()):
    cap, d = n1.shape
    rows = back.shape[1]
    shape = jax.ShapeDtypeStruct((rows // 2, d), bf16)
    vmem = pl.BlockSpec(memory_space=pltpu.VMEM)
    anywhere = pl.BlockSpec(memory_space=pl.ANY)
    return call(
        pair_body,
        (core, back, n1),
        deps,
        in_specs=[pl.BlockSpec(memory_space=pltpu.SMEM)] + [vmem] * 2,
        out_specs=[anywhere] * 2,
        out_shape=[shape] * 2,
        scratch_shapes=[pltpu.VMEM((rows, d), bf16), pltpu.SemaphoreType.DMA((2,))],
        compiler_params=params(10),
        cost_estimate=cost(1e5, 1e4),
        name="pair_grads",
    )


def gains_body(own_ref, other_ref, mlp_ref, out_ref):
    a = jnp.sum(own_ref[...] + other_ref[...], axis=0, keepdims=True)
    m = jnp.sum(mlp_ref[...], axis=0, keepdims=True)
    line = lax.broadcasted_iota(jnp.int32, out_ref.shape, 0)
    out_ref[...] = jnp.where(line == 0, a, jnp.where(line == 1, m, 0.0))


def gain_rows(own, other, mlp_part):
    vmem = pl.BlockSpec(memory_space=pltpu.VMEM)
    return call(
        gains_body,
        (own, other, mlp_part),
        in_specs=[vmem] * 3,
        out_shape=jax.ShapeDtypeStruct(own.shape, f32),
        compiler_params=params(8),
        cost_estimate=cost(1e5, 1e4),
        name="gain_rows",
    )


def unstack_body(core_ref, mine_ref, got_ref, a_ref, i_ref, u_ref):
    first = core_ref[0] == 0
    mine, got = mine_ref[...], got_ref[...]
    full = jnp.concatenate([jnp.where(first, mine, got), jnp.where(first, got, mine)], axis=0)
    at, units = a_ref.shape[0], u_ref.shape[0]
    a_ref[...] = full[:at].astype(f32)
    for n in range(2):
        i_ref[n] = full[at + n * units : at + (n + 1) * units].astype(f32)
    u_ref[...] = full[at + 2 * units :].astype(f32)


def unstack(core, mine, got, width, units, deps=()):
    d = mine.shape[1]
    vmem = pl.BlockSpec(memory_space=pltpu.VMEM)
    return call(
        unstack_body,
        (core, mine, got,),
        deps,
        in_specs=[pl.BlockSpec(memory_space=pltpu.SMEM), vmem, vmem],
        out_shape=[
            jax.ShapeDtypeStruct((width, d), f32),
            jax.ShapeDtypeStruct((2, units, d), f32),
            jax.ShapeDtypeStruct((units, d), f32),
        ],
        compiler_params=params(20),
        cost_estimate=cost(1e8, 10e6),
        name="unstack",
    )


def unpair_body(core_ref, mine_ref, got_ref, out_ref):
    first = core_ref[0] == 0
    half = mine_ref.shape[0] // 3
    for pair in range(3):
        rows = slice(pair * half, (pair + 1) * half)
        mine, got = mine_ref[rows], got_ref[rows]
        full = jnp.concatenate([jnp.where(first, mine, got), jnp.where(first, got, mine)], axis=0)
        for n in range(3):
            turned = full[n * PAIR : (n + 1) * PAIR].T.astype(f32)
            out_ref[n, :, pair * PAIR : (pair + 1) * PAIR] = turned


def unpair(core, mine, got, deps=()):
    d = mine.shape[1]
    vmem = pl.BlockSpec(memory_space=pltpu.VMEM)
    return call(
        unpair_body,
        (core, mine, got,),
        deps,
        in_specs=[pl.BlockSpec(memory_space=pltpu.SMEM), vmem, vmem],
        out_shape=jax.ShapeDtypeStruct((3, d, 3 * PAIR), f32),
        compiler_params=params(14),
        cost_estimate=cost(1e8, 6e6),
        name="unpair",
    )


def combine_body(side_ref, k0, c0, k1, c1, own_ref, far_ref, mine_ref, other_ref):
    low = side_ref[0] == 0
    head = own_ref.shape[0]
    half = mine_ref.shape[1]
    for n, (keep, came, out) in enumerate(((k0, c0, own_ref), (k1, c1, far_ref))):
        total = (keep[...].astype(f32) + came[...].astype(f32)).astype(bf16)
        out[...] = total[:head]
        first, second = total[head : head + half], total[head + half :]
        mine_ref[n] = jnp.where(low, first, second)
        other_ref[n] = jnp.where(low, second, first)


def combine(side, keep0, came0, keep1, came1, head, deps=()):
    rows, d = keep0.shape
    half = (rows - head) // 2
    vmem = pl.BlockSpec(memory_space=pltpu.VMEM)
    cut = jax.ShapeDtypeStruct((2, half, d), bf16)
    return call(
        combine_body,
        (side, keep0, came0, keep1, came1),
        deps,
        in_specs=[pl.BlockSpec(memory_space=pltpu.SMEM)] + [vmem] * 4,
        out_shape=[jax.ShapeDtypeStruct((head, d), bf16)] * 2 + [cut] * 2,
        compiler_params=params(20),
        cost_estimate=cost(1e5, 1e4),
        name="combine",
    )


def second_body(side_ref, own_ref, got_a, mine_ref, got_b, keep_ref, pair_ref, far_ref, over_ref):
    low = side_ref[0] == 0
    total = (own_ref[...].astype(f32) + got_a[...].astype(f32)).astype(bf16)
    half = total.shape[0] // 2
    first, second = total[:half], total[half:]
    keep_ref[...] = jnp.where(low, first, second)
    over_ref[...] = jnp.where(low, second, first)
    pair = (mine_ref[...].astype(f32) + got_b[...].astype(f32)).astype(bf16)
    pair_ref[...] = pair[0]
    far_ref[...] = pair[1]


def second_step(side, own, got_a, mine, got_b, deps=()):
    rows, d = own.shape
    half = mine.shape[1]
    vmem = pl.BlockSpec(memory_space=pltpu.VMEM)
    return call(
        second_body,
        (side, own, got_a, mine, got_b),
        deps,
        in_specs=[pl.BlockSpec(memory_space=pltpu.SMEM)] + [vmem] * 4,
        out_shape=[
            jax.ShapeDtypeStruct((rows // 2, d), bf16),
            jax.ShapeDtypeStruct((half, d), bf16),
            jax.ShapeDtypeStruct((half, d), bf16),
            jax.ShapeDtypeStruct((rows // 2, d), bf16),
        ],
        compiler_params=params(14),
        cost_estimate=cost(1e5, 1e4),
        name="second_step",
    )


def cut_body(low_ref, *refs):
    *terms, keep_ref, over_ref = refs
    low = low_ref[0] == 0
    sums = [
        terms[n][...].astype(f32) + terms[n + 1][...].astype(f32) for n in range(0, len(terms), 2)
    ]
    short = 2 * keep_ref.shape[0] - sum(x.shape[0] for x in sums)
    if short:
        sums.append(jnp.zeros((short, sums[0].shape[1]), f32))
    total = jnp.concatenate(sums, axis=0)
    half = total.shape[0] // 2
    first, second = total[:half], total[half:]
    keep_ref[...] = jnp.where(low, first, second).astype(bf16)
    over_ref[...] = jnp.where(low, second, first).astype(bf16)


def cut_sums(low, terms, deps=()):
    rows = (sum(x.shape[0] for x in terms) // 2 + 31) // 32 * 32
    vmem = pl.BlockSpec(memory_space=pltpu.VMEM)
    return call(
        cut_body,
        (low, *terms),
        deps,
        in_specs=[pl.BlockSpec(memory_space=pltpu.SMEM)] + [vmem] * len(terms),
        out_shape=[jax.ShapeDtypeStruct((rows // 2, terms[0].shape[1]), bf16)] * 2,
        compiler_params=params(12),
        cost_estimate=cost(1e5, 1e4),
        name="cut_sums",
    )


def plus_body(a_ref, b_ref, out_ref):
    out_ref[...] = (a_ref[...].astype(f32) + b_ref[...].astype(f32)).astype(bf16)


def plus(a, b, deps=()):
    vmem = pl.BlockSpec(memory_space=pltpu.VMEM)
    return call(
        plus_body,
        (a, b),
        deps,
        in_specs=[vmem] * 2,
        out_shape=jax.ShapeDtypeStruct(a.shape, bf16),
        compiler_params=params(8),
        cost_estimate=cost(1e5, 1e4),
        name="plus",
    )


def pairs_body(side_ref, first_ref, keep, came, mine_ref, other_ref):
    low = side_ref[0] == 0
    first = first_ref[...]
    second = (keep[...].astype(f32) + came[...].astype(f32)).astype(bf16)
    mine_ref[...] = jnp.where(low, first, second)
    other_ref[...] = jnp.where(low, second, first)


def last_pair_body(side_ref, keep, came, mine_ref, other_ref):
    low = side_ref[0] == 0
    total = (keep[...].astype(f32) + came[...].astype(f32)).astype(bf16)
    half = total.shape[0] // 2
    mine_ref[...] = jnp.where(low, total[:half], total[half:])
    other_ref[...] = jnp.where(low, total[half:], total[:half])


def pairs_step(side, arrays, rows, deps=()):
    vmem = pl.BlockSpec(memory_space=pltpu.VMEM)
    shape = jax.ShapeDtypeStruct((rows, arrays[0].shape[1]), bf16)
    return call(
        pairs_body if len(arrays) == 3 else last_pair_body,
        (side, *arrays),
        deps,
        in_specs=[pl.BlockSpec(memory_space=pltpu.SMEM)] + [vmem] * len(arrays),
        out_shape=[shape] * 2,
        compiler_params=params(10),
        cost_estimate=cost(1e5, 1e4),
        name="pairs_step",
    )


def tail_body(
    b0, b1, b2, w_ref, h_ref, dn_ref, gg_ref
):
    dn = nn(jnp.concatenate([b0[...], b1[...], b2[...]], axis=1), w_ref[...])
    dn_ref[...] = dn.astype(dn_ref.dtype)
    xh, unused = unit_rows(h_ref[...].astype(f32))

    @pl.when(pl.program_id(0) == 0)
    def _():
        gg_ref[...] = jnp.zeros_like(gg_ref)

    gg_ref[...] += jnp.sum((dn * xh).reshape(-1, 8, dn.shape[1]), axis=0)


def tail(parts, w, h, first, dtype, deps=()):
    rows, d = h.shape
    off = first // BLK
    part = pl.BlockSpec((BLK, 3 * PAIR), lambda i: (i + off, 0))
    row = pl.BlockSpec((BLK, d), lambda i: (i, 0))
    return call(
        tail_body,
        (*parts, w, h,),
        deps,
        grid=(rows // BLK,),
        in_specs=[part] * 3 + [whole(w.shape), row],
        out_specs=[row, whole((8, d))],
        out_shape=[
            jax.ShapeDtypeStruct((rows, d), dtype),
            jax.ShapeDtypeStruct((8, d), f32),
        ],
        compiler_params=params(14),
        cost_estimate=cost(1e5, 1e4),
        name="tail",
    )


def last_body(h_ref, gain_ref, own_ref, got_ref, late_ref, dx_ref, out_ref):
    xh, inv = unit_rows(h_ref[...].astype(f32))
    got = jnp.where(pl.program_id(0) == 0, got_ref[...].astype(f32), late_ref[...].astype(f32))
    dn = own_ref[...] + got
    out_ref[...] = (dx_ref[...] + norm_back(dn * gain_ref[...], xh, inv)).astype(bf16)


def last(h, gain, own, got, late, dx, deps=()):
    rows, d = h.shape
    half = rows // 2
    row = pl.BlockSpec((half, d), lambda i: (i, 0))
    return call(
        last_body,
        (h, gain, own, got, late, dx),
        deps,
        grid=(2,),
        in_specs=[row, whole((1, d)), row, whole((half, d)), whole((half, d)), row],
        out_specs=row,
        out_shape=jax.ShapeDtypeStruct((rows, d), bf16),
        compiler_params=params(12),
        cost_estimate=cost(40 * rows * d, 9e6),
        name="last",
    )


def on_device(dp, hidden_in, bounds, attn_gain, w_qkv, w_attn, mlp_gain, w_in, w_out, cotangent):
    rows, d = hidden_in.shape
    cap = 2 * rows
    width = w_attn.shape[0]
    units = w_out.shape[0]
    shard = lax.axis_index("tensor")
    place = lax.axis_index("dp")
    core = place % 2
    core_at = core.astype(jnp.int32).reshape(1)
    side = (place // 2) % 2
    groups = [list(range(c, dp, 2)) for c in range(2)]
    bits = [1 << n for n in range(dp.bit_length() - 1)]

    def over_y(x):
        return lax.ppermute(x, "tensor", [(0, 1), (1, 0)])

    def over(x, bit):
        return lax.ppermute(x, "dp", [(n, n ^ bit) for n in range(dp)])

    def over_core(x):
        return over(x, 1)

    def add(a, b):
        return (a.astype(f32) + b.astype(f32)).astype(bf16)

    def in_order(first, mine, got):
        return jnp.concatenate(
            [jnp.where(first, mine, got), jnp.where(first, got, mine)], axis=0
        )

    hidden_got = over_y(hidden_in)
    cosine, sine, feat_q, feat_k = tables(
        bounds, (shard * rows).astype(jnp.int32).reshape(1), cap
    )
    gain_a = attn_gain.reshape(1, d)
    gain_m = mlp_gain.reshape(1, d)
    held = qkv(hidden_in, gain_a, w_qkv, cosine, sine, 0, ())
    w_own, w_qkv_turned = stack(w_attn, jnp.swapaxes(w_in, 1, 2), w_out, w_qkv)
    quarter = w_own.shape[0] // 4
    piece = lax.dynamic_slice_in_dim(w_own, (2 * core + side) * quarter, quarter, 0)
    hidden_got, piece, held = lax.optimization_barrier((hidden_got, piece, held))
    n1, q, k, v = qkv(hidden_got, gain_a, w_qkv, cosine, sine, rows, held)

    def after(x, *done):
        return lax.optimization_barrier((x, done))[0]

    cut = (quarter // 2 + 15) // 16 * 16
    cuts = (piece[:cut], piece[cut:])
    from_y = [over_y(x) for x in cuts]
    first = attend(0, q, k, v, feat_q, feat_k, ())
    from_x = [over(after(from_y[0], first[0]), 2)]
    second = attend(1, q, k, v, feat_q, feat_k, first[:2])
    from_x.append(over(after(from_y[1], second[0]), 2))
    third = attend(2, q, k, v, feat_q, feat_k, second[:1])
    o_got = [over_y(second[1]), over_y(third[1])]
    pieces = [from_y[0], from_x[0], over_core(from_y[0]), over_core(after(from_x[0], second[0]))]
    pieces += [from_y[1], from_x[1], over_core(from_y[1]), over_core(after(from_x[1], third[0]))]
    at = jnp.arange(2, dtype=jnp.int32)[:, None] * cut + jnp.stack(
        [(2 * c + s) * quarter for c in (core, 1 - core) for s in (side, 1 - side)]
    )
    o_own = third[0]
    o_far = (second[1], second[1], third[1])
    q_tag = [x[2:] for x in (first, second, third)]
    w_got = assemble(at.reshape(8), pieces, w_own.shape, (o_got[0],))
    scalars = jnp.stack([shard * rows, bounds[0, NSEG - 1]]).astype(jnp.int32)
    (
        hidden_out, n2, ga, dx, gm, by_unit, d_own, db01, db2, gg_mlp,
    ) = mlp(scalars, hidden_in, cotangent, o_own, o_got, gain_m, w_own, w_got, units)
    d_got = [over_y(db01), over_y(db2)]
    d_far = (d_got[0], d_got[0], d_got[1])

    def back(pair, start, stop, begun, *deps):
        return attend_back(
            pair, start, stop, begun, *q_tag[pair], q, k, v, feat_k, o_own, o_far[pair],
            d_own, d_far[pair], cosine, sine, deps,
        )

    def split(x, bit):
        low = (place & bit) == 0
        half = x.shape[0] // 2
        first, second = x[:half], x[half:]
        return jnp.where(low, first, second), jnp.where(low, second, first)

    def merge(x, bit):
        return in_order((place & bit) == 0, x, over(x, bit))

    def over_rest(x):
        if len(bits) < 3:
            return x
        mine, other = split(x, bits[2])
        mine = add(mine, over(other, bits[2]))
        for bit in bits[3:]:
            mine = add(mine, over(mine, bit))
        return merge(mine, bits[2])

    keep1, send1 = weight_grads(1, core_at, o_got, by_unit, n2, ga, gm)
    keep0, send0 = weight_grads(0, core_at, (o_own,), by_unit, n2, ga, gm, (keep1,))
    came1 = over_core(send1)
    came0 = over_core(after(send0, d_got[0]))
    head = send0.shape[0] // 32 * 16 - 16
    own_a, far_a, mine_b, other_b = combine(
        side.astype(jnp.int32).reshape(1), keep0, came0, keep1, came1, head
    )
    got_a, got_b = over_y(far_a), over(other_b, 2)
    blocks = cap // KBLK
    back0 = back(0, 0, blocks, (), mine_b, far_a)[0]
    keep, send = pair_grads(core_at, back0, n1)

    side_at = side.astype(jnp.int32).reshape(1)
    mine, mine_b, far_b, other_a = second_step(side_at, own_a, got_a, mine_b, got_b, (back0,))
    got_a, got_b = over(other_a, 2), over_y(far_b)
    begun = back(1, 0, 1, (), keep, mine)
    pair0 = plus(keep, over_core(send))

    if len(bits) > 2:
        low = ((place // 4) % 2).astype(jnp.int32).reshape(1)
        mine, other = cut_sums(low, (mine, got_a, mine_b, got_b), (begun[0],))
        got = over(other, bits[2])
    else:
        mine = jnp.concatenate([add(mine, got_a), add(mine_b, got_b)], axis=0)
    back1 = back(1, 1, blocks, begun, mine, pair0)[0]
    keep, send = pair_grads(core_at, back1, n1)

    if len(bits) > 2:
        mine = plus(mine, got, (back1,))
    if len(bits) > 3:
        got = over(mine, bits[3])
    came = over_core(send)
    q_mine, q_other = pairs_step(side_at, (pair0, keep, came), pair0.shape[0])
    q_got = over(q_other, 2)
    back2 = back(2, 0, blocks, (), mine, q_other)[0]
    if len(bits) > 3:
        mine = plus(mine, got, (back2,))
    parts = (back0, back1, back2)
    keep, send = pair_grads(core_at, back2, n1, (mine, q_got))
    dn_other, gg_other = tail(parts, w_qkv_turned, hidden_got, rows, bf16, (keep,))
    cut_at = rows // 2
    dn_got = over_y(dn_other[:cut_at])
    came = over_core(send)
    if len(bits) > 2:
        for bit in bits[4:]:
            mine = add(mine, over(mine, bit))
        mine = merge(mine, bits[2])
    last_mine, last_other = pairs_step(
        side_at, (keep, came), pair0.shape[0] // 2, (dn_other,)
    )
    dn_own, gg_own = tail(parts, w_qkv_turned, hidden_in, 0, f32, (last_other,))
    gains = gain_rows(gg_own, gg_other, gg_mlp)
    gains = gains + over_core(gains)
    last_got = over(last_other, 2)
    weights = mine
    if len(bits) > 2:
        mine, other = cut_sums(
            low, (q_mine, q_got, last_mine, last_got, gains, over(gains, 2)), (dn_got,)
        )
        lent = over(other, bits[2])
        got = over(after(weights, mine), 2)
        low_side = (place & 2) == 0
        grads = jnp.concatenate(
            [in_order(low_side, weights[: head // 2], got[: head // 2]),
             in_order(low_side, weights[head // 2 : quarter], got[head // 2 : quarter])],
            axis=0,
        )
        mine = plus(mine, lent)
        dn_late = over_y(after(dn_other[cut_at:], mine))
        for bit in bits[3:-1]:
            mine = plus(mine, over(mine, bit))
        if len(bits) > 3:
            mine = plus(mine, over(mine, bits[-1]), (got,))
        mine = merge(mine, bits[2])
    else:
        mine = jnp.concatenate(
            [add(q_mine, q_got), add(last_mine, last_got), add(gains, over(gains, 2))], axis=0
        )
        dn_late = over_y(dn_other[cut_at:])
        got = over(after(weights, mine), 2)
        low_side = (place & 2) == 0
        grads = jnp.concatenate(
            [in_order(low_side, weights[: head // 2], got[: head // 2]),
             in_order(low_side, weights[head // 2 : quarter], got[head // 2 : quarter])],
            axis=0,
        )
    low_side = (place & 2) == 0
    grad_in = last(hidden_in, gain_a, dn_own, dn_got, dn_late, dx)
    first, count = pair0.shape[0], 3 * pair0.shape[0] // 2
    gains = mine[count : count + 2].astype(f32)
    gains = gains + over_y(gains)
    got = over(after(mine[:count], grad_in), 2)
    pairs = jnp.concatenate(
        [in_order(low_side, mine[:first], got[:first]),
         in_order(low_side, mine[first:count], got[first:])],
        axis=0,
    )

    grad_w_attn, grad_w_in, grad_w_out = unstack(core_at, grads, over_core(grads), width, units)
    grad_w_in = jnp.swapaxes(grad_w_in, 1, 2)
    grad_w_qkv = unpair(core_at, pairs, over_core(after(pairs, grad_w_attn)))
    return (
        hidden_out,
        grad_in,
        gains[0],
        grad_w_qkv,
        grad_w_attn,
        gains[1],
        grad_w_in,
        grad_w_out,
    )


def solution(mesh):
    in_specs = (
        P(("dp", "tensor"), None),
        P("dp", None),
        P(),
        P(None, None, "tensor"),
        P("tensor", None),
        P(),
        P(None, None, "tensor"),
        P("tensor", None),
        P(("dp", "tensor"), None),
    )
    out_specs = (
        P(("dp", "tensor"), None),
        P(("dp", "tensor"), None),
        P(),
        P(None, None, "tensor"),
        P("tensor", None),
        P(),
        P(None, None, "tensor"),
        P("tensor", None),
    )
    return jax.shard_map(
        functools.partial(on_device, mesh.shape["dp"]),
        mesh=mesh,
        in_specs=in_specs,
        out_specs=out_specs,
        check_vma=False,
    )
```

```python
import functools

import jax
import jax.numpy as jnp
import numpy as np
from jax import lax
from jax.experimental import pallas as pl
from jax.experimental.pallas import tpu as pltpu
from jax.sharding import PartitionSpec as P

HD = 64
NSEG = 6
PAIR = 2 * HD
BLK = 384
MLP_BLK = 256
COST = 0.15
KBLK = 512
rope_theta = 160000.0
norm_eps = 1e-05
masked_score = -1e30
f32 = jnp.float32
bf16 = jnp.bfloat16


def params(mib):
    return pltpu.CompilerParams(vmem_limit_bytes=mib * 1024 * 1024)


def cost(flops, nbytes):
    return pl.CostEstimate(
        flops=int(flops * COST), bytes_accessed=int(nbytes * COST), transcendentals=0
    )


def nn(a, b):
    return jnp.dot(a, b, preferred_element_type=f32)


def nt(a, b):
    return lax.dot_general(a, b, (((1,), (1,)), ((), ())), preferred_element_type=f32)


def call(body, args, deps=(), *, in_specs, **kw):
    first = len(in_specs)

    def run(*refs):
        body(*refs[:first], *refs[first + len(deps) :])

    return pl.pallas_call(
        run, in_specs=list(in_specs) + [pl.BlockSpec(memory_space=pl.ANY)] * len(deps), **kw
    )(*args, *deps)


def whole(shape):
    return pl.BlockSpec(shape, lambda i: (0,) * len(shape))


def unit_rows(x):
    centred = x - jnp.mean(x, axis=-1, keepdims=True)
    inv = lax.rsqrt(jnp.mean(centred * centred, axis=-1, keepdims=True) + norm_eps)
    return centred * inv, inv


def norm_back(e, xh, inv):
    return inv * (
        e - jnp.mean(e, axis=-1, keepdims=True) - xh * jnp.mean(e * xh, axis=-1, keepdims=True)
    )


def turn(x, cosine, sine, back):
    lane = lax.broadcasted_iota(jnp.int32, x.shape, 1) % HD
    other = jnp.where(lane < HD // 2, pltpu.roll(x, PAIR - HD // 2, 1), pltpu.roll(x, HD // 2, 1))
    return x * cosine - other * sine if back else x * cosine + other * sine


def sincos(x):
    turns = jnp.floor(x * 0.6366197723675814 + 0.5)
    r = ((x - turns * 1.5703125) - turns * 4.837512969970703125e-4) - turns * 7.54978995489188e-8
    z = r * r
    s = r + r * z * (-1.6666654611e-1 + z * (8.3321608736e-3 + z * -1.9515295891e-4))
    c = 1.0 - 0.5 * z + z * z * (
        4.166664568298827e-2 + z * (-1.388731625493765e-3 + z * 2.443315711809948e-5)
    )
    quarter = turns.astype(jnp.int32) & 3
    odd = (quarter & 1) == 1
    sine = jnp.where(odd, c, s)
    cosine = jnp.where(odd, s, c)
    sine = jnp.where(quarter >= 2, -sine, sine)
    cosine = jnp.where(jnp.logical_or(quarter == 1, quarter == 2), -cosine, cosine)
    return sine, cosine


def tables_body(edge_ref, first_ref, freq_ref, cos_ref, sin_ref, fq_ref, fk_ref):
    cap = cos_ref.shape[0]
    ids = lax.broadcasted_iota(jnp.int32, (cap, PAIR), 0) + first_ref[0]
    ids = jnp.where(ids >= cap, ids - cap, ids)
    lane = lax.broadcasted_iota(jnp.int32, ids.shape, 1)
    seg = jnp.zeros(ids.shape, jnp.int32)
    begin = jnp.zeros(ids.shape, jnp.int32)
    for n in range(1, NSEG):
        passed = ids >= edge_ref[0, n]
        seg = jnp.where(passed, seg + 1, seg)
        begin = jnp.where(passed, edge_ref[0, n], begin)
    angle = (ids - begin).astype(f32) * freq_ref[...]
    sine, cosine = sincos(angle)
    slot = lane % HD
    cos_ref[...] = cosine
    sin_ref[...] = jnp.where(slot < HD // 2, -sine, sine)
    same = slot == seg
    fq_ref[...] = jnp.where(same, 1.0, 0.0).astype(bf16)
    fk_ref[...] = jnp.where(
        slot < NSEG,
        jnp.where(same, 0.0, masked_score),
        jnp.where(slot < NSEG + 3, 1.0, 0.0),
    ).astype(bf16)


def tables(edges, first, cap):
    steps = 2.0 * (np.arange(PAIR) % (HD // 2)) / HD
    freq = jnp.asarray(np.exp(-steps * np.log(rope_theta))[None].astype(np.float32))
    smem = pl.BlockSpec(memory_space=pltpu.SMEM)
    table = lambda t: jax.ShapeDtypeStruct((cap, PAIR), t)
    return pl.pallas_call(
        tables_body,
        in_specs=[smem, smem, pl.BlockSpec(memory_space=pltpu.VMEM)],
        out_shape=[table(f32), table(f32), table(bf16), table(bf16)],
        compiler_params=params(8),
        cost_estimate=cost(80 * cap * PAIR, 3e6),
        name="tables",
    )(edges, first, freq)


def stack_body(a_ref, i_ref, u_ref, w_ref, out_ref, qkv_ref):
    at = a_ref.shape[0]
    units = u_ref.shape[0]
    width = w_ref.shape[2]
    out_ref[:at] = a_ref[...]
    for n in range(2):
        out_ref[at + n * units : at + (n + 1) * units] = i_ref[n]
    out_ref[at + 2 * units :] = u_ref[...]
    for n in range(3):
        turned = w_ref[n].T
        for pair in range(width // PAIR):
            to = (3 * pair + n) * PAIR
            qkv_ref[to : to + PAIR] = turned[pair * PAIR : (pair + 1) * PAIR]


def stack(w_attn, w_in_turned, w_out, w_qkv, deps=()):
    at, d = w_attn.shape
    rows = at + 3 * w_out.shape[0]
    vmem = pl.BlockSpec(memory_space=pltpu.VMEM)
    return call(
        stack_body,
        (w_attn, w_in_turned, w_out, w_qkv),
        deps,
        in_specs=[vmem] * 4,
        out_shape=[
            jax.ShapeDtypeStruct((rows, d), bf16),
            jax.ShapeDtypeStruct((3 * w_qkv.shape[2], d), bf16),
        ],
        compiler_params=params(12),
        cost_estimate=cost(1e8, 10e6),
        name="stack",
    )


def qkv_body(h_ref, gain_ref, w_ref, cos_ref, sin_ref, *refs):
    n1_ref, q_ref, k_ref, v_ref = refs[-4:]
    unit, inv = unit_rows(h_ref[...].astype(f32))
    n1 = (unit * gain_ref[...]).astype(bf16)
    n1_ref[...] = n1
    cosine, sine = cos_ref[...], sin_ref[...]
    width = w_ref.shape[2]
    for which, out, scale in ((0, q_ref, 0.125), (1, k_ref, 1.0)):
        full = nn(n1, w_ref[which])
        for at in range(0, width, PAIR):
            turned = turn(full[:, at : at + PAIR], cosine, sine, False).astype(bf16)
            if scale != 1.0:
                turned = (turned.astype(f32) * scale).astype(bf16)
            out[:, at : at + PAIR] = turned
    v_ref[...] = nn(n1, w_ref[2]).astype(bf16)


def qkv(h, gain, w, cosine, sine, first, held, deps=()):
    rows, d = h.shape
    cap, width = cosine.shape[0], w.shape[2]
    off = first // BLK
    by_row = lambda n: pl.BlockSpec((BLK, n), lambda i: (i + off, 0))
    shapes = [jax.ShapeDtypeStruct((cap, n), bf16) for n in (d, width, width, width)]
    return call(
        qkv_body,
        (h, gain, w, cosine, sine, *held),
        deps,
        grid=(rows // BLK,),
        in_specs=[
            pl.BlockSpec((BLK, d), lambda i: (i, 0)),
            whole((1, d)),
            whole(w.shape),
            by_row(PAIR),
            by_row(PAIR),
        ]
        + [pl.BlockSpec(memory_space=pl.ANY)] * len(held),
        out_specs=[by_row(d), by_row(width), by_row(width), by_row(width)],
        out_shape=shapes,
        input_output_aliases={5 + n: n for n in range(len(held))},
        compiler_params=params(14),
        cost_estimate=cost(2 * 2 * rows * d * 3 * width, 12e6),
        name="qkv",
    )


def assemble_body(at_ref, *refs):
    pieces, out_ref, sems = refs[:-2], refs[-2], refs[-1]
    copies = []
    for n, ref in enumerate(pieces):
        to = pl.ds(pl.multiple_of(at_ref[n], 8), ref.shape[0])
        copies.append(pltpu.make_async_copy(ref, out_ref.at[to], sems.at[n]))
        copies[-1].start()
    for copy in copies:
        copy.wait()


def assemble(at, pieces, shape, deps=()):
    anywhere = pl.BlockSpec(memory_space=pl.ANY)
    return call(
        assemble_body,
        (at, *pieces),
        deps,
        in_specs=[pl.BlockSpec(memory_space=pltpu.SMEM)] + [anywhere] * len(pieces),
        out_specs=pl.BlockSpec(memory_space=pltpu.VMEM),
        out_shape=jax.ShapeDtypeStruct(shape, bf16),
        scratch_shapes=[pltpu.SemaphoreType.DMA((len(pieces),))],
        compiler_params=params(8),
        cost_estimate=cost(1e6, 6e6),
        name="assemble",
    )


def lanes_of(head, shape):
    lane = lax.broadcasted_iota(jnp.int32, shape, 1)
    return (lane < HD) if head == 0 else (lane >= HD)


def attend_body(q_ref, k_ref, v_ref, fq_ref, fk_ref, *refs):
    o0_ref, o1_ref, qa_ref, qb_ref = refs[-4:]
    q, k, v, fq, fk = q_ref[...], k_ref[...], v_ref[...], fq_ref[...], fk_ref[...]
    v_turned = v.T
    rows = q.shape[0]
    line = lax.broadcasted_iota(jnp.int32, (PAIR, rows), 0)
    tag = jnp.zeros((PAIR, rows), f32)
    mixed = []
    scores = [
        nt(jnp.where(lanes_of(n, k.shape), k, fk), jnp.where(lanes_of(n, q.shape), q, fq))
        for n in (0, 1)
    ]
    for head, score in enumerate(scores):
        top = jnp.max(score, axis=0, keepdims=True)
        expo = jnp.exp(score - top)
        total = jnp.sum(expo, axis=0, keepdims=True)
        at = head * HD
        mixed.append(nn(v_turned[at : at + HD], expo.astype(bf16)) * (1.0 / total))
        left = -(top + jnp.log(total))
        for part in range(3):
            head_bits = left.astype(bf16).astype(f32)
            left = left - head_bits
            tag = jnp.where(line == HD - at + NSEG + part, head_bits, tag)
    o = jnp.concatenate(mixed, axis=0).T.astype(bf16)
    tag = tag.T
    fq = fq.astype(f32) + tag
    wide = q.astype(f32)
    qa_ref[...] = jnp.where(lanes_of(0, q.shape), wide, fq).astype(bf16)
    qb_ref[...] = jnp.where(lanes_of(1, q.shape), wide, fq).astype(bf16)

    @pl.when(pl.program_id(0) == 0)
    def _():
        o0_ref[...] = o

    @pl.when(pl.program_id(0) == 1)
    def _():
        o1_ref[...] = o


def attend(pair, q, k, v, feat_q, feat_k, held):
    cap, width = q.shape
    rows = cap // 2
    part = pl.BlockSpec((rows, PAIR), lambda i: (i, 0))
    full = pl.BlockSpec((cap, PAIR), lambda i: (0, pair))
    column = lambda n: pl.BlockSpec((rows, PAIR), lambda i: (0, n))
    far = width - PAIR if pair < 2 else PAIR
    return pl.pallas_call(
        attend_body,
        grid=(2,),
        in_specs=[
            pl.BlockSpec((rows, PAIR), lambda i: (i, pair)),
            full,
            full,
            part,
            whole((cap, PAIR)),
        ]
        + [pl.BlockSpec(memory_space=pl.ANY)] * len(held),
        out_specs=[column(pair), column(pair % 2)] + [part] * 2,
        out_shape=[
            jax.ShapeDtypeStruct((rows, width), bf16),
            jax.ShapeDtypeStruct((rows, far), bf16),
        ]
        + [jax.ShapeDtypeStruct((cap, PAIR), bf16)] * 2,
        input_output_aliases={5 + n: n for n in range(len(held))},
        compiler_params=params(12),
        cost_estimate=cost(2 * 2 * 2 * cap * cap * 256 * 2, 3e6),
        name="attend",
    )(q, k, v, feat_q, feat_k, *held)


def back_body(
    start, begun, ends, qa_ref, qb_ref, q_ref, k_ref, v_ref, fk_ref, o0_ref, o1_ref, d0_ref, d1_ref, cos_ref, sin_ref,
    *refs,
):
    dqt_in, low_in = refs[:2] if begun else (None, None)
    outs = refs[2:-4] if begun else refs[:-4]
    dol_ref, da_ref, db_ref, dqt_ref = refs[-4:]
    out_ref = outs[0]
    step = pl.program_id(0)
    half = d0_ref.shape[0]
    cap = 2 * half

    @pl.when(step == 0)
    def _():
        dol_ref[:half] = d0_ref[...]
        dol_ref[half:] = d1_ref[...]
        dol = dol_ref[...]
        slot = lax.broadcasted_iota(jnp.int32, dol.shape, 1) % HD
        wide = dol.astype(f32)
        prod = wide * jnp.concatenate([o0_ref[...], o1_ref[...]], axis=0).astype(f32)
        for head, out in ((0, da_ref), (1, db_ref)):
            mine = lanes_of(head, dol.shape)
            left = -jnp.sum(jnp.where(mine, prod, 0.0), axis=-1, keepdims=True)
            tagged = jnp.where(mine, wide, 0.0)
            for part in range(3):
                head_bits = left.astype(bf16).astype(f32)
                left = left - head_bits
                tagged = jnp.where(
                    jnp.logical_and(jnp.logical_not(mine), slot == NSEG + part), head_bits, tagged
                )
            out[...] = tagged.astype(bf16)
        if begun:
            dqt_ref[...] = dqt_in[...]
            out_ref[: start * KBLK, PAIR:] = low_in[...]
        else:
            dqt_ref[...] = jnp.zeros_like(dqt_ref)

    k, v, fk, q, dol = k_ref[...], v_ref[...], fk_ref[...], q_ref[...], dol_ref[...]
    k_turned = k.T
    slot = lax.broadcasted_iota(jnp.int32, v.shape, 1) % HD
    ones = jnp.where(
        jnp.logical_and(slot >= NSEG, slot < NSEG + 3), 1.0, 0.0
    ).astype(bf16)
    heads = ((0, qa_ref, da_ref), (1, qb_ref, db_ref))
    scores = [nt(jnp.where(lanes_of(h, k.shape), k, fk), a[...]) for h, a, b in heads]
    grads = [nt(jnp.where(lanes_of(h, v.shape), v, ones), b[...]) for h, a, b in heads]
    probs = [jnp.exp(s) for s in scores]
    dvs = [nn(p.astype(bf16), dol) for p in probs]
    dss = [(p * g).astype(bf16) for p, g in zip(probs, grads)]
    dks = [nn(s, q) for s in dss]
    for h in (0, 1):
        dqt_ref[h * HD : h * HD + HD] += nn(k_turned[h * HD : h * HD + HD], dss[h])
    first = lanes_of(0, k.shape)
    rows = pl.ds(pl.multiple_of((step + start) * KBLK, KBLK), KBLK)
    dk = turn(jnp.where(first, dks[0], dks[1]), cos_ref[rows], sin_ref[rows], True).astype(bf16)
    dv = jnp.where(first, dvs[0], dvs[1]).astype(bf16)
    if ends:
        out_ref[rows, PAIR : 2 * PAIR] = dk
        out_ref[rows, 2 * PAIR :] = dv
    else:
        outs[1][:, :PAIR] = dk
        outs[1][:, PAIR:] = dv

    @pl.when(step == pl.num_programs(0) - 1)
    def _():
        if ends:
            dq = dqt_ref[...].T * 0.125
            out_ref[:, :PAIR] = turn(dq, cos_ref[...], sin_ref[...], True).astype(bf16)
        else:
            out_ref[...] = dqt_ref[...]


def attend_back(
    pair, start, stop, begun, qa, qb, q, k, v, feat_k, o0, o1, d0, d1, cosine, sine, deps=()
):
    cap = q.shape[0]
    ends = stop * KBLK == cap
    full = whole((cap, PAIR))
    block = pl.BlockSpec((KBLK, PAIR), lambda i: (i + start, pair))
    part = pl.BlockSpec((KBLK, PAIR), lambda i: (i + start, 0))
    column = lambda n: pl.BlockSpec((cap // 2, PAIR), lambda i: (0, n))
    if ends:
        out_specs = [whole((cap, 3 * PAIR))]
        out_shape = [jax.ShapeDtypeStruct((cap, 3 * PAIR), bf16)]
    else:
        out_specs = [whole((PAIR, cap)), pl.BlockSpec((KBLK, 2 * PAIR), lambda i: (i, 0))]
        out_shape = [
            jax.ShapeDtypeStruct((PAIR, cap), f32),
            jax.ShapeDtypeStruct(((stop - start) * KBLK, 2 * PAIR), bf16),
        ]
    return call(
        functools.partial(back_body, start, bool(begun), ends),
        (qa, qb, q, k, v, feat_k, o0, o1, d0, d1, cosine, sine, *begun),
        deps,
        grid=(stop - start,),
        in_specs=[
            full,
            full,
            pl.BlockSpec((cap, PAIR), lambda i: (0, pair)),
            block,
            block,
            part,
            column(pair),
            column(pair % 2),
            column(pair),
            column(pair % 2),
            full,
            full,
        ]
        + [whole(x.shape) for x in begun],
        out_specs=out_specs,
        out_shape=out_shape,
        scratch_shapes=[
            pltpu.VMEM((cap, PAIR), bf16),
            pltpu.VMEM((cap, PAIR), bf16),
            pltpu.VMEM((cap, PAIR), bf16),
            pltpu.VMEM((PAIR, cap), f32),
        ],
        compiler_params=params(58),
        cost_estimate=cost(5 * 2 * 2 * (stop - start) * KBLK * cap * 256 * 2, 6e6),
        name="attend_back",
    )


def mlp_body(
    sc_ref, h_ref, cot_ref, oa_ref, ob01, ob2, gain_ref, own_ref, got_ref,
    out_ref, n2_ref, ga_ref, dx_ref, gm_ref, unit_ref, da_ref, db01, db2, gg_ref,
):
    step = pl.program_id(0)
    oa = oa_ref[...]
    ob = jnp.concatenate([ob01[...], ob2[...]], axis=1)
    width = oa.shape[1]
    units = unit_ref.shape[2]
    in0 = slice(width, width + units)
    in1 = slice(width + units, width + 2 * units)
    up = slice(width + 2 * units, width + 3 * units)
    x1 = h_ref[...].astype(f32) + (nn(oa, own_ref[:width]) + nn(ob, got_ref[:width]))
    xh, inv = unit_rows(x1)
    gain = gain_ref[...]
    n2 = (xh * gain).astype(bf16)
    n2_ref[...] = n2
    ids = sc_ref[0] + step * MLP_BLK + lax.broadcasted_iota(jnp.int32, x1.shape, 0)
    g = jnp.where(ids < sc_ref[1], cot_ref[...].astype(f32), 0.0)
    gm = g.astype(bf16)
    gm_ref[...] = gm
    m = jnp.zeros_like(x1)
    dn2 = jnp.zeros_like(x1)
    for n, w_ref in enumerate((own_ref, got_ref)):
        act = nt(n2, w_ref[in0])
        gate = nt(n2, w_ref[in1])
        phi = 0.5 * (1.0 + lax.erf(act * 0.7071067811865476))
        bell = jnp.exp(-0.5 * act * act) * 0.3989422804014327
        gelu = act * phi
        hidden = (gelu * gate).astype(bf16)
        unit_ref[3 * n + 2] = hidden
        m = m + nn(hidden, w_ref[up])
        dh = nt(gm, w_ref[up])
        dact = (dh * gate * (phi + act * bell)).astype(bf16)
        dgate = (dh * gelu).astype(bf16)
        unit_ref[3 * n] = dact
        unit_ref[3 * n + 1] = dgate
        dn2 = dn2 + nn(dact, w_ref[in0]) + nn(dgate, w_ref[in1])
    out_ref[...] = (x1 + m).astype(bf16)

    @pl.when(step == 0)
    def _():
        gg_ref[...] = jnp.zeros_like(gg_ref)

    gg_ref[...] += jnp.sum((dn2 * xh).reshape(-1, 8, x1.shape[1]), axis=0)
    dx = g + norm_back(dn2 * gain, xh, inv)
    dx_ref[...] = dx
    ga = dx.astype(bf16)
    ga_ref[...] = ga
    da_ref[...] = nt(ga, own_ref[:width]).astype(bf16)
    db = nt(ga, got_ref[:width]).astype(bf16)
    db01[...] = db[:, : 2 * PAIR]
    db2[...] = db[:, 2 * PAIR :]


def mlp(scalars, h, cot, o_own, o_got, gain, w_own, w_got, units, deps=()):
    rows, d = h.shape
    row = lambda n: pl.BlockSpec((MLP_BLK, n), lambda i: (i, 0))
    out = lambda n, t=bf16: jax.ShapeDtypeStruct((rows, n), t)
    return call(
        mlp_body,
        (scalars, h, cot, o_own, *o_got, gain, w_own, w_got),
        deps,
        grid=(rows // MLP_BLK,),
        in_specs=[pl.BlockSpec(memory_space=pltpu.SMEM), row(d), row(d)]
        + [row(3 * PAIR), row(2 * PAIR), row(PAIR)]
        + [whole((1, d))]
        + [whole(w_own.shape)] * 2,
        out_specs=[row(d)] * 5
        + [pl.BlockSpec((6, MLP_BLK, units), lambda i: (0, i, 0))]
        + [row(3 * PAIR), row(2 * PAIR), row(PAIR)]
        + [whole((8, d))],
        out_shape=[out(d), out(d), out(d), out(d, f32), out(d)]
        + [jax.ShapeDtypeStruct((6, rows, units), bf16)]
        + [out(3 * PAIR), out(2 * PAIR), out(PAIR)]
        + [jax.ShapeDtypeStruct((8, d), f32)],
        compiler_params=params(26),
        cost_estimate=cost(2 * 2 * 4 * rows * w_own.size, 24e6),
        name="mlp",
    )


def tn(a, b):
    return lax.dot_general(a, b, (((0,), (0,)), ((), ())), preferred_element_type=f32)


def grads_body(
    side, many, core_ref, *refs
):
    outs, unit_ref = refs[:many], refs[many]
    n2_ref, ga_ref, gm_ref, keep_ref, send_ref, held_ref, sems = refs[many + 1 :]
    core = core_ref[0]
    half = keep_ref.shape[0]
    n2, ga, gm = n2_ref[...], ga_ref[...], gm_ref[...]
    parts = [(x[...], ga) for x in outs]
    parts += [(unit_ref[n], n2 if n < 2 else gm) for n in range(3)]
    at = 0
    for left, right in parts:
        res = tn(left, right).astype(bf16)
        held_ref[at : at + res.shape[0]] = res
        at += res.shape[0]
    copies = []
    for out, which in ((keep_ref, core), (send_ref, 1 - core)):
        rows = pl.ds(pl.multiple_of(which * half, 16), half)
        copies.append(pltpu.make_async_copy(held_ref.at[rows], out, sems.at[len(copies)]))
        copies[-1].start()
    for copy in copies:
        copy.wait()


def weight_grads(side, core, o, by_unit, n2, ga, gm, deps=()):
    rows, d = n2.shape
    units = by_unit.shape[2]
    total = 3 * PAIR + 3 * units
    shape = jax.ShapeDtypeStruct((total // 2, d), bf16)
    vmem = pl.BlockSpec(memory_space=pltpu.VMEM)
    anywhere = pl.BlockSpec(memory_space=pl.ANY)
    return call(
        functools.partial(grads_body, side, len(o)),
        (core, *o, by_unit, n2, ga, gm),
        deps,
        grid=(1,),
        in_specs=[pl.BlockSpec(memory_space=pltpu.SMEM)]
        + [whole(x.shape) for x in o]
        + [pl.BlockSpec((3, rows, units), lambda i: (side, 0, 0))]
        + [whole((rows, d))] * 3,
        out_specs=[anywhere] * 2,
        out_shape=[shape] * 2,
        scratch_shapes=[pltpu.VMEM((total, d), bf16), pltpu.SemaphoreType.DMA((2,))],
        compiler_params=params(18),
        cost_estimate=cost(1e5, 1e4),
        name="weight_grads",
    )


def pair_body(core_ref, back_ref, n1_ref, keep_ref, send_ref, held_ref, sems):
    half = keep_ref.shape[0]
    held_ref[...] = tn(back_ref[...], n1_ref[...]).astype(bf16)
    copies = []
    for out, which in ((keep_ref, core_ref[0]), (send_ref, 1 - core_ref[0])):
        rows = pl.ds(pl.multiple_of(which * half, 16), half)
        copies.append(pltpu.make_async_copy(held_ref.at[rows], out, sems.at[len(copies)]))
        copies[-1].start()
    for copy in copies:
        copy.wait()


def pair_grads(core, back, n1, deps=()):
    cap, d = n1.shape
    rows = back.shape[1]
    shape = jax.ShapeDtypeStruct((rows // 2, d), bf16)
    vmem = pl.BlockSpec(memory_space=pltpu.VMEM)
    anywhere = pl.BlockSpec(memory_space=pl.ANY)
    return call(
        pair_body,
        (core, back, n1),
        deps,
        in_specs=[pl.BlockSpec(memory_space=pltpu.SMEM)] + [vmem] * 2,
        out_specs=[anywhere] * 2,
        out_shape=[shape] * 2,
        scratch_shapes=[pltpu.VMEM((rows, d), bf16), pltpu.SemaphoreType.DMA((2,))],
        compiler_params=params(10),
        cost_estimate=cost(1e5, 1e4),
        name="pair_grads",
    )


def gains_body(own_ref, other_ref, mlp_ref, out_ref):
    a = jnp.sum(own_ref[...] + other_ref[...], axis=0, keepdims=True)
    m = jnp.sum(mlp_ref[...], axis=0, keepdims=True)
    line = lax.broadcasted_iota(jnp.int32, out_ref.shape, 0)
    out_ref[...] = jnp.where(line == 0, a, jnp.where(line == 1, m, 0.0))


def gain_rows(own, other, mlp_part):
    vmem = pl.BlockSpec(memory_space=pltpu.VMEM)
    return call(
        gains_body,
        (own, other, mlp_part),
        in_specs=[vmem] * 3,
        out_shape=jax.ShapeDtypeStruct(own.shape, f32),
        compiler_params=params(8),
        cost_estimate=cost(1e5, 1e4),
        name="gain_rows",
    )


def unstack_body(core_ref, mine_ref, got_ref, a_ref, i_ref, u_ref):
    first = core_ref[0] == 0
    mine, got = mine_ref[...], got_ref[...]
    full = jnp.concatenate([jnp.where(first, mine, got), jnp.where(first, got, mine)], axis=0)
    at, units = a_ref.shape[0], u_ref.shape[0]
    a_ref[...] = full[:at].astype(f32)
    for n in range(2):
        i_ref[n] = full[at + n * units : at + (n + 1) * units].astype(f32)
    u_ref[...] = full[at + 2 * units :].astype(f32)


def unstack(core, mine, got, width, units, deps=()):
    d = mine.shape[1]
    vmem = pl.BlockSpec(memory_space=pltpu.VMEM)
    return call(
        unstack_body,
        (core, mine, got,),
        deps,
        in_specs=[pl.BlockSpec(memory_space=pltpu.SMEM), vmem, vmem],
        out_shape=[
            jax.ShapeDtypeStruct((width, d), f32),
            jax.ShapeDtypeStruct((2, units, d), f32),
            jax.ShapeDtypeStruct((units, d), f32),
        ],
        compiler_params=params(20),
        cost_estimate=cost(1e8, 10e6),
        name="unstack",
    )


def unpair_body(core_ref, mine_ref, got_ref, out_ref):
    first = core_ref[0] == 0
    half = mine_ref.shape[0] // 3
    for pair in range(3):
        rows = slice(pair * half, (pair + 1) * half)
        mine, got = mine_ref[rows], got_ref[rows]
        full = jnp.concatenate([jnp.where(first, mine, got), jnp.where(first, got, mine)], axis=0)
        for n in range(3):
            turned = full[n * PAIR : (n + 1) * PAIR].T.astype(f32)
            out_ref[n, :, pair * PAIR : (pair + 1) * PAIR] = turned


def unpair(core, mine, got, deps=()):
    d = mine.shape[1]
    vmem = pl.BlockSpec(memory_space=pltpu.VMEM)
    return call(
        unpair_body,
        (core, mine, got,),
        deps,
        in_specs=[pl.BlockSpec(memory_space=pltpu.SMEM), vmem, vmem],
        out_shape=jax.ShapeDtypeStruct((3, d, 3 * PAIR), f32),
        compiler_params=params(14),
        cost_estimate=cost(1e8, 6e6),
        name="unpair",
    )


def combine_body(side_ref, k0, c0, k1, c1, own_ref, far_ref, mine_ref, other_ref):
    low = side_ref[0] == 0
    head = own_ref.shape[0]
    half = mine_ref.shape[1]
    for n, (keep, came, out) in enumerate(((k0, c0, own_ref), (k1, c1, far_ref))):
        total = (keep[...].astype(f32) + came[...].astype(f32)).astype(bf16)
        out[...] = total[:head]
        first, second = total[head : head + half], total[head + half :]
        mine_ref[n] = jnp.where(low, first, second)
        other_ref[n] = jnp.where(low, second, first)


def combine(side, keep0, came0, keep1, came1, head, deps=()):
    rows, d = keep0.shape
    half = (rows - head) // 2
    vmem = pl.BlockSpec(memory_space=pltpu.VMEM)
    cut = jax.ShapeDtypeStruct((2, half, d), bf16)
    return call(
        combine_body,
        (side, keep0, came0, keep1, came1),
        deps,
        in_specs=[pl.BlockSpec(memory_space=pltpu.SMEM)] + [vmem] * 4,
        out_shape=[jax.ShapeDtypeStruct((head, d), bf16)] * 2 + [cut] * 2,
        compiler_params=params(20),
        cost_estimate=cost(1e5, 1e4),
        name="combine",
    )


def second_body(side_ref, own_ref, got_a, mine_ref, got_b, keep_ref, pair_ref, far_ref, over_ref):
    low = side_ref[0] == 0
    total = (own_ref[...].astype(f32) + got_a[...].astype(f32)).astype(bf16)
    half = total.shape[0] // 2
    first, second = total[:half], total[half:]
    keep_ref[...] = jnp.where(low, first, second)
    over_ref[...] = jnp.where(low, second, first)
    pair = (mine_ref[...].astype(f32) + got_b[...].astype(f32)).astype(bf16)
    pair_ref[...] = pair[0]
    far_ref[...] = pair[1]


def second_step(side, own, got_a, mine, got_b, deps=()):
    rows, d = own.shape
    half = mine.shape[1]
    vmem = pl.BlockSpec(memory_space=pltpu.VMEM)
    return call(
        second_body,
        (side, own, got_a, mine, got_b),
        deps,
        in_specs=[pl.BlockSpec(memory_space=pltpu.SMEM)] + [vmem] * 4,
        out_shape=[
            jax.ShapeDtypeStruct((rows // 2, d), bf16),
            jax.ShapeDtypeStruct((half, d), bf16),
            jax.ShapeDtypeStruct((half, d), bf16),
            jax.ShapeDtypeStruct((rows // 2, d), bf16),
        ],
        compiler_params=params(14),
        cost_estimate=cost(1e5, 1e4),
        name="second_step",
    )


def cut_body(low_ref, *refs):
    *terms, keep_ref, over_ref = refs
    low = low_ref[0] == 0
    sums = [
        terms[n][...].astype(f32) + terms[n + 1][...].astype(f32) for n in range(0, len(terms), 2)
    ]
    short = 2 * keep_ref.shape[0] - sum(x.shape[0] for x in sums)
    if short:
        sums.append(jnp.zeros((short, sums[0].shape[1]), f32))
    total = jnp.concatenate(sums, axis=0)
    half = total.shape[0] // 2
    first, second = total[:half], total[half:]
    keep_ref[...] = jnp.where(low, first, second).astype(bf16)
    over_ref[...] = jnp.where(low, second, first).astype(bf16)


def cut_sums(low, terms, deps=()):
    rows = (sum(x.shape[0] for x in terms) // 2 + 31) // 32 * 32
    vmem = pl.BlockSpec(memory_space=pltpu.VMEM)
    return call(
        cut_body,
        (low, *terms),
        deps,
        in_specs=[pl.BlockSpec(memory_space=pltpu.SMEM)] + [vmem] * len(terms),
        out_shape=[jax.ShapeDtypeStruct((rows // 2, terms[0].shape[1]), bf16)] * 2,
        compiler_params=params(12),
        cost_estimate=cost(1e5, 1e4),
        name="cut_sums",
    )


def plus_body(a_ref, b_ref, out_ref):
    out_ref[...] = (a_ref[...].astype(f32) + b_ref[...].astype(f32)).astype(bf16)


def plus(a, b, deps=()):
    vmem = pl.BlockSpec(memory_space=pltpu.VMEM)
    return call(
        plus_body,
        (a, b),
        deps,
        in_specs=[vmem] * 2,
        out_shape=jax.ShapeDtypeStruct(a.shape, bf16),
        compiler_params=params(8),
        cost_estimate=cost(1e5, 1e4),
        name="plus",
    )


def pairs_body(side_ref, first_ref, keep, came, mine_ref, other_ref):
    low = side_ref[0] == 0
    first = first_ref[...]
    second = (keep[...].astype(f32) + came[...].astype(f32)).astype(bf16)
    mine_ref[...] = jnp.where(low, first, second)
    other_ref[...] = jnp.where(low, second, first)


def last_pair_body(side_ref, keep, came, mine_ref, other_ref):
    low = side_ref[0] == 0
    total = (keep[...].astype(f32) + came[...].astype(f32)).astype(bf16)
    half = total.shape[0] // 2
    mine_ref[...] = jnp.where(low, total[:half], total[half:])
    other_ref[...] = jnp.where(low, total[half:], total[:half])


def pairs_step(side, arrays, rows, deps=()):
    vmem = pl.BlockSpec(memory_space=pltpu.VMEM)
    shape = jax.ShapeDtypeStruct((rows, arrays[0].shape[1]), bf16)
    return call(
        pairs_body if len(arrays) == 3 else last_pair_body,
        (side, *arrays),
        deps,
        in_specs=[pl.BlockSpec(memory_space=pltpu.SMEM)] + [vmem] * len(arrays),
        out_shape=[shape] * 2,
        compiler_params=params(10),
        cost_estimate=cost(1e5, 1e4),
        name="pairs_step",
    )


def tail_body(
    b0, b1, b2, w_ref, h_ref, dn_ref, gg_ref
):
    dn = nn(jnp.concatenate([b0[...], b1[...], b2[...]], axis=1), w_ref[...])
    dn_ref[...] = dn.astype(dn_ref.dtype)
    xh, unused = unit_rows(h_ref[...].astype(f32))

    @pl.when(pl.program_id(0) == 0)
    def _():
        gg_ref[...] = jnp.zeros_like(gg_ref)

    gg_ref[...] += jnp.sum((dn * xh).reshape(-1, 8, dn.shape[1]), axis=0)


def tail(parts, w, h, first, dtype, deps=()):
    rows, d = h.shape
    off = first // BLK
    part = pl.BlockSpec((BLK, 3 * PAIR), lambda i: (i + off, 0))
    row = pl.BlockSpec((BLK, d), lambda i: (i, 0))
    return call(
        tail_body,
        (*parts, w, h,),
        deps,
        grid=(rows // BLK,),
        in_specs=[part] * 3 + [whole(w.shape), row],
        out_specs=[row, whole((8, d))],
        out_shape=[
            jax.ShapeDtypeStruct((rows, d), dtype),
            jax.ShapeDtypeStruct((8, d), f32),
        ],
        compiler_params=params(14),
        cost_estimate=cost(1e5, 1e4),
        name="tail",
    )


def last_body(h_ref, gain_ref, own_ref, got_ref, late_ref, dx_ref, out_ref):
    xh, inv = unit_rows(h_ref[...].astype(f32))
    got = jnp.where(pl.program_id(0) == 0, got_ref[...].astype(f32), late_ref[...].astype(f32))
    dn = own_ref[...] + got
    out_ref[...] = (dx_ref[...] + norm_back(dn * gain_ref[...], xh, inv)).astype(bf16)


def last(h, gain, own, got, late, dx, deps=()):
    rows, d = h.shape
    half = rows // 2
    row = pl.BlockSpec((half, d), lambda i: (i, 0))
    return call(
        last_body,
        (h, gain, own, got, late, dx),
        deps,
        grid=(2,),
        in_specs=[row, whole((1, d)), row, whole((half, d)), whole((half, d)), row],
        out_specs=row,
        out_shape=jax.ShapeDtypeStruct((rows, d), bf16),
        compiler_params=params(12),
        cost_estimate=cost(40 * rows * d, 9e6),
        name="last",
    )


def on_device(dp, hidden_in, bounds, attn_gain, w_qkv, w_attn, mlp_gain, w_in, w_out, cotangent):
    rows, d = hidden_in.shape
    cap = 2 * rows
    width = w_attn.shape[0]
    units = w_out.shape[0]
    shard = lax.axis_index("tensor")
    place = lax.axis_index("dp")
    core = place % 2
    core_at = core.astype(jnp.int32).reshape(1)
    side = (place // 2) % 2
    groups = [list(range(c, dp, 2)) for c in range(2)]
    bits = [1 << n for n in range(dp.bit_length() - 1)]

    def over_y(x):
        return lax.ppermute(x, "tensor", [(0, 1), (1, 0)])

    def over(x, bit):
        return lax.ppermute(x, "dp", [(n, n ^ bit) for n in range(dp)])

    def over_core(x):
        return over(x, 1)

    def add(a, b):
        return (a.astype(f32) + b.astype(f32)).astype(bf16)

    def in_order(first, mine, got):
        return jnp.concatenate(
            [jnp.where(first, mine, got), jnp.where(first, got, mine)], axis=0
        )

    hidden_got = over_y(hidden_in)
    cosine, sine, feat_q, feat_k = tables(
        bounds, (shard * rows).astype(jnp.int32).reshape(1), cap
    )
    gain_a = attn_gain.reshape(1, d)
    gain_m = mlp_gain.reshape(1, d)
    held = qkv(hidden_in, gain_a, w_qkv, cosine, sine, 0, ())
    w_own, w_qkv_turned = stack(w_attn, jnp.swapaxes(w_in, 1, 2), w_out, w_qkv)
    quarter = w_own.shape[0] // 4
    piece = lax.dynamic_slice_in_dim(w_own, (2 * core + side) * quarter, quarter, 0)
    hidden_got, piece, held = lax.optimization_barrier((hidden_got, piece, held))
    n1, q, k, v = qkv(hidden_got, gain_a, w_qkv, cosine, sine, rows, held)

    def after(x, *done):
        return lax.optimization_barrier((x, done))[0]

    cut = (quarter // 2 + 15) // 16 * 16
    cuts = (piece[:cut], piece[cut:])
    from_y = [over_y(x) for x in cuts]
    first = attend(0, q, k, v, feat_q, feat_k, ())
    from_x = [over(after(from_y[0], first[0]), 2)]
    second = attend(1, q, k, v, feat_q, feat_k, first[:2])
    from_x.append(over(after(from_y[1], second[0]), 2))
    third = attend(2, q, k, v, feat_q, feat_k, second[:1])
    o_got = [over_y(second[1]), over_y(third[1])]
    pieces = [from_y[0], from_x[0], over_core(from_y[0]), over_core(after(from_x[0], second[0]))]
    pieces += [from_y[1], from_x[1], over_core(from_y[1]), over_core(after(from_x[1], third[0]))]
    at = jnp.arange(2, dtype=jnp.int32)[:, None] * cut + jnp.stack(
        [(2 * c + s) * quarter for c in (core, 1 - core) for s in (side, 1 - side)]
    )
    o_own = third[0]
    o_far = (second[1], second[1], third[1])
    q_tag = [x[2:] for x in (first, second, third)]
    w_got = assemble(at.reshape(8), pieces, w_own.shape, (o_got[0],))
    scalars = jnp.stack([shard * rows, bounds[0, NSEG - 1]]).astype(jnp.int32)
    (
        hidden_out, n2, ga, dx, gm, by_unit, d_own, db01, db2, gg_mlp,
    ) = mlp(scalars, hidden_in, cotangent, o_own, o_got, gain_m, w_own, w_got, units)
    d_got = [over_y(db01), over_y(db2)]
    d_far = (d_got[0], d_got[0], d_got[1])

    def back(pair, start, stop, begun, *deps):
        return attend_back(
            pair, start, stop, begun, *q_tag[pair], q, k, v, feat_k, o_own, o_far[pair],
            d_own, d_far[pair], cosine, sine, deps,
        )

    def split(x, bit):
        low = (place & bit) == 0
        half = x.shape[0] // 2
        first, second = x[:half], x[half:]
        return jnp.where(low, first, second), jnp.where(low, second, first)

    def merge(x, bit):
        return in_order((place & bit) == 0, x, over(x, bit))

    def over_rest(x):
        if len(bits) < 3:
            return x
        mine, other = split(x, bits[2])
        mine = add(mine, over(other, bits[2]))
        for bit in bits[3:]:
            mine = add(mine, over(mine, bit))
        return merge(mine, bits[2])

    keep1, send1 = weight_grads(1, core_at, o_got, by_unit, n2, ga, gm)
    keep0, send0 = weight_grads(0, core_at, (o_own,), by_unit, n2, ga, gm, (keep1,))
    came1 = over_core(send1)
    came0 = over_core(after(send0, d_got[0]))
    head = send0.shape[0] // 32 * 16 - 16
    own_a, far_a, mine_b, other_b = combine(
        side.astype(jnp.int32).reshape(1), keep0, came0, keep1, came1, head
    )
    got_a, got_b = over_y(far_a), over(other_b, 2)
    blocks = cap // KBLK
    back0 = back(0, 0, blocks, (), mine_b, far_a)[0]
    keep, send = pair_grads(core_at, back0, n1)

    side_at = side.astype(jnp.int32).reshape(1)
    mine, mine_b, far_b, other_a = second_step(side_at, own_a, got_a, mine_b, got_b, (back0,))
    got_a, got_b = over(other_a, 2), over_y(far_b)
    begun = back(1, 0, 1, (), keep, mine)
    pair0 = plus(keep, over_core(send))

    if len(bits) > 2:
        low = ((place // 4) % 2).astype(jnp.int32).reshape(1)
        mine, other = cut_sums(low, (mine, got_a, mine_b, got_b), (begun[0],))
        got = over(other, bits[2])
    else:
        mine = jnp.concatenate([add(mine, got_a), add(mine_b, got_b)], axis=0)
    back1 = back(1, 1, blocks, begun, mine, pair0)[0]
    keep, send = pair_grads(core_at, back1, n1)

    if len(bits) > 2:
        mine = plus(mine, got, (back1,))
    if len(bits) > 3:
        got = over(mine, bits[3])
    came = over_core(send)
    q_mine, q_other = pairs_step(side_at, (pair0, keep, came), pair0.shape[0])
    q_got = over(q_other, 2)
    back2 = back(2, 0, blocks, (), mine, q_other)[0]
    if len(bits) > 3:
        mine = plus(mine, got, (back2,))
    parts = (back0, back1, back2)
    keep, send = pair_grads(core_at, back2, n1, (mine, q_got))
    dn_other, gg_other = tail(parts, w_qkv_turned, hidden_got, rows, bf16, (keep,))
    cut_at = rows // 2
    dn_got = over_y(dn_other[:cut_at])
    came = over_core(send)
    if len(bits) > 2:
        for bit in bits[4:]:
            mine = add(mine, over(mine, bit))
        mine = merge(mine, bits[2])
    last_mine, last_other = pairs_step(
        side_at, (keep, came), pair0.shape[0] // 2, (dn_other,)
    )
    dn_own, gg_own = tail(parts, w_qkv_turned, hidden_in, 0, f32, (last_other,))
    gains = gain_rows(gg_own, gg_other, gg_mlp)
    gains = gains + over_core(gains)
    last_got = over(last_other, 2)
    weights = mine
    if len(bits) > 2:
        mine, other = cut_sums(
            low, (q_mine, q_got, last_mine, last_got, gains, over(gains, 2)), (dn_got,)
        )
        lent = over(other, bits[2])
        got = over(after(weights, mine), 2)
        low_side = (place & 2) == 0
        grads = jnp.concatenate(
            [in_order(low_side, weights[: head // 2], got[: head // 2]),
             in_order(low_side, weights[head // 2 : quarter], got[head // 2 : quarter])],
            axis=0,
        )
        mine = plus(mine, lent)
        dn_late = over_y(after(dn_other[cut_at:], mine))
        for bit in bits[3:-1]:
            mine = plus(mine, over(mine, bit))
        if len(bits) > 3:
            mine = plus(mine, over(mine, bits[-1]), (got,))
        mine = merge(mine, bits[2])
    else:
        mine = jnp.concatenate(
            [add(q_mine, q_got), add(last_mine, last_got), add(gains, over(gains, 2))], axis=0
        )
        dn_late = over_y(dn_other[cut_at:])
        got = over(after(weights, mine), 2)
        low_side = (place & 2) == 0
        grads = jnp.concatenate(
            [in_order(low_side, weights[: head // 2], got[: head // 2]),
             in_order(low_side, weights[head // 2 : quarter], got[head // 2 : quarter])],
            axis=0,
        )
    low_side = (place & 2) == 0
    grad_in = last(hidden_in, gain_a, dn_own, dn_got, dn_late, dx)
    first, count = pair0.shape[0], 3 * pair0.shape[0] // 2
    gains = mine[count : count + 2].astype(f32)
    gains = gains + over_y(gains)
    got = over(after(mine[:count], grad_in), 2)
    pairs = jnp.concatenate(
        [in_order(low_side, mine[:first], got[:first]),
         in_order(low_side, mine[first:count], got[first:])],
        axis=0,
    )

    grad_w_attn, grad_w_in, grad_w_out = unstack(core_at, grads, over_core(grads), width, units)
    grad_w_in = jnp.swapaxes(grad_w_in, 1, 2)
    grad_w_qkv = unpair(core_at, pairs, over_core(after(pairs, grad_w_attn)))
    return (
        hidden_out,
        grad_in,
        gains[0],
        grad_w_qkv,
        grad_w_attn,
        gains[1],
        grad_w_in,
        grad_w_out,
    )


def solution(mesh):
    in_specs = (
        P(("dp", "tensor"), None),
        P("dp", None),
        P(),
        P(None, None, "tensor"),
        P("tensor", None),
        P(),
        P(None, None, "tensor"),
        P("tensor", None),
        P(("dp", "tensor"), None),
    )
    out_specs = (
        P(("dp", "tensor"), None),
        P(("dp", "tensor"), None),
        P(),
        P(None, None, "tensor"),
        P("tensor", None),
        P(),
        P(None, None, "tensor"),
        P("tensor", None),
    )
    return jax.shard_map(
        functools.partial(on_device, mesh.shape["dp"]),
        mesh=mesh,
        in_specs=in_specs,
        out_specs=out_specs,
        check_vma=False,
    )
```

```python
import functools

import jax
import jax.numpy as jnp
import numpy as np
from jax import lax
from jax.experimental import pallas as pl
from jax.experimental.pallas import tpu as pltpu
from jax.sharding import PartitionSpec as P

HD = 64
NSEG = 6
PAIR = 2 * HD
BLK = 384
MLP_BLK = 256
COST = 0.12
KBLK = 512
rope_theta = 160000.0
norm_eps = 1e-05
masked_score = -1e30
f32 = jnp.float32
bf16 = jnp.bfloat16


def params(mib):
    return pltpu.CompilerParams(vmem_limit_bytes=mib * 1024 * 1024)


def cost(flops, nbytes):
    return pl.CostEstimate(
        flops=int(flops * COST), bytes_accessed=int(nbytes * COST), transcendentals=0
    )


def nn(a, b):
    return jnp.dot(a, b, preferred_element_type=f32)


def nt(a, b):
    return lax.dot_general(a, b, (((1,), (1,)), ((), ())), preferred_element_type=f32)


def call(body, args, deps=(), *, in_specs, **kw):
    first = len(in_specs)

    def run(*refs):
        body(*refs[:first], *refs[first + len(deps) :])

    return pl.pallas_call(
        run, in_specs=list(in_specs) + [pl.BlockSpec(memory_space=pl.ANY)] * len(deps), **kw
    )(*args, *deps)


def whole(shape):
    return pl.BlockSpec(shape, lambda i: (0,) * len(shape))


def unit_rows(x):
    centred = x - jnp.mean(x, axis=-1, keepdims=True)
    inv = lax.rsqrt(jnp.mean(centred * centred, axis=-1, keepdims=True) + norm_eps)
    return centred * inv, inv


def norm_back(e, xh, inv):
    return inv * (
        e - jnp.mean(e, axis=-1, keepdims=True) - xh * jnp.mean(e * xh, axis=-1, keepdims=True)
    )


def turn(x, cosine, sine, back):
    lane = lax.broadcasted_iota(jnp.int32, x.shape, 1) % HD
    other = jnp.where(lane < HD // 2, pltpu.roll(x, PAIR - HD // 2, 1), pltpu.roll(x, HD // 2, 1))
    return x * cosine - other * sine if back else x * cosine + other * sine


def sincos(x):
    turns = jnp.floor(x * 0.6366197723675814 + 0.5)
    r = ((x - turns * 1.5703125) - turns * 4.837512969970703125e-4) - turns * 7.54978995489188e-8
    z = r * r
    s = r + r * z * (-1.6666654611e-1 + z * (8.3321608736e-3 + z * -1.9515295891e-4))
    c = 1.0 - 0.5 * z + z * z * (
        4.166664568298827e-2 + z * (-1.388731625493765e-3 + z * 2.443315711809948e-5)
    )
    quarter = turns.astype(jnp.int32) & 3
    odd = (quarter & 1) == 1
    sine = jnp.where(odd, c, s)
    cosine = jnp.where(odd, s, c)
    sine = jnp.where(quarter >= 2, -sine, sine)
    cosine = jnp.where(jnp.logical_or(quarter == 1, quarter == 2), -cosine, cosine)
    return sine, cosine


def tables_body(edge_ref, first_ref, freq_ref, cos_ref, sin_ref, fq_ref, fk_ref):
    cap = cos_ref.shape[0]
    ids = lax.broadcasted_iota(jnp.int32, (cap, PAIR), 0) + first_ref[0]
    ids = jnp.where(ids >= cap, ids - cap, ids)
    lane = lax.broadcasted_iota(jnp.int32, ids.shape, 1)
    seg = jnp.zeros(ids.shape, jnp.int32)
    begin = jnp.zeros(ids.shape, jnp.int32)
    for n in range(1, NSEG):
        passed = ids >= edge_ref[0, n]
        seg = jnp.where(passed, seg + 1, seg)
        begin = jnp.where(passed, edge_ref[0, n], begin)
    angle = (ids - begin).astype(f32) * freq_ref[...]
    sine, cosine = sincos(angle)
    slot = lane % HD
    cos_ref[...] = cosine
    sin_ref[...] = jnp.where(slot < HD // 2, -sine, sine)
    same = slot == seg
    fq_ref[...] = jnp.where(same, 1.0, 0.0).astype(bf16)
    fk_ref[...] = jnp.where(
        slot < NSEG,
        jnp.where(same, 0.0, masked_score),
        jnp.where(slot < NSEG + 3, 1.0, 0.0),
    ).astype(bf16)


def tables(edges, first, cap):
    steps = 2.0 * (np.arange(PAIR) % (HD // 2)) / HD
    freq = jnp.asarray(np.exp(-steps * np.log(rope_theta))[None].astype(np.float32))
    smem = pl.BlockSpec(memory_space=pltpu.SMEM)
    table = lambda t: jax.ShapeDtypeStruct((cap, PAIR), t)
    return pl.pallas_call(
        tables_body,
        in_specs=[smem, smem, pl.BlockSpec(memory_space=pltpu.VMEM)],
        out_shape=[table(f32), table(f32), table(bf16), table(bf16)],
        compiler_params=params(8),
        cost_estimate=cost(80 * cap * PAIR, 3e6),
        name="tables",
    )(edges, first, freq)


def stack_body(a_ref, i_ref, u_ref, w_ref, out_ref, qkv_ref):
    at = a_ref.shape[0]
    units = u_ref.shape[0]
    width = w_ref.shape[2]
    out_ref[:at] = a_ref[...]
    for n in range(2):
        out_ref[at + n * units : at + (n + 1) * units] = i_ref[n]
    out_ref[at + 2 * units :] = u_ref[...]
    for n in range(3):
        turned = w_ref[n].T
        for pair in range(width // PAIR):
            to = (3 * pair + n) * PAIR
            qkv_ref[to : to + PAIR] = turned[pair * PAIR : (pair + 1) * PAIR]


def stack(w_attn, w_in_turned, w_out, w_qkv, deps=()):
    at, d = w_attn.shape
    rows = at + 3 * w_out.shape[0]
    vmem = pl.BlockSpec(memory_space=pltpu.VMEM)
    return call(
        stack_body,
        (w_attn, w_in_turned, w_out, w_qkv),
        deps,
        in_specs=[vmem] * 4,
        out_shape=[
            jax.ShapeDtypeStruct((rows, d), bf16),
            jax.ShapeDtypeStruct((3 * w_qkv.shape[2], d), bf16),
        ],
        compiler_params=params(12),
        cost_estimate=cost(1e8, 10e6),
        name="stack",
    )


def qkv_body(h_ref, gain_ref, w_ref, cos_ref, sin_ref, *refs):
    n1_ref, q_ref, k_ref, v_ref = refs[-4:]
    unit, inv = unit_rows(h_ref[...].astype(f32))
    n1 = (unit * gain_ref[...]).astype(bf16)
    n1_ref[...] = n1
    cosine, sine = cos_ref[...], sin_ref[...]
    width = w_ref.shape[2]
    for which, out, scale in ((0, q_ref, 0.125), (1, k_ref, 1.0)):
        full = nn(n1, w_ref[which])
        for at in range(0, width, PAIR):
            turned = turn(full[:, at : at + PAIR], cosine, sine, False).astype(bf16)
            if scale != 1.0:
                turned = (turned.astype(f32) * scale).astype(bf16)
            out[:, at : at + PAIR] = turned
    v_ref[...] = nn(n1, w_ref[2]).astype(bf16)


def qkv(h, gain, w, cosine, sine, first, held, deps=()):
    rows, d = h.shape
    cap, width = cosine.shape[0], w.shape[2]
    off = first // BLK
    by_row = lambda n: pl.BlockSpec((BLK, n), lambda i: (i + off, 0))
    shapes = [jax.ShapeDtypeStruct((cap, n), bf16) for n in (d, width, width, width)]
    return call(
        qkv_body,
        (h, gain, w, cosine, sine, *held),
        deps,
        grid=(rows // BLK,),
        in_specs=[
            pl.BlockSpec((BLK, d), lambda i: (i, 0)),
            whole((1, d)),
            whole(w.shape),
            by_row(PAIR),
            by_row(PAIR),
        ]
        + [pl.BlockSpec(memory_space=pl.ANY)] * len(held),
        out_specs=[by_row(d), by_row(width), by_row(width), by_row(width)],
        out_shape=shapes,
        input_output_aliases={5 + n: n for n in range(len(held))},
        compiler_params=params(14),
        cost_estimate=cost(2 * 2 * rows * d * 3 * width, 12e6),
        name="qkv",
    )


def assemble_body(at_ref, *refs):
    pieces, out_ref, sems = refs[:-2], refs[-2], refs[-1]
    copies = []
    for n, ref in enumerate(pieces):
        to = pl.ds(pl.multiple_of(at_ref[n], 8), ref.shape[0])
        copies.append(pltpu.make_async_copy(ref, out_ref.at[to], sems.at[n]))
        copies[-1].start()
    for copy in copies:
        copy.wait()


def assemble(at, pieces, shape, deps=()):
    anywhere = pl.BlockSpec(memory_space=pl.ANY)
    return call(
        assemble_body,
        (at, *pieces),
        deps,
        in_specs=[pl.BlockSpec(memory_space=pltpu.SMEM)] + [anywhere] * len(pieces),
        out_specs=pl.BlockSpec(memory_space=pltpu.VMEM),
        out_shape=jax.ShapeDtypeStruct(shape, bf16),
        scratch_shapes=[pltpu.SemaphoreType.DMA((len(pieces),))],
        compiler_params=params(8),
        cost_estimate=cost(1e6, 6e6),
        name="assemble",
    )


def lanes_of(head, shape):
    lane = lax.broadcasted_iota(jnp.int32, shape, 1)
    return (lane < HD) if head == 0 else (lane >= HD)


def attend_body(q_ref, k_ref, v_ref, fq_ref, fk_ref, *refs):
    o0_ref, o1_ref, qa_ref, qb_ref = refs[-4:]
    q, k, v, fq, fk = q_ref[...], k_ref[...], v_ref[...], fq_ref[...], fk_ref[...]
    v_turned = v.T
    rows = q.shape[0]
    line = lax.broadcasted_iota(jnp.int32, (PAIR, rows), 0)
    tag = jnp.zeros((PAIR, rows), f32)
    mixed = []
    scores = [
        nt(jnp.where(lanes_of(n, k.shape), k, fk), jnp.where(lanes_of(n, q.shape), q, fq))
        for n in (0, 1)
    ]
    for head, score in enumerate(scores):
        top = jnp.max(score, axis=0, keepdims=True)
        expo = jnp.exp(score - top)
        total = jnp.sum(expo, axis=0, keepdims=True)
        at = head * HD
        mixed.append(nn(v_turned[at : at + HD], expo.astype(bf16)) * (1.0 / total))
        left = -(top + jnp.log(total))
        for part in range(3):
            head_bits = left.astype(bf16).astype(f32)
            left = left - head_bits
            tag = jnp.where(line == HD - at + NSEG + part, head_bits, tag)
    o = jnp.concatenate(mixed, axis=0).T.astype(bf16)
    tag = tag.T
    fq = fq.astype(f32) + tag
    wide = q.astype(f32)
    qa_ref[...] = jnp.where(lanes_of(0, q.shape), wide, fq).astype(bf16)
    qb_ref[...] = jnp.where(lanes_of(1, q.shape), wide, fq).astype(bf16)

    @pl.when(pl.program_id(0) == 0)
    def _():
        o0_ref[...] = o

    @pl.when(pl.program_id(0) == 1)
    def _():
        o1_ref[...] = o


def attend(pair, q, k, v, feat_q, feat_k, held):
    cap, width = q.shape
    rows = cap // 2
    part = pl.BlockSpec((rows, PAIR), lambda i: (i, 0))
    full = pl.BlockSpec((cap, PAIR), lambda i: (0, pair))
    column = lambda n: pl.BlockSpec((rows, PAIR), lambda i: (0, n))
    far = width - PAIR if pair < 2 else PAIR
    return pl.pallas_call(
        attend_body,
        grid=(2,),
        in_specs=[
            pl.BlockSpec((rows, PAIR), lambda i: (i, pair)),
            full,
            full,
            part,
            whole((cap, PAIR)),
        ]
        + [pl.BlockSpec(memory_space=pl.ANY)] * len(held),
        out_specs=[column(pair), column(pair % 2)] + [part] * 2,
        out_shape=[
            jax.ShapeDtypeStruct((rows, width), bf16),
            jax.ShapeDtypeStruct((rows, far), bf16),
        ]
        + [jax.ShapeDtypeStruct((cap, PAIR), bf16)] * 2,
        input_output_aliases={5 + n: n for n in range(len(held))},
        compiler_params=params(12),
        cost_estimate=cost(2 * 2 * 2 * cap * cap * 256 * 2, 3e6),
        name="attend",
    )(q, k, v, feat_q, feat_k, *held)


def back_body(
    start, begun, ends, qa_ref, qb_ref, q_ref, k_ref, v_ref, fk_ref, o0_ref, o1_ref, d0_ref, d1_ref, cos_ref, sin_ref,
    *refs,
):
    dqt_in, low_in = refs[:2] if begun else (None, None)
    outs = refs[2:-4] if begun else refs[:-4]
    dol_ref, da_ref, db_ref, dqt_ref = refs[-4:]
    out_ref = outs[0]
    step = pl.program_id(0)
    half = d0_ref.shape[0]
    cap = 2 * half

    @pl.when(step == 0)
    def _():
        dol_ref[:half] = d0_ref[...]
        dol_ref[half:] = d1_ref[...]
        dol = dol_ref[...]
        slot = lax.broadcasted_iota(jnp.int32, dol.shape, 1) % HD
        wide = dol.astype(f32)
        prod = wide * jnp.concatenate([o0_ref[...], o1_ref[...]], axis=0).astype(f32)
        for head, out in ((0, da_ref), (1, db_ref)):
            mine = lanes_of(head, dol.shape)
            left = -jnp.sum(jnp.where(mine, prod, 0.0), axis=-1, keepdims=True)
            tagged = jnp.where(mine, wide, 0.0)
            for part in range(3):
                head_bits = left.astype(bf16).astype(f32)
                left = left - head_bits
                tagged = jnp.where(
                    jnp.logical_and(jnp.logical_not(mine), slot == NSEG + part), head_bits, tagged
                )
            out[...] = tagged.astype(bf16)
        if begun:
            dqt_ref[...] = dqt_in[...]
            out_ref[: start * KBLK, PAIR:] = low_in[...]
        else:
            dqt_ref[...] = jnp.zeros_like(dqt_ref)

    k, v, fk, q, dol = k_ref[...], v_ref[...], fk_ref[...], q_ref[...], dol_ref[...]
    k_turned = k.T
    slot = lax.broadcasted_iota(jnp.int32, v.shape, 1) % HD
    ones = jnp.where(
        jnp.logical_and(slot >= NSEG, slot < NSEG + 3), 1.0, 0.0
    ).astype(bf16)
    heads = ((0, qa_ref, da_ref), (1, qb_ref, db_ref))
    scores = [nt(jnp.where(lanes_of(h, k.shape), k, fk), a[...]) for h, a, b in heads]
    grads = [nt(jnp.where(lanes_of(h, v.shape), v, ones), b[...]) for h, a, b in heads]
    probs = [jnp.exp(s) for s in scores]
    dvs = [nn(p.astype(bf16), dol) for p in probs]
    dss = [(p * g).astype(bf16) for p, g in zip(probs, grads)]
    dks = [nn(s, q) for s in dss]
    for h in (0, 1):
        dqt_ref[h * HD : h * HD + HD] += nn(k_turned[h * HD : h * HD + HD], dss[h])
    first = lanes_of(0, k.shape)
    rows = pl.ds(pl.multiple_of((step + start) * KBLK, KBLK), KBLK)
    dk = turn(jnp.where(first, dks[0], dks[1]), cos_ref[rows], sin_ref[rows], True).astype(bf16)
    dv = jnp.where(first, dvs[0], dvs[1]).astype(bf16)
    if ends:
        out_ref[rows, PAIR : 2 * PAIR] = dk
        out_ref[rows, 2 * PAIR :] = dv
    else:
        outs[1][:, :PAIR] = dk
        outs[1][:, PAIR:] = dv

    @pl.when(step == pl.num_programs(0) - 1)
    def _():
        if ends:
            dq = dqt_ref[...].T * 0.125
            out_ref[:, :PAIR] = turn(dq, cos_ref[...], sin_ref[...], True).astype(bf16)
        else:
            out_ref[...] = dqt_ref[...]


def attend_back(
    pair, start, stop, begun, qa, qb, q, k, v, feat_k, o0, o1, d0, d1, cosine, sine, deps=()
):
    cap = q.shape[0]
    ends = stop * KBLK == cap
    full = whole((cap, PAIR))
    block = pl.BlockSpec((KBLK, PAIR), lambda i: (i + start, pair))
    part = pl.BlockSpec((KBLK, PAIR), lambda i: (i + start, 0))
    column = lambda n: pl.BlockSpec((cap // 2, PAIR), lambda i: (0, n))
    if ends:
        out_specs = [whole((cap, 3 * PAIR))]
        out_shape = [jax.ShapeDtypeStruct((cap, 3 * PAIR), bf16)]
    else:
        out_specs = [whole((PAIR, cap)), pl.BlockSpec((KBLK, 2 * PAIR), lambda i: (i, 0))]
        out_shape = [
            jax.ShapeDtypeStruct((PAIR, cap), f32),
            jax.ShapeDtypeStruct(((stop - start) * KBLK, 2 * PAIR), bf16),
        ]
    return call(
        functools.partial(back_body, start, bool(begun), ends),
        (qa, qb, q, k, v, feat_k, o0, o1, d0, d1, cosine, sine, *begun),
        deps,
        grid=(stop - start,),
        in_specs=[
            full,
            full,
            pl.BlockSpec((cap, PAIR), lambda i: (0, pair)),
            block,
            block,
            part,
            column(pair),
            column(pair % 2),
            column(pair),
            column(pair % 2),
            full,
            full,
        ]
        + [whole(x.shape) for x in begun],
        out_specs=out_specs,
        out_shape=out_shape,
        scratch_shapes=[
            pltpu.VMEM((cap, PAIR), bf16),
            pltpu.VMEM((cap, PAIR), bf16),
            pltpu.VMEM((cap, PAIR), bf16),
            pltpu.VMEM((PAIR, cap), f32),
        ],
        compiler_params=params(58),
        cost_estimate=cost(5 * 2 * 2 * (stop - start) * KBLK * cap * 256 * 2, 6e6),
        name="attend_back",
    )


def mlp_body(
    sc_ref, h_ref, cot_ref, oa_ref, ob01, ob2, gain_ref, own_ref, got_ref,
    out_ref, n2_ref, ga_ref, dx_ref, gm_ref, unit_ref, da_ref, db01, db2, gg_ref,
):
    step = pl.program_id(0)
    oa = oa_ref[...]
    ob = jnp.concatenate([ob01[...], ob2[...]], axis=1)
    width = oa.shape[1]
    units = unit_ref.shape[2]
    in0 = slice(width, width + units)
    in1 = slice(width + units, width + 2 * units)
    up = slice(width + 2 * units, width + 3 * units)
    x1 = h_ref[...].astype(f32) + (nn(oa, own_ref[:width]) + nn(ob, got_ref[:width]))
    xh, inv = unit_rows(x1)
    gain = gain_ref[...]
    n2 = (xh * gain).astype(bf16)
    n2_ref[...] = n2
    ids = sc_ref[0] + step * MLP_BLK + lax.broadcasted_iota(jnp.int32, x1.shape, 0)
    g = jnp.where(ids < sc_ref[1], cot_ref[...].astype(f32), 0.0)
    gm = g.astype(bf16)
    gm_ref[...] = gm
    m = jnp.zeros_like(x1)
    dn2 = jnp.zeros_like(x1)
    for n, w_ref in enumerate((own_ref, got_ref)):
        act = nt(n2, w_ref[in0])
        gate = nt(n2, w_ref[in1])
        phi = 0.5 * (1.0 + lax.erf(act * 0.7071067811865476))
        bell = jnp.exp(-0.5 * act * act) * 0.3989422804014327
        gelu = act * phi
        hidden = (gelu * gate).astype(bf16)
        unit_ref[3 * n + 2] = hidden
        m = m + nn(hidden, w_ref[up])
        dh = nt(gm, w_ref[up])
        dact = (dh * gate * (phi + act * bell)).astype(bf16)
        dgate = (dh * gelu).astype(bf16)
        unit_ref[3 * n] = dact
        unit_ref[3 * n + 1] = dgate
        dn2 = dn2 + nn(dact, w_ref[in0]) + nn(dgate, w_ref[in1])
    out_ref[...] = (x1 + m).astype(bf16)

    @pl.when(step == 0)
    def _():
        gg_ref[...] = jnp.zeros_like(gg_ref)

    gg_ref[...] += jnp.sum((dn2 * xh).reshape(-1, 8, x1.shape[1]), axis=0)
    dx = g + norm_back(dn2 * gain, xh, inv)
    dx_ref[...] = dx
    ga = dx.astype(bf16)
    ga_ref[...] = ga
    da_ref[...] = nt(ga, own_ref[:width]).astype(bf16)
    db = nt(ga, got_ref[:width]).astype(bf16)
    db01[...] = db[:, : 2 * PAIR]
    db2[...] = db[:, 2 * PAIR :]


def mlp(scalars, h, cot, o_own, o_got, gain, w_own, w_got, units, deps=()):
    rows, d = h.shape
    row = lambda n: pl.BlockSpec((MLP_BLK, n), lambda i: (i, 0))
    out = lambda n, t=bf16: jax.ShapeDtypeStruct((rows, n), t)
    return call(
        mlp_body,
        (scalars, h, cot, o_own, *o_got, gain, w_own, w_got),
        deps,
        grid=(rows // MLP_BLK,),
        in_specs=[pl.BlockSpec(memory_space=pltpu.SMEM), row(d), row(d)]
        + [row(3 * PAIR), row(2 * PAIR), row(PAIR)]
        + [whole((1, d))]
        + [whole(w_own.shape)] * 2,
        out_specs=[row(d)] * 5
        + [pl.BlockSpec((6, MLP_BLK, units), lambda i: (0, i, 0))]
        + [row(3 * PAIR), row(2 * PAIR), row(PAIR)]
        + [whole((8, d))],
        out_shape=[out(d), out(d), out(d), out(d, f32), out(d)]
        + [jax.ShapeDtypeStruct((6, rows, units), bf16)]
        + [out(3 * PAIR), out(2 * PAIR), out(PAIR)]
        + [jax.ShapeDtypeStruct((8, d), f32)],
        compiler_params=params(26),
        cost_estimate=cost(2 * 2 * 4 * rows * w_own.size, 24e6),
        name="mlp",
    )


def tn(a, b):
    return lax.dot_general(a, b, (((0,), (0,)), ((), ())), preferred_element_type=f32)


def grads_body(
    side, many, core_ref, *refs
):
    outs, unit_ref = refs[:many], refs[many]
    n2_ref, ga_ref, gm_ref, keep_ref, send_ref, held_ref, sems = refs[many + 1 :]
    core = core_ref[0]
    half = keep_ref.shape[0]
    n2, ga, gm = n2_ref[...], ga_ref[...], gm_ref[...]
    parts = [(x[...], ga) for x in outs]
    parts += [(unit_ref[n], n2 if n < 2 else gm) for n in range(3)]
    at = 0
    for left, right in parts:
        res = tn(left, right).astype(bf16)
        held_ref[at : at + res.shape[0]] = res
        at += res.shape[0]
    copies = []
    for out, which in ((keep_ref, core), (send_ref, 1 - core)):
        rows = pl.ds(pl.multiple_of(which * half, 16), half)
        copies.append(pltpu.make_async_copy(held_ref.at[rows], out, sems.at[len(copies)]))
        copies[-1].start()
    for copy in copies:
        copy.wait()


def weight_grads(side, core, o, by_unit, n2, ga, gm, deps=()):
    rows, d = n2.shape
    units = by_unit.shape[2]
    total = 3 * PAIR + 3 * units
    shape = jax.ShapeDtypeStruct((total // 2, d), bf16)
    vmem = pl.BlockSpec(memory_space=pltpu.VMEM)
    anywhere = pl.BlockSpec(memory_space=pl.ANY)
    return call(
        functools.partial(grads_body, side, len(o)),
        (core, *o, by_unit, n2, ga, gm),
        deps,
        grid=(1,),
        in_specs=[pl.BlockSpec(memory_space=pltpu.SMEM)]
        + [whole(x.shape) for x in o]
        + [pl.BlockSpec((3, rows, units), lambda i: (side, 0, 0))]
        + [whole((rows, d))] * 3,
        out_specs=[anywhere] * 2,
        out_shape=[shape] * 2,
        scratch_shapes=[pltpu.VMEM((total, d), bf16), pltpu.SemaphoreType.DMA((2,))],
        compiler_params=params(18),
        cost_estimate=cost(1e5, 1e4),
        name="weight_grads",
    )


def pair_body(core_ref, back_ref, n1_ref, keep_ref, send_ref, held_ref, sems):
    half = keep_ref.shape[0]
    held_ref[...] = tn(back_ref[...], n1_ref[...]).astype(bf16)
    copies = []
    for out, which in ((keep_ref, core_ref[0]), (send_ref, 1 - core_ref[0])):
        rows = pl.ds(pl.multiple_of(which * half, 16), half)
        copies.append(pltpu.make_async_copy(held_ref.at[rows], out, sems.at[len(copies)]))
        copies[-1].start()
    for copy in copies:
        copy.wait()


def pair_grads(core, back, n1, deps=()):
    cap, d = n1.shape
    rows = back.shape[1]
    shape = jax.ShapeDtypeStruct((rows // 2, d), bf16)
    vmem = pl.BlockSpec(memory_space=pltpu.VMEM)
    anywhere = pl.BlockSpec(memory_space=pl.ANY)
    return call(
        pair_body,
        (core, back, n1),
        deps,
        in_specs=[pl.BlockSpec(memory_space=pltpu.SMEM)] + [vmem] * 2,
        out_specs=[anywhere] * 2,
        out_shape=[shape] * 2,
        scratch_shapes=[pltpu.VMEM((rows, d), bf16), pltpu.SemaphoreType.DMA((2,))],
        compiler_params=params(10),
        cost_estimate=cost(1e5, 1e4),
        name="pair_grads",
    )


def gains_body(own_ref, other_ref, mlp_ref, out_ref):
    a = jnp.sum(own_ref[...] + other_ref[...], axis=0, keepdims=True)
    m = jnp.sum(mlp_ref[...], axis=0, keepdims=True)
    line = lax.broadcasted_iota(jnp.int32, out_ref.shape, 0)
    out_ref[...] = jnp.where(line == 0, a, jnp.where(line == 1, m, 0.0))


def gain_rows(own, other, mlp_part):
    vmem = pl.BlockSpec(memory_space=pltpu.VMEM)
    return call(
        gains_body,
        (own, other, mlp_part),
        in_specs=[vmem] * 3,
        out_shape=jax.ShapeDtypeStruct(own.shape, f32),
        compiler_params=params(8),
        cost_estimate=cost(1e5, 1e4),
        name="gain_rows",
    )


def unstack_body(core_ref, mine_ref, got_ref, a_ref, i_ref, u_ref):
    first = core_ref[0] == 0
    mine, got = mine_ref[...], got_ref[...]
    full = jnp.concatenate([jnp.where(first, mine, got), jnp.where(first, got, mine)], axis=0)
    at, units = a_ref.shape[0], u_ref.shape[0]
    a_ref[...] = full[:at].astype(f32)
    for n in range(2):
        i_ref[n] = full[at + n * units : at + (n + 1) * units].astype(f32)
    u_ref[...] = full[at + 2 * units :].astype(f32)


def unstack(core, mine, got, width, units, deps=()):
    d = mine.shape[1]
    vmem = pl.BlockSpec(memory_space=pltpu.VMEM)
    return call(
        unstack_body,
        (core, mine, got,),
        deps,
        in_specs=[pl.BlockSpec(memory_space=pltpu.SMEM), vmem, vmem],
        out_shape=[
            jax.ShapeDtypeStruct((width, d), f32),
            jax.ShapeDtypeStruct((2, units, d), f32),
            jax.ShapeDtypeStruct((units, d), f32),
        ],
        compiler_params=params(20),
        cost_estimate=cost(1e8, 10e6),
        name="unstack",
    )


def unpair_body(core_ref, mine_ref, got_ref, out_ref):
    first = core_ref[0] == 0
    half = mine_ref.shape[0] // 3
    for pair in range(3):
        rows = slice(pair * half, (pair + 1) * half)
        mine, got = mine_ref[rows], got_ref[rows]
        full = jnp.concatenate([jnp.where(first, mine, got), jnp.where(first, got, mine)], axis=0)
        for n in range(3):
            turned = full[n * PAIR : (n + 1) * PAIR].T.astype(f32)
            out_ref[n, :, pair * PAIR : (pair + 1) * PAIR] = turned


def unpair(core, mine, got, deps=()):
    d = mine.shape[1]
    vmem = pl.BlockSpec(memory_space=pltpu.VMEM)
    return call(
        unpair_body,
        (core, mine, got,),
        deps,
        in_specs=[pl.BlockSpec(memory_space=pltpu.SMEM), vmem, vmem],
        out_shape=jax.ShapeDtypeStruct((3, d, 3 * PAIR), f32),
        compiler_params=params(14),
        cost_estimate=cost(1e8, 6e6),
        name="unpair",
    )


def combine_body(side_ref, k0, c0, k1, c1, own_ref, far_ref, mine_ref, other_ref):
    low = side_ref[0] == 0
    head = own_ref.shape[0]
    half = mine_ref.shape[1]
    for n, (keep, came, out) in enumerate(((k0, c0, own_ref), (k1, c1, far_ref))):
        total = (keep[...].astype(f32) + came[...].astype(f32)).astype(bf16)
        out[...] = total[:head]
        first, second = total[head : head + half], total[head + half :]
        mine_ref[n] = jnp.where(low, first, second)
        other_ref[n] = jnp.where(low, second, first)


def combine(side, keep0, came0, keep1, came1, head, deps=()):
    rows, d = keep0.shape
    half = (rows - head) // 2
    vmem = pl.BlockSpec(memory_space=pltpu.VMEM)
    cut = jax.ShapeDtypeStruct((2, half, d), bf16)
    return call(
        combine_body,
        (side, keep0, came0, keep1, came1),
        deps,
        in_specs=[pl.BlockSpec(memory_space=pltpu.SMEM)] + [vmem] * 4,
        out_shape=[jax.ShapeDtypeStruct((head, d), bf16)] * 2 + [cut] * 2,
        compiler_params=params(20),
        cost_estimate=cost(1e5, 1e4),
        name="combine",
    )


def second_body(side_ref, own_ref, got_a, mine_ref, got_b, keep_ref, pair_ref, far_ref, over_ref):
    low = side_ref[0] == 0
    total = (own_ref[...].astype(f32) + got_a[...].astype(f32)).astype(bf16)
    half = total.shape[0] // 2
    first, second = total[:half], total[half:]
    keep_ref[...] = jnp.where(low, first, second)
    over_ref[...] = jnp.where(low, second, first)
    pair = (mine_ref[...].astype(f32) + got_b[...].astype(f32)).astype(bf16)
    pair_ref[...] = pair[0]
    far_ref[...] = pair[1]


def second_step(side, own, got_a, mine, got_b, deps=()):
    rows, d = own.shape
    half = mine.shape[1]
    vmem = pl.BlockSpec(memory_space=pltpu.VMEM)
    return call(
        second_body,
        (side, own, got_a, mine, got_b),
        deps,
        in_specs=[pl.BlockSpec(memory_space=pltpu.SMEM)] + [vmem] * 4,
        out_shape=[
            jax.ShapeDtypeStruct((rows // 2, d), bf16),
            jax.ShapeDtypeStruct((half, d), bf16),
            jax.ShapeDtypeStruct((half, d), bf16),
            jax.ShapeDtypeStruct((rows // 2, d), bf16),
        ],
        compiler_params=params(14),
        cost_estimate=cost(1e5, 1e4),
        name="second_step",
    )


def cut_body(low_ref, *refs):
    *terms, keep_ref, over_ref = refs
    low = low_ref[0] == 0
    sums = [
        terms[n][...].astype(f32) + terms[n + 1][...].astype(f32) for n in range(0, len(terms), 2)
    ]
    short = 2 * keep_ref.shape[0] - sum(x.shape[0] for x in sums)
    if short:
        sums.append(jnp.zeros((short, sums[0].shape[1]), f32))
    total = jnp.concatenate(sums, axis=0)
    half = total.shape[0] // 2
    first, second = total[:half], total[half:]
    keep_ref[...] = jnp.where(low, first, second).astype(bf16)
    over_ref[...] = jnp.where(low, second, first).astype(bf16)


def cut_sums(low, terms, deps=()):
    rows = (sum(x.shape[0] for x in terms) // 2 + 31) // 32 * 32
    vmem = pl.BlockSpec(memory_space=pltpu.VMEM)
    return call(
        cut_body,
        (low, *terms),
        deps,
        in_specs=[pl.BlockSpec(memory_space=pltpu.SMEM)] + [vmem] * len(terms),
        out_shape=[jax.ShapeDtypeStruct((rows // 2, terms[0].shape[1]), bf16)] * 2,
        compiler_params=params(12),
        cost_estimate=cost(1e5, 1e4),
        name="cut_sums",
    )


def plus_body(a_ref, b_ref, out_ref):
    out_ref[...] = (a_ref[...].astype(f32) + b_ref[...].astype(f32)).astype(bf16)


def plus(a, b, deps=()):
    vmem = pl.BlockSpec(memory_space=pltpu.VMEM)
    return call(
        plus_body,
        (a, b),
        deps,
        in_specs=[vmem] * 2,
        out_shape=jax.ShapeDtypeStruct(a.shape, bf16),
        compiler_params=params(8),
        cost_estimate=cost(1e5, 1e4),
        name="plus",
    )


def pairs_body(side_ref, first_ref, keep, came, mine_ref, other_ref):
    low = side_ref[0] == 0
    first = first_ref[...]
    second = (keep[...].astype(f32) + came[...].astype(f32)).astype(bf16)
    mine_ref[...] = jnp.where(low, first, second)
    other_ref[...] = jnp.where(low, second, first)


def last_pair_body(side_ref, keep, came, mine_ref, other_ref):
    low = side_ref[0] == 0
    total = (keep[...].astype(f32) + came[...].astype(f32)).astype(bf16)
    half = total.shape[0] // 2
    mine_ref[...] = jnp.where(low, total[:half], total[half:])
    other_ref[...] = jnp.where(low, total[half:], total[:half])


def pairs_step(side, arrays, rows, deps=()):
    vmem = pl.BlockSpec(memory_space=pltpu.VMEM)
    shape = jax.ShapeDtypeStruct((rows, arrays[0].shape[1]), bf16)
    return call(
        pairs_body if len(arrays) == 3 else last_pair_body,
        (side, *arrays),
        deps,
        in_specs=[pl.BlockSpec(memory_space=pltpu.SMEM)] + [vmem] * len(arrays),
        out_shape=[shape] * 2,
        compiler_params=params(10),
        cost_estimate=cost(1e5, 1e4),
        name="pairs_step",
    )


def tail_body(
    b0, b1, b2, w_ref, h_ref, dn_ref, gg_ref
):
    dn = nn(jnp.concatenate([b0[...], b1[...], b2[...]], axis=1), w_ref[...])
    dn_ref[...] = dn.astype(dn_ref.dtype)
    xh, unused = unit_rows(h_ref[...].astype(f32))

    @pl.when(pl.program_id(0) == 0)
    def _():
        gg_ref[...] = jnp.zeros_like(gg_ref)

    gg_ref[...] += jnp.sum((dn * xh).reshape(-1, 8, dn.shape[1]), axis=0)


def tail(parts, w, h, first, dtype, deps=()):
    rows, d = h.shape
    off = first // BLK
    part = pl.BlockSpec((BLK, 3 * PAIR), lambda i: (i + off, 0))
    row = pl.BlockSpec((BLK, d), lambda i: (i, 0))
    return call(
        tail_body,
        (*parts, w, h,),
        deps,
        grid=(rows // BLK,),
        in_specs=[part] * 3 + [whole(w.shape), row],
        out_specs=[row, whole((8, d))],
        out_shape=[
            jax.ShapeDtypeStruct((rows, d), dtype),
            jax.ShapeDtypeStruct((8, d), f32),
        ],
        compiler_params=params(14),
        cost_estimate=cost(1e5, 1e4),
        name="tail",
    )


def last_body(h_ref, gain_ref, own_ref, got_ref, late_ref, dx_ref, out_ref):
    xh, inv = unit_rows(h_ref[...].astype(f32))
    got = jnp.where(pl.program_id(0) == 0, got_ref[...].astype(f32), late_ref[...].astype(f32))
    dn = own_ref[...] + got
    out_ref[...] = (dx_ref[...] + norm_back(dn * gain_ref[...], xh, inv)).astype(bf16)


def last(h, gain, own, got, late, dx, deps=()):
    rows, d = h.shape
    half = rows // 2
    row = pl.BlockSpec((half, d), lambda i: (i, 0))
    return call(
        last_body,
        (h, gain, own, got, late, dx),
        deps,
        grid=(2,),
        in_specs=[row, whole((1, d)), row, whole((half, d)), whole((half, d)), row],
        out_specs=row,
        out_shape=jax.ShapeDtypeStruct((rows, d), bf16),
        compiler_params=params(12),
        cost_estimate=cost(40 * rows * d, 9e6),
        name="last",
    )


def on_device(dp, hidden_in, bounds, attn_gain, w_qkv, w_attn, mlp_gain, w_in, w_out, cotangent):
    rows, d = hidden_in.shape
    cap = 2 * rows
    width = w_attn.shape[0]
    units = w_out.shape[0]
    shard = lax.axis_index("tensor")
    place = lax.axis_index("dp")
    core = place % 2
    core_at = core.astype(jnp.int32).reshape(1)
    side = (place // 2) % 2
    groups = [list(range(c, dp, 2)) for c in range(2)]
    bits = [1 << n for n in range(dp.bit_length() - 1)]

    def over_y(x):
        return lax.ppermute(x, "tensor", [(0, 1), (1, 0)])

    def over(x, bit):
        return lax.ppermute(x, "dp", [(n, n ^ bit) for n in range(dp)])

    def over_core(x):
        return over(x, 1)

    def add(a, b):
        return (a.astype(f32) + b.astype(f32)).astype(bf16)

    def in_order(first, mine, got):
        return jnp.concatenate(
            [jnp.where(first, mine, got), jnp.where(first, got, mine)], axis=0
        )

    hidden_got = over_y(hidden_in)
    cosine, sine, feat_q, feat_k = tables(
        bounds, (shard * rows).astype(jnp.int32).reshape(1), cap
    )
    gain_a = attn_gain.reshape(1, d)
    gain_m = mlp_gain.reshape(1, d)
    held = qkv(hidden_in, gain_a, w_qkv, cosine, sine, 0, ())
    w_own, w_qkv_turned = stack(w_attn, jnp.swapaxes(w_in, 1, 2), w_out, w_qkv)
    quarter = w_own.shape[0] // 4
    piece = lax.dynamic_slice_in_dim(w_own, (2 * core + side) * quarter, quarter, 0)
    hidden_got, piece, held = lax.optimization_barrier((hidden_got, piece, held))
    n1, q, k, v = qkv(hidden_got, gain_a, w_qkv, cosine, sine, rows, held)

    def after(x, *done):
        return lax.optimization_barrier((x, done))[0]

    cut = (quarter // 2 + 15) // 16 * 16
    cuts = (piece[:cut], piece[cut:])
    from_y = [over_y(x) for x in cuts]
    first = attend(0, q, k, v, feat_q, feat_k, ())
    from_x = [over(after(from_y[0], first[0]), 2)]
    second = attend(1, q, k, v, feat_q, feat_k, first[:2])
    from_x.append(over(after(from_y[1], second[0]), 2))
    third = attend(2, q, k, v, feat_q, feat_k, second[:1])
    o_got = [over_y(second[1]), over_y(third[1])]
    pieces = [from_y[0], from_x[0], over_core(from_y[0]), over_core(after(from_x[0], second[0]))]
    pieces += [from_y[1], from_x[1], over_core(from_y[1]), over_core(after(from_x[1], third[0]))]
    at = jnp.arange(2, dtype=jnp.int32)[:, None] * cut + jnp.stack(
        [(2 * c + s) * quarter for c in (core, 1 - core) for s in (side, 1 - side)]
    )
    o_own = third[0]
    o_far = (second[1], second[1], third[1])
    q_tag = [x[2:] for x in (first, second, third)]
    w_got = assemble(at.reshape(8), pieces, w_own.shape, (o_got[0],))
    scalars = jnp.stack([shard * rows, bounds[0, NSEG - 1]]).astype(jnp.int32)
    (
        hidden_out, n2, ga, dx, gm, by_unit, d_own, db01, db2, gg_mlp,
    ) = mlp(scalars, hidden_in, cotangent, o_own, o_got, gain_m, w_own, w_got, units)
    d_got = [over_y(db01), over_y(db2)]
    d_far = (d_got[0], d_got[0], d_got[1])

    def back(pair, start, stop, begun, *deps):
        return attend_back(
            pair, start, stop, begun, *q_tag[pair], q, k, v, feat_k, o_own, o_far[pair],
            d_own, d_far[pair], cosine, sine, deps,
        )

    def split(x, bit):
        low = (place & bit) == 0
        half = x.shape[0] // 2
        first, second = x[:half], x[half:]
        return jnp.where(low, first, second), jnp.where(low, second, first)

    def merge(x, bit):
        return in_order((place & bit) == 0, x, over(x, bit))

    def over_rest(x):
        if len(bits) < 3:
            return x
        mine, other = split(x, bits[2])
        mine = add(mine, over(other, bits[2]))
        for bit in bits[3:]:
            mine = add(mine, over(mine, bit))
        return merge(mine, bits[2])

    keep1, send1 = weight_grads(1, core_at, o_got, by_unit, n2, ga, gm)
    keep0, send0 = weight_grads(0, core_at, (o_own,), by_unit, n2, ga, gm, (keep1,))
    came1 = over_core(send1)
    came0 = over_core(after(send0, d_got[0]))
    head = send0.shape[0] // 32 * 16 - 16
    own_a, far_a, mine_b, other_b = combine(
        side.astype(jnp.int32).reshape(1), keep0, came0, keep1, came1, head
    )
    got_a, got_b = over_y(far_a), over(other_b, 2)
    blocks = cap // KBLK
    back0 = back(0, 0, blocks, (), mine_b, far_a)[0]
    keep, send = pair_grads(core_at, back0, n1)

    side_at = side.astype(jnp.int32).reshape(1)
    mine, mine_b, far_b, other_a = second_step(side_at, own_a, got_a, mine_b, got_b, (back0,))
    got_a, got_b = over(other_a, 2), over_y(far_b)
    begun = back(1, 0, 1, (), keep, mine)
    pair0 = plus(keep, over_core(send))

    if len(bits) > 2:
        low = ((place // 4) % 2).astype(jnp.int32).reshape(1)
        mine, other = cut_sums(low, (mine, got_a, mine_b, got_b), (begun[0],))
        got = over(other, bits[2])
    else:
        mine = jnp.concatenate([add(mine, got_a), add(mine_b, got_b)], axis=0)
    back1 = back(1, 1, blocks, begun, mine, pair0)[0]
    keep, send = pair_grads(core_at, back1, n1)

    if len(bits) > 2:
        mine = plus(mine, got, (back1,))
    if len(bits) > 3:
        got = over(mine, bits[3])
    came = over_core(send)
    q_mine, q_other = pairs_step(side_at, (pair0, keep, came), pair0.shape[0])
    q_got = over(q_other, 2)
    back2 = back(2, 0, blocks, (), mine, q_other)[0]
    if len(bits) > 3:
        mine = plus(mine, got, (back2,))
    parts = (back0, back1, back2)
    keep, send = pair_grads(core_at, back2, n1, (mine, q_got))
    dn_other, gg_other = tail(parts, w_qkv_turned, hidden_got, rows, bf16, (keep,))
    cut_at = rows // 2
    dn_got = over_y(dn_other[:cut_at])
    came = over_core(send)
    if len(bits) > 2:
        for bit in bits[4:]:
            mine = add(mine, over(mine, bit))
        mine = merge(mine, bits[2])
    last_mine, last_other = pairs_step(
        side_at, (keep, came), pair0.shape[0] // 2, (dn_other,)
    )
    dn_own, gg_own = tail(parts, w_qkv_turned, hidden_in, 0, f32, (last_other,))
    gains = gain_rows(gg_own, gg_other, gg_mlp)
    gains = gains + over_core(gains)
    last_got = over(last_other, 2)
    weights = mine
    if len(bits) > 2:
        mine, other = cut_sums(
            low, (q_mine, q_got, last_mine, last_got, gains, over(gains, 2)), (dn_got,)
        )
        lent = over(other, bits[2])
        got = over(after(weights, mine), 2)
        low_side = (place & 2) == 0
        grads = jnp.concatenate(
            [in_order(low_side, weights[: head // 2], got[: head // 2]),
             in_order(low_side, weights[head // 2 : quarter], got[head // 2 : quarter])],
            axis=0,
        )
        mine = plus(mine, lent)
        dn_late = over_y(after(dn_other[cut_at:], mine))
        for bit in bits[3:-1]:
            mine = plus(mine, over(mine, bit))
        if len(bits) > 3:
            mine = plus(mine, over(mine, bits[-1]), (got,))
        mine = merge(mine, bits[2])
    else:
        mine = jnp.concatenate(
            [add(q_mine, q_got), add(last_mine, last_got), add(gains, over(gains, 2))], axis=0
        )
        dn_late = over_y(dn_other[cut_at:])
        got = over(after(weights, mine), 2)
        low_side = (place & 2) == 0
        grads = jnp.concatenate(
            [in_order(low_side, weights[: head // 2], got[: head // 2]),
             in_order(low_side, weights[head // 2 : quarter], got[head // 2 : quarter])],
            axis=0,
        )
    low_side = (place & 2) == 0
    grad_in = last(hidden_in, gain_a, dn_own, dn_got, dn_late, dx)
    first, count = pair0.shape[0], 3 * pair0.shape[0] // 2
    gains = mine[count : count + 2].astype(f32)
    gains = gains + over_y(gains)
    got = over(after(mine[:count], grad_in), 2)
    pairs = jnp.concatenate(
        [in_order(low_side, mine[:first], got[:first]),
         in_order(low_side, mine[first:count], got[first:])],
        axis=0,
    )

    grad_w_attn, grad_w_in, grad_w_out = unstack(core_at, grads, over_core(grads), width, units)
    grad_w_in = jnp.swapaxes(grad_w_in, 1, 2)
    grad_w_qkv = unpair(core_at, pairs, over_core(after(pairs, grad_w_attn)))
    return (
        hidden_out,
        grad_in,
        gains[0],
        grad_w_qkv,
        grad_w_attn,
        gains[1],
        grad_w_in,
        grad_w_out,
    )


def solution(mesh):
    in_specs = (
        P(("dp", "tensor"), None),
        P("dp", None),
        P(),
        P(None, None, "tensor"),
        P("tensor", None),
        P(),
        P(None, None, "tensor"),
        P("tensor", None),
        P(("dp", "tensor"), None),
    )
    out_specs = (
        P(("dp", "tensor"), None),
        P(("dp", "tensor"), None),
        P(),
        P(None, None, "tensor"),
        P("tensor", None),
        P(),
        P(None, None, "tensor"),
        P("tensor", None),
    )
    return jax.shard_map(
        functools.partial(on_device, mesh.shape["dp"]),
        mesh=mesh,
        in_specs=in_specs,
        out_specs=out_specs,
        check_vma=False,
    )
```
